32 devices in a mesh: grp: 2 (over x), ad: 16 (over z, y, core).
Axes of the slice: x: 2, y: 2, z: 4, core: 2. Of those that a mesh axis runs over, the one named last changes fastest.
Arguments:
- tokens: bfloat16 [4096, 8192], P(('grp', 'ad')), parts along dimension 0, may hold values from -6 to 6
- cotangent: bfloat16 [4096, 1024], P(('grp', 'ad')), parts along dimension 0, may hold values from -0.1796875 to 0.1796875
- owner: int32 [4096, 1], P(('grp', 'ad')), parts along dimension 0, may hold values from 0 to 15; in each aligned block of 128 rows (0 to 127, 128 to 255, ...) at most 16 rows name the same one
- token_local_adapter: int32 [4096], P(('grp', 'ad')), parts along dimension 0, may hold values from 0 to 1
- segment: int32 [32, 128], P(('grp', 'ad')), parts along dimension 0, may hold values from 0 to 3, never falling along the last dimension, each value on 1 to 64 neighbouring positions
- pair_sequence_order: int32 [32, 4], P(('grp', 'ad')), parts along dimension 0, may hold values from 0 to 3, each once within a row
- frozen_margin_score: float32 [32, 4], P(('grp', 'ad')), parts along dimension 0, may hold values from -12 to 12
- adapter_down_weight: bfloat16 [32, 64, 8192], P('ad'), may hold values from -0.0625 to 0.0625
- adapter_up_weight: bfloat16 [32, 64, 1024], P('ad'), may hold values from -0.75 to 0.75
Outputs:
- input_grad: bfloat16 [4096, 8192], P(('grp', 'ad')), parts along dimension 0
- grad_a: bfloat16 [64, 64, 8192], P(('grp', 'ad')), parts along dimension 0
- grad_b: bfloat16 [64, 64, 1024], P(('grp', 'ad')), parts along dimension 0
- pair_loss: float32 [64], P(('grp', 'ad')), parts along dimension 0
The draws below stay inside these ranges and needn't reach their ends.
There are 2 independent parts, one for each index of `grp`. The reference program is written for one: setup_inputs(seed, part) draws one part's arguments, and reference() takes and returns one part's arrays. A program takes and returns all parts, laid end to end along the dimension named above; an argument that names none is the same for every part. Nothing has to cross between parts.
Inputs may be any that keep to these rules, and one draw needn't show every extreme that they name: The rows of one device name one owner at most 16 times; in some device some owner is named exactly 16 times. `segment`: within each row, sequence numbers never fall; each of the 4 sequences holds 1 to 64 consecutive positions. `pair_sequence_order`: each row is a permutation of the device's sequences.
All inputs are finite; a program needn't handle non-finite values.
Results may differ from the reference program's by a relative error of at most 0.0085.
Values may be sent and summed in bfloat16 or wider, within the bound.
No kernel may reach another device: no remote copies, remote signals or barrier semaphores. Data moves between devices by JAX's collectives and lax.ppermute only.
A program may use at most 128 MiB of HBM per device.

```python
import math
import jax
import jax.numpy as jnp
import numpy as np
from jax import lax

MODEL_WIDTH = 8192
VALUE_WIDTH = 1024
ADAPTER_RANK = 64
ADAPTERS_LOCAL = 2
TOK_DEV = 128
SEQ_DEV = 4
TOKENS = 2048
ADAPTER_TOTAL = 32
CAP = 16
PAIRS = 32
N_AD = 16


def with_ends(result, key, smallest, high):
    longest = result.shape.index(max(result.shape))
    spots = []
    for shift in (0, 1):
        where = [jax.random.randint(jax.random.fold_in(key, axis), (), 0, length) for axis, length in enumerate(result.shape)]
        where[longest] = (where[longest] + shift) % result.shape[longest]
        spots.append(tuple(where))
    return result.at[spots[0]].set(smallest).at[spots[1]].set(high)


def level_of(rng, dims, pieces, low, top_value):
    loudness = 1.0
    for axis_at, parts in pieces:
        heights = jax.random.uniform(jax.random.fold_in(jax.random.fold_in(rng, 6), axis_at), (parts,), jnp.float32, low / len(pieces), top_value / len(pieces))
        loudness = loudness * jnp.repeat(jnp.exp(heights), dims[axis_at] // parts).reshape((-1,) + (1,) * (len(dims) - 1 - axis_at))
    return loudness


def profile(count, total, bound, skew):
    portions = [(1 << 20) // math.isqrt(rank ** skew) + 1 for rank in range(2, count + 1)]
    spare, holding = total - bound - (count - 1), [1] * (count - 1)
    while spare > 0:
        candidates = [i for i in range(count - 1) if holding[i] < bound]
        mass, left = sum([portions[i] for i in candidates]), spare
        for i in candidates:
            extra = min(bound - holding[i], max(1, left * portions[i] // mass), spare)
            holding[i] = holding[i] + extra
            spare = spare - extra
    return np.array([bound] + holding)


def uneven_parts(own_key, amount, total, reach, skew):
    if amount == 2:
        one = jax.random.randint(own_key, (), max(1, total - reach), min(reach, total - 1) + 1)
        return jnp.stack([one, total - one])
    sizes = jnp.asarray(profile(amount, total, reach, skew), jnp.int32)
    twos = (amount - 1) // 2
    donor, sink = sizes[1:1 + 2 * twos:2], sizes[2:2 + 2 * twos:2]
    room = jnp.minimum(donor - 1, reach - sink)
    passed = jax.random.randint(jax.random.fold_in(own_key, 1), (twos,), 0, 1 << 20) % (room + 1)
    sizes = sizes.at[1:1 + 2 * twos:2].set(donor - passed).at[2:2 + 2 * twos:2].set(sink + passed)
    return sizes[jax.random.permutation(jax.random.fold_in(own_key, 2), amount)]


def deal_out(stream_key, own, number, rows, amount, top, limit, skew):
    ranking = jax.random.permutation(stream_key, amount)
    packed, ordinary = shares(amount, rows * top, limit, skew, True), shares(amount, rows * top, limit, skew, False)
    places = jnp.arange(amount)

    def named(tallies, turn):
        used = int((tallies > 0).sum())
        fixed = max(1, used // 4)
        passed = fixed + (places - fixed + turn * (used - fixed)) % max(1, amount - fixed)
        return jnp.zeros((amount,), jnp.int32).at[ranking[jnp.where(places < fixed, places, passed)]].set(jnp.asarray(tallies, jnp.int32))

    tallies = jnp.where(number % 4 == 0, named(packed, number // 4), named(ordinary, number - number // 4 - 1))
    mixed = jax.random.permutation(jax.random.fold_in(own, 3), amount)
    source_of, receiver = mixed[0:amount // 2 * 2:2], mixed[1:amount // 2 * 2:2]
    room = jnp.minimum(tallies[source_of] - 1, limit - tallies[receiver]) // 2
    room = jnp.where((source_of == ranking[0]) | (receiver == ranking[0]) | (tallies[receiver] == 0), 0, jnp.maximum(room, 0))
    passed = jax.random.randint(jax.random.fold_in(own, 4), (amount // 2,), 0, 1 << 20) % (room + 1)
    tallies = tallies.at[source_of].add(-passed).at[receiver].add(passed)
    items = jnp.searchsorted(jnp.cumsum(tallies), jnp.arange(rows * top), side="right").astype(jnp.int32)
    grid = items.reshape(top, rows).T
    grid = grid[jax.random.permutation(jax.random.fold_in(own, 1), rows)]
    turn = jax.random.randint(jax.random.fold_in(own, 2), (rows, 1), 0, top)
    return jnp.take_along_axis(grid, (jnp.arange(top)[None, :] + turn) % top, axis=1)


def shares(number_of, total, most, slope, full):
    portions = [(1 << 20) // math.isqrt(grade ** slope) + 1 for grade in range(1, number_of + 1)]
    largest = most if full else min(most, max(-(-total // number_of), total * portions[0] // sum(portions)))
    least = 1 if total - largest >= number_of - 1 else 0
    holding, spare = [largest] + [least] * (number_of - 1), total - largest - least * (number_of - 1)
    while spare > 0:
        candidates = [i for i in range(1, number_of) if holding[i] < largest] or [i for i in range(1, number_of) if holding[i] < most]
        mass, budget = sum([portions[i] for i in candidates]), spare
        for i in candidates:
            addition = min(most - holding[i], max(1, budget * portions[i] // mass), spare)
            holding[i] = holding[i] + addition
            spare = spare - addition
    return np.array(holding)


def centred(rng, dims, width, most, shards=(), held_as=jnp.bfloat16):
    array = jax.random.normal(rng, dims, jnp.float32) * width
    if len(shards) > 0:
        array = level_of(rng, dims, shards, -0.22, 0.18) * array
    return jnp.clip(array, min=-most, max=most).astype(held_as)


def setup_inputs(seed: int = 0, part: int = 0) -> dict:
    key_list = jax.random.split(jax.random.key(seed), 10)
    part_keys = jax.random.split(jax.random.fold_in(key_list[9], part), 10)
    tokens = centred(part_keys[0], (TOKENS, MODEL_WIDTH), 1.0, 6.0, ((0, 16),))
    cotangent = centred(part_keys[1], (TOKENS, VALUE_WIDTH), 0.03, 0.1796875, ((0, 16),))
    owner_keys = jax.random.split(jax.random.fold_in(part_keys[2], 1), TOKENS // TOK_DEV)
    owner_turns = jax.random.permutation(jax.random.fold_in(part_keys[2], 3), TOKENS // TOK_DEV)
    owner = jax.vmap(lambda own, number: deal_out(jax.random.fold_in(part_keys[2], 2), own, number, TOK_DEV, N_AD, 1, CAP, 2))(owner_keys, owner_turns).reshape((TOKENS, 1))
    token_local_adapter = with_ends(jax.random.randint(part_keys[3], (TOKENS,), 0, ADAPTERS_LOCAL), jax.random.fold_in(part_keys[3], 1), 0, ADAPTERS_LOCAL - 1).astype(jnp.int32)
    segment = jax.vmap(lambda own: jnp.searchsorted(jnp.cumsum(uneven_parts(own, SEQ_DEV, TOK_DEV, TOK_DEV // 2, 1)), jnp.arange(TOK_DEV), side="right"))(jax.random.split(part_keys[4], N_AD)).reshape((N_AD, TOK_DEV)).astype(jnp.int32)
    pair_sequence_order = jax.vmap(lambda own: jax.random.permutation(own, SEQ_DEV))(jax.random.split(part_keys[5], N_AD)).reshape((N_AD, SEQ_DEV)).astype(jnp.int32)
    frozen_margin_score = centred(part_keys[6], (N_AD, SEQ_DEV), 3.0, 12.0, ((0, 16),), jnp.float32)
    adapter_down_weight = centred(key_list[7], (ADAPTER_TOTAL, ADAPTER_RANK, MODEL_WIDTH), MODEL_WIDTH ** -0.5, 0.0625, ((0, 16),))
    adapter_up_weight = centred(key_list[8], (ADAPTER_TOTAL, ADAPTER_RANK, VALUE_WIDTH), ADAPTER_RANK ** -0.5, 0.75, ((0, 16),))
    return dict(tokens=tokens, cotangent=cotangent, owner=owner, token_local_adapter=token_local_adapter, segment=segment, pair_sequence_order=pair_sequence_order, frozen_margin_score=frozen_margin_score, adapter_down_weight=adapter_down_weight, adapter_up_weight=adapter_up_weight)


SCALE = 2.0
BETA = 0.1
LOSS_SCALE = 256.0


def adapter_rows(rows_input, rows_gradient, rows_adapter_index, down_pair, up_pair):
    count_rows = rows_input.shape[0]
    rank_size = down_pair.shape[1]
    contract = (((1,), (1,)), ((), ()))
    hidden = jnp.zeros((count_rows, rank_size), jnp.float32)
    pulled = jnp.zeros((count_rows, rank_size), jnp.float32)
    for which in range(down_pair.shape[0]):
        member = (rows_adapter_index == which)[:, None]
        hidden = jnp.where(member, lax.dot_general(rows_input, down_pair[which], contract, preferred_element_type=jnp.float32), hidden)
        pulled = jnp.where(member, lax.dot_general(rows_gradient, up_pair[which], contract, preferred_element_type=jnp.float32), pulled)
    hidden_rank_rows = hidden.astype(jnp.bfloat16)
    pulled_rank_rows = pulled.astype(jnp.bfloat16)
    outgoing = jnp.zeros((count_rows, up_pair.shape[2]), jnp.float32)
    projected = jnp.zeros((count_rows, down_pair.shape[2]), jnp.float32)
    for which in range(down_pair.shape[0]):
        member = (rows_adapter_index == which)[:, None]
        outgoing = outgoing + jnp.dot(jnp.where(member, hidden_rank_rows, 0), up_pair[which], preferred_element_type=jnp.float32)
        projected = projected + jnp.dot(jnp.where(member, pulled_rank_rows, 0), down_pair[which], preferred_element_type=jnp.float32)
    return hidden_rank_rows, pulled_rank_rows, (SCALE * outgoing).astype(jnp.bfloat16), projected.astype(jnp.bfloat16)


def adapter_grads(rows_input, rows_gradient, rows_adapter_index, hidden_rank_rows, pulled_rank_rows, row_weight, count):
    upper = (row_weight[:, None] * hidden_rank_rows.astype(jnp.float32)).astype(jnp.bfloat16)
    lower = (row_weight[:, None] * pulled_rank_rows.astype(jnp.float32)).astype(jnp.bfloat16)
    contract = (((0,), (0,)), ((), ()))
    grads_down = []
    grads_up = []
    for which in range(count):
        member = (rows_adapter_index == which)[:, None]
        grads_up.append(SCALE * lax.dot_general(jnp.where(member, upper, 0), rows_gradient, contract, preferred_element_type=jnp.float32))
        grads_down.append(SCALE * lax.dot_general(jnp.where(member, lower, 0), rows_input, contract, preferred_element_type=jnp.float32))
    return jnp.stack(grads_down).astype(jnp.bfloat16), jnp.stack(grads_up).astype(jnp.bfloat16)


def pair_terms(outgoing, cotangent, segment_row, order_row, base_row):
    seqs = base_row.shape[0]
    tokdot = jnp.sum(outgoing.astype(jnp.float32) * cotangent.astype(jnp.float32), axis=1)
    seq_hot = (segment_row[:, None] == jnp.arange(seqs, dtype=jnp.int32)[None, :]).astype(jnp.float32)
    scores = base_row + jnp.dot(tokdot, seq_hot, precision=lax.Precision.HIGHEST)
    pair_pick = (order_row[:, None] == jnp.arange(seqs, dtype=jnp.int32)[None, :]).astype(jnp.float32)
    ordered = jnp.sum(pair_pick * scores[None, :], axis=1).reshape(seqs // 2, 2)
    margin = BETA * (ordered[:, 0] - ordered[:, 1])
    losses = jax.nn.softplus(-margin)
    lean = jax.nn.sigmoid(-margin)
    by_order = jnp.stack([-BETA * lean, BETA * lean], axis=1).reshape(seqs)
    seq_weight = jnp.sum(pair_pick * by_order[:, None], axis=0)
    row_weight = LOSS_SCALE * jnp.sum(seq_hot * seq_weight[None, :], axis=1)
    return losses, row_weight


def reference(tokens, cotangent, owner, token_local_adapter, segment, pair_sequence_order, frozen_margin_score, adapter_down_weight, adapter_up_weight):
    target_owner = owner[:, 0]
    rows_max = N_AD * CAP
    sorted_rows = jnp.argsort(target_owner, stable=True).astype(jnp.int32)
    counts = jnp.sum((target_owner[:, None] == jnp.arange(N_AD, dtype=jnp.int32)[None, :]).astype(jnp.int32), axis=0)
    starts = (jnp.cumsum(counts) - counts).astype(jnp.int32)
    sorted_pad = jnp.concatenate([sorted_rows, jnp.full((rows_max,), TOKENS, jnp.int32)])
    x_pad = jnp.concatenate([tokens, jnp.zeros((1, MODEL_WIDTH), tokens.dtype)])
    g_pad = jnp.concatenate([cotangent, jnp.zeros((1, VALUE_WIDTH), cotangent.dtype)])
    id_pad = jnp.concatenate([token_local_adapter, jnp.zeros((1,), jnp.int32)])
    down_matrix_view = adapter_down_weight.reshape(N_AD, ADAPTERS_LOCAL, ADAPTER_RANK, MODEL_WIDTH)
    up_matrix_view = adapter_up_weight.reshape(N_AD, ADAPTERS_LOCAL, ADAPTER_RANK, VALUE_WIDTH)

    def owner_rows(owner_id):
        picked = lax.dynamic_slice(sorted_pad, (starts[owner_id],), (rows_max,))
        valid = jnp.arange(rows_max, dtype=jnp.int32) < counts[owner_id]
        return jnp.where(valid, picked, TOKENS).astype(jnp.int32)

    def forward_step(carry, owner_id):
        out_tok, proj_tok, hid_tok, pull_tok = carry
        picked = owner_rows(owner_id)
        hidden_rank_rows, pulled_rank_rows, outgoing, projected = adapter_rows(x_pad[picked], g_pad[picked], id_pad[picked], down_matrix_view[owner_id], up_matrix_view[owner_id])
        carry = (out_tok.at[picked].set(outgoing), proj_tok.at[picked].set(projected), hid_tok.at[picked].set(hidden_rank_rows), pull_tok.at[picked].set(pulled_rank_rows))
        return carry, None

    start_carry = (jnp.zeros((TOKENS + 1, VALUE_WIDTH), jnp.bfloat16), jnp.zeros((TOKENS + 1, MODEL_WIDTH), jnp.bfloat16), jnp.zeros((TOKENS + 1, ADAPTER_RANK), jnp.bfloat16), jnp.zeros((TOKENS + 1, ADAPTER_RANK), jnp.bfloat16))
    (out_tok, proj_tok, hid_tok, pull_tok), _ = lax.scan(forward_step, start_carry, jnp.arange(N_AD, dtype=jnp.int32))
    losses, row_weight = jax.vmap(pair_terms)(out_tok[:TOKENS].reshape(N_AD, TOK_DEV, VALUE_WIDTH), cotangent.reshape(N_AD, TOK_DEV, VALUE_WIDTH), segment, pair_sequence_order, frozen_margin_score)
    row_weight = row_weight.reshape(TOKENS)
    input_grad = (SCALE * row_weight[:, None] * proj_tok[:TOKENS].astype(jnp.float32)).astype(jnp.bfloat16)
    weight_pad = jnp.concatenate([row_weight, jnp.zeros((1,), jnp.float32)])

    def grad_step(carry, owner_id):
        picked = owner_rows(owner_id)
        grad_down, grad_up = adapter_grads(x_pad[picked], g_pad[picked], id_pad[picked], hid_tok[picked], pull_tok[picked], weight_pad[picked], ADAPTERS_LOCAL)
        return carry, (grad_down, grad_up)

    _, (grad_down, grad_up) = lax.scan(grad_step, 0, jnp.arange(N_AD, dtype=jnp.int32))
    return input_grad, grad_down.reshape(ADAPTER_TOTAL, ADAPTER_RANK, MODEL_WIDTH), grad_up.reshape(ADAPTER_TOTAL, ADAPTER_RANK, VALUE_WIDTH), losses.reshape(PAIRS)
```

```python
import jax
import jax.numpy as jnp
from jax import lax
from jax.sharding import PartitionSpec as P

SCALE = 2.0
BETA = 0.1
LOSS_SCALE = 256.0

F32 = jnp.float32
BF16 = jnp.bfloat16


def rows_by_slot(owners, n_dev, capacity):
    rows = owners.shape[1]
    hot = (owners[:, :, None] == jnp.arange(n_dev, dtype=jnp.int32)).astype(BF16)
    earlier = (
        jnp.arange(rows, dtype=jnp.int32)[:, None] > jnp.arange(rows, dtype=jnp.int32)[None, :]
    ).astype(BF16)
    before = jnp.einsum("rq,dqk->drk", earlier, hot, preferred_element_type=F32)
    rank = jnp.sum(before * hot.astype(F32), axis=2).astype(jnp.int32)
    return owners * capacity + rank


def pair_weights(scores, order):
    devices, seqs = scores.shape
    pick = (order[:, :, None] == jnp.arange(seqs, dtype=jnp.int32)).astype(F32)
    ordered = jnp.sum(pick * scores[:, None, :], axis=2).reshape(devices, seqs // 2, 2)
    margin = BETA * (ordered[:, :, 0] - ordered[:, :, 1])
    losses = jax.nn.softplus(-margin)
    lean = jax.nn.sigmoid(-margin)
    by_order = jnp.stack([-BETA * lean, BETA * lean], axis=2).reshape(devices, seqs)
    return losses, jnp.sum(pick * by_order[:, :, None], axis=1)


def body(
    tokens,
    cotangent,
    owner,
    token_local_adapter,
    segment,
    pair_sequence_order,
    frozen_margin_score,
    adapter_down_weight,
    adapter_up_weight,
):
    rows, width = tokens.shape
    out_width = cotangent.shape[1]
    n_dev = lax.axis_size("ad")
    me = lax.axis_index("ad")
    capacity = max(2, 2 * rows // n_dev)
    slots = n_dev * capacity
    count, rank_size, _ = adapter_down_weight.shape
    seqs = frozen_margin_score.shape[1]
    lanes = count * rank_size
    down = adapter_down_weight.reshape(lanes, width)
    up = adapter_up_weight.reshape(lanes, out_width)

    meta = jnp.concatenate(
        [
            owner.reshape(1, rows).astype(F32),
            token_local_adapter[None].astype(F32),
            segment.astype(F32),
            jnp.pad(
                jnp.concatenate([pair_sequence_order.astype(F32), frozen_margin_score], axis=1),
                ((0, 0), (0, rows - 2 * seqs)),
            ),
        ]
    )
    all_meta = lax.all_gather(meta, "ad")

    slot_index = rows_by_slot(owner.reshape(1, rows), n_dev, capacity)[0]
    to_slot = (jnp.arange(slots, dtype=jnp.int32)[:, None] == slot_index[None, :]).astype(BF16)
    send_g = jnp.dot(to_slot, cotangent, preferred_element_type=BF16)
    send_x = jnp.dot(to_slot, tokens, preferred_element_type=BF16)
    got_g = lax.all_to_all(
        send_g.reshape(n_dev, capacity, out_width), "ad", split_axis=0, concat_axis=0, tiled=True
    ).reshape(slots, out_width)
    got_x = lax.all_to_all(
        send_x.reshape(n_dev, capacity, width), "ad", split_axis=0, concat_axis=0, tiled=True
    ).reshape(slots, width)

    all_owner = all_meta[:, 0].astype(jnp.int32)
    all_slot = rows_by_slot(all_owner, n_dev, capacity)
    mine = (
        all_slot[:, None, :] == me * capacity + jnp.arange(capacity, dtype=jnp.int32)[None, :, None]
    ).astype(F32)
    slot_adapter = jnp.sum(mine * all_meta[:, 1][:, None, :], axis=2).reshape(slots)
    slot_seq = jnp.sum(mine * all_meta[:, 2][:, None, :], axis=2)
    slot_used = jnp.sum(mine, axis=2)
    slot_seq_hot = (
        slot_seq[:, :, None] == jnp.arange(seqs, dtype=F32)
    ).astype(F32) * slot_used[:, :, None]
    lane_adapter = (jnp.arange(lanes, dtype=jnp.int32) // rank_size).astype(F32)
    member = slot_adapter[:, None] == lane_adapter[None, :]

    contract = (((1,), (1,)), ((), ()))
    pulled = jnp.where(
        member, lax.dot_general(got_g, up, contract, preferred_element_type=F32), 0.0
    )
    pulled_rows = pulled.astype(BF16)
    projected = jnp.dot(pulled_rows, down, preferred_element_type=BF16)
    got_p = lax.all_to_all(
        projected.reshape(n_dev, capacity, width), "ad", split_axis=0, concat_axis=0, tiled=True
    ).reshape(slots, width)

    hidden_rows = jnp.where(
        member, lax.dot_general(got_x, down, contract, preferred_element_type=F32), 0.0
    ).astype(BF16)
    inner = SCALE * jnp.sum(hidden_rows.astype(F32) * pulled, axis=1)
    part = jnp.sum(slot_seq_hot * inner.reshape(n_dev, capacity)[:, :, None], axis=1)
    scores = lax.psum(part, "ad") + all_meta[:, 3, seqs : 2 * seqs]
    losses, seq_weight = pair_weights(scores, all_meta[:, 3, :seqs].astype(jnp.int32))

    slot_weight = LOSS_SCALE * jnp.sum(slot_seq_hot * seq_weight[:, None, :], axis=2).reshape(slots)
    upper = (slot_weight[:, None] * hidden_rows.astype(F32)).astype(BF16)
    lower = (slot_weight[:, None] * pulled_rows.astype(F32)).astype(BF16)
    rows_contract = (((0,), (0,)), ((), ()))
    grad_up = (
        SCALE * lax.dot_general(upper, got_g, rows_contract, preferred_element_type=F32)
    ).astype(BF16)
    grad_down = (
        SCALE * lax.dot_general(lower, got_x, rows_contract, preferred_element_type=F32)
    ).astype(BF16)

    my_weight = lax.dynamic_index_in_dim(seq_weight, me, keepdims=False)
    my_losses = lax.dynamic_index_in_dim(losses, me, keepdims=False)
    seq_hot = (segment[0][:, None] == jnp.arange(seqs, dtype=jnp.int32)).astype(F32)
    row_weight = LOSS_SCALE * jnp.sum(seq_hot * my_weight[None, :], axis=1)
    picked = lax.dot_general(to_slot, got_p, rows_contract, preferred_element_type=F32)
    input_grad = (SCALE * row_weight[:, None] * picked).astype(BF16)
    return (
        input_grad,
        grad_down.reshape(count, rank_size, width),
        grad_up.reshape(count, rank_size, out_width),
        my_losses,
    )


def solution(mesh):
    placed = (
        P(("grp", "ad"), None),
        P(("grp", "ad"), None),
        P(("grp", "ad"), None),
        P(("grp", "ad")),
        P(("grp", "ad"), None),
        P(("grp", "ad"), None),
        P(("grp", "ad"), None),
        P("ad", None, None),
        P("ad", None, None),
    )
    return jax.shard_map(
        body,
        mesh=mesh,
        in_specs=placed,
        out_specs=(
            P(("grp", "ad"), None),
            P(("grp", "ad"), None, None),
            P(("grp", "ad"), None, None),
            P(("grp", "ad")),
        ),
        check_vma=False,
    )
```

```python
import jax
import jax.numpy as jnp
from jax import lax
from jax.sharding import PartitionSpec as P

SCALE = 2.0
BETA = 0.1
LOSS_SCALE = 256.0
PLANES = 4

F32 = jnp.float32
BF16 = jnp.bfloat16


def rows_by_slot(owners, n_dev, capacity):
    rows = owners.shape[1]
    hot = (owners[:, :, None] == jnp.arange(n_dev, dtype=jnp.int32)).astype(BF16)
    earlier = (
        jnp.arange(rows, dtype=jnp.int32)[:, None] > jnp.arange(rows, dtype=jnp.int32)[None, :]
    ).astype(BF16)
    before = jnp.einsum("rq,dqk->drk", earlier, hot, preferred_element_type=F32)
    rank = jnp.sum(before * hot.astype(F32), axis=2).astype(jnp.int32)
    return owners * capacity + rank


def pair_weights(scores, order):
    devices, seqs = scores.shape
    pick = (order[:, :, None] == jnp.arange(seqs, dtype=jnp.int32)).astype(F32)
    ordered = jnp.sum(pick * scores[:, None, :], axis=2).reshape(devices, seqs // 2, 2)
    margin = BETA * (ordered[:, :, 0] - ordered[:, :, 1])
    losses = jax.nn.softplus(-margin)
    lean = jax.nn.sigmoid(-margin)
    by_order = jnp.stack([-BETA * lean, BETA * lean], axis=2).reshape(devices, seqs)
    return losses, jnp.sum(pick * by_order[:, :, None], axis=1)


def share(block):
    n_dev = lax.axis_size("ad")
    return lax.all_to_all(
        jnp.broadcast_to(block[None], (n_dev,) + block.shape),
        "ad",
        split_axis=0,
        concat_axis=0,
        tiled=True,
    )


def body(
    tokens,
    cotangent,
    owner,
    token_local_adapter,
    segment,
    pair_sequence_order,
    frozen_margin_score,
    adapter_down_weight,
    adapter_up_weight,
):
    rows, width = tokens.shape
    out_width = cotangent.shape[1]
    n_grp, n_dev = lax.axis_size("grp"), lax.axis_size("ad")
    grp, me = lax.axis_index("grp"), lax.axis_index("ad")
    inner = n_dev // PLANES
    plane = me // inner
    capacity = max(2, 2 * rows // n_dev)
    slots = n_dev * capacity
    plane_slots = inner * capacity
    count, rank_size, _ = adapter_down_weight.shape
    seqs = frozen_margin_score.shape[1]
    lanes = count * rank_size
    down = adapter_down_weight.reshape(lanes, width)
    up = adapter_up_weight.reshape(lanes, out_width)

    in_plane = [[z * inner + q for q in range(inner)] for z in range(PLANES)]
    across = [[z * inner + q for z in range(PLANES)] for q in range(inner)]

    def other_plane(block, flip):
        return lax.ppermute(
            block,
            ("grp", "ad"),
            [
                (g * n_dev + z * inner + q, g * n_dev + (z ^ flip) * inner + q)
                for g in range(n_grp)
                for z in range(PLANES)
                for q in range(inner)
            ],
        )

    def other_grp(block):
        return lax.ppermute(block, "grp", [(0, 1), (1, 0)])

    half_mine = lax.dynamic_index_in_dim(adapter_down_weight, grp, keepdims=False)
    half_other = lax.dynamic_index_in_dim(adapter_down_weight, 1 - grp, keepdims=False)
    far = other_plane(half_mine, 2)
    near = other_plane(half_mine, 1)
    last = other_plane(far, 1)
    halves = {
        0: (half_mine, half_other),
        2: (far, other_grp(far)),
        1: (near, other_grp(near)),
        3: (last, other_grp(last)),
    }

    meta = jnp.concatenate(
        [
            owner.reshape(1, rows).astype(F32),
            token_local_adapter[None].astype(F32),
            segment.astype(F32),
            jnp.pad(
                jnp.concatenate([pair_sequence_order.astype(F32), frozen_margin_score], axis=1),
                ((0, 0), (0, rows - 2 * seqs)),
            ),
        ]
    )
    all_meta = share(meta)

    slot_index = rows_by_slot(owner.reshape(1, rows), n_dev, capacity)[0]
    to_slot = (jnp.arange(slots, dtype=jnp.int32)[:, None] == slot_index[None, :]).astype(BF16)
    send_g = jnp.dot(to_slot, cotangent, preferred_element_type=BF16)
    got_g = lax.all_to_all(
        send_g.reshape(n_dev, capacity, out_width), "ad", split_axis=0, concat_axis=0, tiled=True
    ).reshape(slots, out_width)
    send_x = jnp.dot(to_slot, tokens, preferred_element_type=BF16)
    send_x, _ = lax.optimization_barrier((send_x, far))
    got_x = lax.all_to_all(
        send_x.reshape(n_dev, capacity, width), "ad", split_axis=0, concat_axis=0, tiled=True
    ).reshape(slots, width)

    all_owner = all_meta[:, 0].astype(jnp.int32)
    all_slot = rows_by_slot(all_owner, n_dev, capacity)
    mine = (
        all_slot[:, None, :] == me * capacity + jnp.arange(capacity, dtype=jnp.int32)[None, :, None]
    ).astype(F32)
    slot_adapter = jnp.sum(mine * all_meta[:, 1][:, None, :], axis=2).reshape(slots)
    slot_seq = jnp.sum(mine * all_meta[:, 2][:, None, :], axis=2)
    slot_used = jnp.sum(mine, axis=2)
    slot_seq_hot = (
        slot_seq[:, :, None] == jnp.arange(seqs, dtype=F32)
    ).astype(F32) * slot_used[:, :, None]
    lane_adapter = (jnp.arange(lanes, dtype=jnp.int32) // rank_size).astype(F32)
    member = slot_adapter[:, None] == lane_adapter[None, :]

    contract = (((1,), (1,)), ((), ()))
    pulled = jnp.where(
        member, lax.dot_general(got_g, up, contract, preferred_element_type=F32), 0.0
    )
    pulled_rows = pulled.astype(BF16)

    pulled_here = lax.all_to_all(
        pulled_rows.reshape(PLANES, plane_slots, lanes),
        "ad",
        split_axis=0,
        concat_axis=0,
        tiled=True,
        axis_index_groups=across,
    ).reshape(PLANES, plane_slots, count, rank_size)
    to_slot_planes = to_slot.reshape(PLANES, plane_slots, rows)
    rows_contract = (((0,), (0,)), ((), ()))
    picked = []
    for flip in (0, 2, 1, 3):
        mine_down, other_down = halves[flip]
        from_plane = lax.dynamic_index_in_dim(pulled_here, plane ^ flip, keepdims=False)
        made = jnp.dot(
            lax.dynamic_index_in_dim(from_plane, grp, axis=1, keepdims=False),
            mine_down,
            preferred_element_type=F32,
        ) + jnp.dot(
            lax.dynamic_index_in_dim(from_plane, 1 - grp, axis=1, keepdims=False),
            other_down,
            preferred_element_type=F32,
        )
        got_p = lax.all_to_all(
            made.astype(BF16).reshape(inner, capacity, width),
            "ad",
            split_axis=0,
            concat_axis=0,
            tiled=True,
            axis_index_groups=in_plane,
        ).reshape(plane_slots, width)
        pick = lax.dynamic_index_in_dim(to_slot_planes, plane ^ flip, keepdims=False)
        picked.append(
            lax.dot_general(pick, got_p, rows_contract, preferred_element_type=F32)
        )

    hidden_rows = jnp.where(
        member, lax.dot_general(got_x, down, contract, preferred_element_type=F32), 0.0
    ).astype(BF16)
    inner_product = SCALE * jnp.sum(hidden_rows.astype(F32) * pulled, axis=1)
    part = jnp.sum(slot_seq_hot * inner_product.reshape(n_dev, capacity)[:, :, None], axis=1)
    scores = jnp.sum(share(part), axis=0) + all_meta[:, 3, seqs : 2 * seqs]
    losses, seq_weight = pair_weights(scores, all_meta[:, 3, :seqs].astype(jnp.int32))

    slot_weight = LOSS_SCALE * jnp.sum(slot_seq_hot * seq_weight[:, None, :], axis=2).reshape(slots)
    upper = (slot_weight[:, None] * hidden_rows.astype(F32)).astype(BF16)
    lower = (slot_weight[:, None] * pulled_rows.astype(F32)).astype(BF16)
    grad_up = (
        SCALE * lax.dot_general(upper, got_g, rows_contract, preferred_element_type=F32)
    ).astype(BF16)
    grad_down = (
        SCALE * lax.dot_general(lower, got_x, rows_contract, preferred_element_type=F32)
    ).astype(BF16)

    my_weight = lax.dynamic_index_in_dim(seq_weight, me, keepdims=False)
    my_losses = lax.dynamic_index_in_dim(losses, me, keepdims=False)
    seq_hot = (segment[0][:, None] == jnp.arange(seqs, dtype=jnp.int32)).astype(F32)
    row_weight = LOSS_SCALE * jnp.sum(seq_hot * my_weight[None, :], axis=1)
    input_grad = (
        SCALE * row_weight[:, None] * ((picked[0] + picked[1]) + (picked[2] + picked[3]))
    ).astype(BF16)
    return (
        input_grad,
        grad_down.reshape(count, rank_size, width),
        grad_up.reshape(count, rank_size, out_width),
        my_losses,
    )


def solution(mesh):
    placed = (
        P(("grp", "ad"), None),
        P(("grp", "ad"), None),
        P(("grp", "ad"), None),
        P(("grp", "ad")),
        P(("grp", "ad"), None),
        P(("grp", "ad"), None),
        P(("grp", "ad"), None),
        P("ad", None, None),
        P("ad", None, None),
    )
    return jax.shard_map(
        body,
        mesh=mesh,
        in_specs=placed,
        out_specs=(
            P(("grp", "ad"), None),
            P(("grp", "ad"), None, None),
            P(("grp", "ad"), None, None),
            P(("grp", "ad")),
        ),
        check_vma=False,
    )
```

```python
import functools

import jax
import jax.numpy as jnp
from jax import lax
from jax.experimental import pallas as pl
from jax.experimental.pallas import tpu as pltpu
from jax.sharding import PartitionSpec as P

SCALE = 2.0
BETA = 0.1
LOSS_SCALE = 256.0
MARKS = 128
GATE_FLOPS = 2 * 10**11

F32 = jnp.float32
BF16 = jnp.bfloat16


def gate(*arrays):
    return pl.pallas_call(
        lambda *refs: None,
        out_shape=[jax.ShapeDtypeStruct(array.shape, array.dtype) for array in arrays],
        in_specs=[pl.BlockSpec(memory_space=pl.ANY)] * len(arrays),
        out_specs=[pl.BlockSpec(memory_space=pl.ANY)] * len(arrays),
        input_output_aliases={at: at for at in range(len(arrays))},
        cost_estimate=pl.CostEstimate(flops=GATE_FLOPS, bytes_accessed=0, transcendentals=0),
        name="gate",
    )(*arrays)


def project_kernel(side, split, capacity, out_width, n_outs, spot_ref, g_ref, which, *refs):
    n_spots = g_ref.shape[0]
    n_parts = (len(refs) - n_outs) // 2
    mine, other, outs = refs[:n_parts], refs[n_parts : 2 * n_parts], refs[2 * n_parts :]
    first = side * capacity
    spot = spot_ref[0]
    rows = jnp.concatenate(
        [g_ref[spot ^ flip, first : first + capacity, :] for flip in range(n_spots)], axis=0
    )
    marks = rows[:, out_width:].astype(F32)
    contract = (((1,), (1,)), ((), ()))
    pulls = []
    for at, parts in enumerate((mine, other)):
        member = jnp.sum(marks * which[at : at + 1, :], axis=1, keepdims=True)
        pull = lax.dot_general(
            rows[:, :out_width], parts[0][:, :out_width], contract, preferred_element_type=F32
        )
        pulls.append((member * pull).astype(BF16))
    done = 0
    for at in range(n_parts):
        start, end = (out_width if at == 0 else 0), mine[at].shape[1]
        while start < end:
            size = min(1024, end - start)
            columns = slice(start, start + size)
            made = jnp.dot(pulls[0], mine[at][:, columns], preferred_element_type=F32)
            made = made + jnp.dot(pulls[1], other[at][:, columns], preferred_element_type=F32)
            made = made.astype(BF16)
            for flip in range(n_spots):
                row = made[flip * capacity : (flip + 1) * capacity]
                if split:
                    chip = flip // 2 * capacity
                    outs[flip % 2][chip : chip + capacity, done : done + size] = row
                else:
                    core = flip % 2 * capacity
                    outs[flip // 2][core : core + capacity, done : done + size] = row
            start, done = start + size, done + size


def project(side, split, capacity, out_width, width, spot, got_g, which, mine, other):
    n_spots = got_g.shape[0]
    chips = n_spots // 2
    blocks = [(chips * capacity, width)] * 2 if split else [(2 * capacity, width)] * chips
    if capacity % 16 == 0:
        return pl.pallas_call(
            functools.partial(project_kernel, side, split, capacity, out_width, len(blocks)),
            out_shape=[jax.ShapeDtypeStruct(block, BF16) for block in blocks],
            in_specs=[pl.BlockSpec(memory_space=pltpu.SMEM)]
            + [pl.BlockSpec(memory_space=pltpu.VMEM)] * (2 + len(mine) + len(other)),
            cost_estimate=pl.CostEstimate(flops=1000, bytes_accessed=1000, transcendentals=0),
            name="project",
        )(spot.reshape(1), got_g, which, *mine, *other)
    order = spot ^ jnp.arange(n_spots, dtype=jnp.int32)
    rows = got_g[order, side * capacity : (side + 1) * capacity].reshape(n_spots * capacity, -1)
    marks = rows[:, out_width:].astype(F32)
    made = 0.0
    for at, parts in enumerate((mine, other)):
        whole = jnp.concatenate(parts, axis=1)
        pull = jnp.dot(rows[:, :out_width], whole[:, :out_width].T, preferred_element_type=F32)
        pull = (jnp.sum(marks * which[at], axis=1, keepdims=True) * pull).astype(BF16)
        made = made + jnp.dot(pull, whole[:, out_width:], preferred_element_type=F32)
    made = made.astype(BF16).reshape(chips, 2, capacity, width)
    if split:
        return [made[:, core].reshape(chips * capacity, width) for core in range(2)]
    return list(made.reshape(chips, 2 * capacity, width))


def select_kernel(pick_ref, weight_ref, *refs):
    blocks, out = refs[:-1], refs[-1]
    rows = jnp.concatenate([block[...] for block in blocks], axis=0)
    picked = jnp.dot(pick_ref[...], rows, preferred_element_type=F32)
    out[...] = (weight_ref[...] * picked).astype(BF16)


def select(pick, weight, blocks, used):
    width = blocks[0].shape[1]
    rows, slots = pick.shape
    if any(size % 16 for size in used):
        blocks = [block[:size] for block, size in zip(blocks, used)]
        picked = jnp.dot(pick, jnp.concatenate(blocks), preferred_element_type=F32)
        return (weight * picked).astype(BF16)
    columns = 2048
    return pl.pallas_call(
        select_kernel,
        out_shape=jax.ShapeDtypeStruct((rows, width), BF16),
        grid=(width // columns,),
        in_specs=[
            pl.BlockSpec((rows, slots), lambda i: (0, 0)),
            pl.BlockSpec((rows, 1), lambda i: (0, 0)),
        ]
        + [pl.BlockSpec((size, columns), lambda i: (0, i)) for size in used],
        out_specs=pl.BlockSpec((rows, columns), lambda i: (0, i)),
        cost_estimate=pl.CostEstimate(
            flops=2 * rows * slots * width,
            bytes_accessed=2 * (rows + slots) * width,
            transcendentals=0,
        ),
        name="select",
    )(pick, weight, *blocks)


def rows_by_slot(owners, n_dev, capacity):
    rows = owners.shape[1]
    hot = (owners[:, :, None] == jnp.arange(n_dev, dtype=jnp.int32)).astype(BF16)
    earlier = (
        jnp.arange(rows, dtype=jnp.int32)[:, None] > jnp.arange(rows, dtype=jnp.int32)[None, :]
    ).astype(BF16)
    before = jnp.einsum("rq,dqk->drk", earlier, hot, preferred_element_type=F32)
    rank = jnp.sum(before * hot.astype(F32), axis=2).astype(jnp.int32)
    return owners * capacity + rank


def pair_weights(scores, order):
    devices, seqs = scores.shape
    pick = (order[:, :, None] == jnp.arange(seqs, dtype=jnp.int32)).astype(F32)
    ordered = jnp.sum(pick * scores[:, None, :], axis=2).reshape(devices, seqs // 2, 2)
    margin = BETA * (ordered[:, :, 0] - ordered[:, :, 1])
    losses = jax.nn.softplus(-margin)
    lean = jax.nn.sigmoid(-margin)
    by_order = jnp.stack([-BETA * lean, BETA * lean], axis=2).reshape(devices, seqs)
    return losses, jnp.sum(pick * by_order[:, :, None], axis=1)


def share(block):
    n_dev = lax.axis_size("ad")
    return lax.all_to_all(
        jnp.broadcast_to(block[None], (n_dev,) + block.shape),
        "ad",
        split_axis=0,
        concat_axis=0,
        tiled=True,
    )


def body(
    tokens,
    cotangent,
    owner,
    token_local_adapter,
    segment,
    pair_sequence_order,
    frozen_margin_score,
    adapter_down_weight,
    adapter_up_weight,
):
    rows, width = tokens.shape
    out_width = cotangent.shape[1]
    n_grp, n_dev = lax.axis_size("grp"), lax.axis_size("ad")
    grp, me = lax.axis_index("grp"), lax.axis_index("ad")
    half_size = n_dev // 2
    spot = me % half_size
    capacity = max(2, 2 * rows // n_dev)
    slots = n_dev * capacity
    count, rank_size, _ = adapter_down_weight.shape
    seqs = frozen_margin_score.shape[1]
    lanes = count * rank_size
    down = adapter_down_weight.reshape(lanes, width)
    up = adapter_up_weight.reshape(lanes, out_width)

    def flipped(block, flip):
        return lax.ppermute(block, "ad", [(at, at ^ flip) for at in range(n_dev)])

    def other_grp(block):
        return lax.ppermute(block, "grp", [(0, 1), (1, 0)])

    def half(which):
        return jnp.concatenate(
            [
                lax.dynamic_index_in_dim(adapter_up_weight, which, keepdims=False),
                lax.dynamic_index_in_dim(adapter_down_weight, which, keepdims=False),
            ],
            axis=1,
        )

    half_mine = half(grp)
    far = flipped(half_mine, half_size)
    half_other = half(1 - grp)

    (owner,) = gate(lax.optimization_barrier((owner, half_mine))[0])
    slot_index = rows_by_slot(owner.reshape(1, rows), n_dev, capacity)[0]
    to_slot = (jnp.arange(slots, dtype=jnp.int32)[:, None] == slot_index[None, :]).astype(BF16)
    row_adapter = token_local_adapter[:, None] == jnp.arange(count, dtype=jnp.int32)
    row_seq = segment[0][:, None] == jnp.arange(seqs, dtype=jnp.int32)
    marks = jnp.concatenate([row_adapter, row_seq], axis=1).astype(BF16)
    marked = jnp.concatenate(
        [cotangent, jnp.pad(marks, ((0, 0), (0, MARKS - count - seqs)))], axis=1
    )
    sent = jnp.dot(
        to_slot, jnp.concatenate([tokens, marked], axis=1), preferred_element_type=BF16
    )

    halves = [list(range(half_size)), list(range(half_size, n_dev))]
    base = me - spot
    half_spot = jnp.arange(half_size, dtype=jnp.int32)[:, None, None]
    side = jnp.arange(2, dtype=jnp.int32)[None, :, None]
    half_slot = (((base + half_spot) ^ (side * half_size)) * capacity) + jnp.arange(
        capacity, dtype=jnp.int32
    )
    to_half = (half_slot[..., None] == slot_index).astype(BF16)
    half_g = lax.all_to_all(
        jnp.dot(to_half.reshape(slots, rows), marked, preferred_element_type=BF16).reshape(
            half_size, 2 * capacity, out_width + MARKS
        ),
        "ad",
        split_axis=0,
        concat_axis=0,
        tiled=True,
        axis_index_groups=halves,
    )

    lane = jnp.arange(MARKS, dtype=jnp.int32)[None, :]
    which = (lane == jnp.stack([grp, 1 - grp])[:, None]).astype(F32)

    def land(blocks):
        return [block if at == 0 else flipped(block, 2 * at) for at, block in enumerate(blocks)]

    def hand_over(blocks):
        return blocks + [flipped(jnp.concatenate([block[capacity:] for block in blocks]), 1)]

    made_near = project(
        0, False, capacity, out_width, width, spot, half_g, which, [half_mine], [half_other]
    )
    landed_near = land(made_near)
    (sent,) = gate(lax.optimization_barrier((sent, made_near))[0])
    got = lax.all_to_all(
        sent.reshape(n_dev, capacity, width + out_width + MARKS),
        "ad",
        split_axis=0,
        concat_axis=0,
        tiled=True,
    ).reshape(slots, width + out_width + MARKS)
    got_x = got[:, :width]

    got_g = got[:, width : width + out_width]
    slot_marks = got[:, width + out_width : width + out_width + count + seqs].astype(F32)
    member = jnp.repeat(slot_marks[:, :count], rank_size, axis=1)
    slot_seq_hot = slot_marks[:, count:].reshape(n_dev, capacity, seqs)

    contract = (((1,), (1,)), ((), ()))
    pulled = member * lax.dot_general(got_g, up, contract, preferred_element_type=F32)
    pulled_rows = pulled.astype(BF16)

    (far,) = gate(lax.optimization_barrier((far, sent, landed_near))[0])
    far_other = other_grp(far)
    kept, handed = project(
        1, True, capacity, out_width, width, spot, half_g, which, [far], [far_other]
    )
    taken = flipped(handed, 1)
    landed_far = land(
        [
            jnp.concatenate([kept[at : at + capacity], taken[at : at + capacity]])
            for at in range(0, half_size // 2 * capacity, capacity)
        ]
    )
    rows_contract = (((0,), (0,)), ((), ()))

    hidden_rows = (
        member * lax.dot_general(got_x, down, contract, preferred_element_type=F32)
    ).astype(BF16)
    inner_product = SCALE * jnp.sum(hidden_rows.astype(F32) * pulled, axis=1)
    part = jnp.sum(slot_seq_hot * inner_product.reshape(n_dev, capacity)[:, :, None], axis=1)
    chips = half_size // 2
    order = [2 * at for at in range(chips)] + [2 * at + 1 for at in range(chips)]
    near_flips = spot ^ jnp.array(order, dtype=jnp.int32)
    far_flips = spot ^ jnp.arange(half_size, dtype=jnp.int32)
    pick = jnp.concatenate([to_half[near_flips, 0], to_half[far_flips, 1]])
    pick = pick.reshape(slots, rows).T
    told = share(
        jnp.concatenate(
            [
                part.reshape(1, n_dev * seqs),
                pair_sequence_order.astype(F32),
                frozen_margin_score,
            ],
            axis=1,
        )
    )[:, 0]
    scores = jnp.sum(told[:, : n_dev * seqs], axis=0).reshape(n_dev, seqs)
    scores = scores + told[:, n_dev * seqs + seqs :]
    losses, seq_weight = pair_weights(
        scores, told[:, n_dev * seqs : n_dev * seqs + seqs].astype(jnp.int32)
    )

    slot_weight = LOSS_SCALE * jnp.sum(slot_seq_hot * seq_weight[:, None, :], axis=2).reshape(slots)
    upper = (slot_weight[:, None] * hidden_rows.astype(F32)).astype(BF16)
    lower = (slot_weight[:, None] * pulled_rows.astype(F32)).astype(BF16)
    grad_up = (
        SCALE * lax.dot_general(upper, got_g, rows_contract, preferred_element_type=F32)
    ).astype(BF16)
    grad_down = (
        SCALE * lax.dot_general(lower, got_x, rows_contract, preferred_element_type=F32)
    ).astype(BF16)

    my_weight = lax.dynamic_index_in_dim(seq_weight, me, keepdims=False)
    my_losses = lax.dynamic_index_in_dim(losses, me, keepdims=False)
    row_weight = LOSS_SCALE * jnp.sum(row_seq.astype(F32) * my_weight[None, :], axis=1)
    landed_far = lax.optimization_barrier((landed_far, told))[0]
    landed = hand_over(landed_near) + landed_far
    input_grad = select(
        pick,
        SCALE * row_weight[:, None],
        landed,
        [capacity] * chips + [chips * capacity] + [2 * capacity] * chips,
    )
    return (
        input_grad,
        grad_down.reshape(count, rank_size, width),
        grad_up.reshape(count, rank_size, out_width),
        my_losses,
    )


def solution(mesh):
    placed = (
        P(("grp", "ad"), None),
        P(("grp", "ad"), None),
        P(("grp", "ad"), None),
        P(("grp", "ad")),
        P(("grp", "ad"), None),
        P(("grp", "ad"), None),
        P(("grp", "ad"), None),
        P("ad", None, None),
        P("ad", None, None),
    )
    return jax.shard_map(
        body,
        mesh=mesh,
        in_specs=placed,
        out_specs=(
            P(("grp", "ad"), None),
            P(("grp", "ad"), None, None),
            P(("grp", "ad"), None, None),
            P(("grp", "ad")),
        ),
        check_vma=False,
    )
```

```python
import functools

import jax
import jax.numpy as jnp
from jax import lax
from jax.experimental import pallas as pl
from jax.experimental.pallas import tpu as pltpu
from jax.sharding import PartitionSpec as P

SCALE = 2.0
BETA = 0.1
LOSS_SCALE = 256.0
MARKS = 128
GATE_FLOPS = 2 * 10**11

F32 = jnp.float32
BF16 = jnp.bfloat16


def gate(*arrays):
    return pl.pallas_call(
        lambda *refs: None,
        out_shape=[jax.ShapeDtypeStruct(array.shape, array.dtype) for array in arrays],
        in_specs=[pl.BlockSpec(memory_space=pl.ANY)] * len(arrays),
        out_specs=[pl.BlockSpec(memory_space=pl.ANY)] * len(arrays),
        input_output_aliases={at: at for at in range(len(arrays))},
        cost_estimate=pl.CostEstimate(flops=GATE_FLOPS, bytes_accessed=0, transcendentals=0),
        name="gate",
    )(*arrays)


def project_kernel(side, split, capacity, out_width, n_outs, spot_ref, g_ref, which, *refs):
    n_spots = g_ref.shape[0]
    n_parts = (len(refs) - n_outs) // 2
    mine, other, outs = refs[:n_parts], refs[n_parts : 2 * n_parts], refs[2 * n_parts :]
    first = side * capacity
    spot = spot_ref[0]
    rows = jnp.concatenate(
        [g_ref[spot ^ flip, first : first + capacity, :] for flip in range(n_spots)], axis=0
    )
    marks = rows[:, out_width:].astype(F32)
    contract = (((1,), (1,)), ((), ()))
    pulls = []
    for at, parts in enumerate((mine, other)):
        member = jnp.sum(marks * which[at : at + 1, :], axis=1, keepdims=True)
        pull = lax.dot_general(
            rows[:, :out_width], parts[0][:, :out_width], contract, preferred_element_type=F32
        )
        pulls.append((member * pull).astype(BF16))
    done = 0
    for at in range(n_parts):
        start, end = (out_width if at == 0 else 0), mine[at].shape[1]
        while start < end:
            size = min(1024, end - start)
            columns = slice(start, start + size)
            made = jnp.dot(pulls[0], mine[at][:, columns], preferred_element_type=F32)
            made = made + jnp.dot(pulls[1], other[at][:, columns], preferred_element_type=F32)
            made = made.astype(BF16)
            for flip in range(n_spots):
                row = made[flip * capacity : (flip + 1) * capacity]
                if split:
                    chip = flip // 2 * capacity
                    outs[flip % 2][chip : chip + capacity, done : done + size] = row
                else:
                    core = flip % 2 * capacity
                    outs[flip // 2][core : core + capacity, done : done + size] = row
            start, done = start + size, done + size


def project(side, split, capacity, out_width, width, spot, got_g, which, mine, other):
    n_spots = got_g.shape[0]
    chips = n_spots // 2
    blocks = [(chips * capacity, width)] * 2 if split else [(2 * capacity, width)] * chips
    if capacity % 16 == 0:
        return pl.pallas_call(
            functools.partial(project_kernel, side, split, capacity, out_width, len(blocks)),
            out_shape=[jax.ShapeDtypeStruct(block, BF16) for block in blocks],
            in_specs=[pl.BlockSpec(memory_space=pltpu.SMEM)]
            + [pl.BlockSpec(memory_space=pltpu.VMEM)] * (2 + len(mine) + len(other)),
            cost_estimate=pl.CostEstimate(flops=1000, bytes_accessed=1000, transcendentals=0),
            name="project",
        )(spot.reshape(1), got_g, which, *mine, *other)
    order = spot ^ jnp.arange(n_spots, dtype=jnp.int32)
    rows = got_g[order, side * capacity : (side + 1) * capacity].reshape(n_spots * capacity, -1)
    marks = rows[:, out_width:].astype(F32)
    made = 0.0
    for at, parts in enumerate((mine, other)):
        whole = jnp.concatenate(parts, axis=1)
        pull = jnp.dot(rows[:, :out_width], whole[:, :out_width].T, preferred_element_type=F32)
        pull = (jnp.sum(marks * which[at], axis=1, keepdims=True) * pull).astype(BF16)
        made = made + jnp.dot(pull, whole[:, out_width:], preferred_element_type=F32)
    made = made.astype(BF16).reshape(chips, 2, capacity, width)
    if split:
        return [made[:, core].reshape(chips * capacity, width) for core in range(2)]
    return list(made.reshape(chips, 2 * capacity, width))


def iota(shape, axis):
    return lax.broadcasted_iota(jnp.int32, shape, axis)


def exact_dot(hot, values):
    return jnp.dot(hot, values, precision=lax.Precision.HIGHEST, preferred_element_type=F32)


def column_parts(width, columns):
    return [slice(start, min(start + columns, width)) for start in range(0, width, columns)]


def sequence_lanes(score_lanes, count, seqs):
    shape = (MARKS, score_lanes)
    return (iota(shape, 0) == count + iota(shape, 1) % seqs).astype(F32)


def score_kernel(
    count, seqs, rank_size, capacity, columns, own_ref, got_hbm, down_hbm, up_hbm, *refs
):
    hidden_ref, pulled_ref, told_ref, got, down, up, got_sems, down_sems, up_sem = refs
    width, out_width = down.shape[1], up.shape[1]
    parts = column_parts(width, columns)
    tail = slice(width, got.shape[1])
    copies = []
    for at, part in enumerate(parts):
        copies.append(
            (
                pltpu.make_async_copy(got_hbm.at[:, part], got.at[:, part], got_sems.at[at]),
                pltpu.make_async_copy(down_hbm.at[:, part], down.at[:, part], down_sems.at[at]),
            )
        )
    tail_copy = pltpu.make_async_copy(got_hbm.at[:, tail], got.at[:, tail], got_sems.at[len(parts)])
    up_copy = pltpu.make_async_copy(up_hbm, up, up_sem)
    tail_copy.start()
    up_copy.start()
    for pair in copies:
        for copy in pair:
            copy.start()
    contract = (((1,), (1,)), ((), ()))
    tail_copy.wait()
    up_copy.wait()
    marks = got[:, width + out_width :].astype(F32)
    slots, lanes = hidden_ref.shape
    lane = iota((slots, lanes), 1) // rank_size
    member = jnp.zeros((slots, lanes), F32)
    for which in range(count):
        member = jnp.where(lane == which, marks[:, which : which + 1], member)
    pulled = member * lax.dot_general(
        got[:, width : width + out_width], up[...], contract, preferred_element_type=F32
    )
    pulled_ref[...] = pulled.astype(BF16)
    total = jnp.zeros((slots, lanes), F32)
    for pair, part in zip(copies, parts):
        for copy in pair:
            copy.wait()
        total = total + lax.dot_general(
            got[:, part], down[:, part], contract, preferred_element_type=F32
        )
    hidden = (member * total).astype(BF16)
    hidden_ref[...] = hidden
    inner = SCALE * jnp.sum(hidden.astype(F32) * pulled, axis=1, keepdims=True)
    n_dev, _, all_lanes = told_ref.shape
    hot = iota((n_dev, slots), 1) // capacity == iota((n_dev, slots), 0)
    part = exact_dot(hot.astype(F32), marks * inner)
    score_lanes = all_lanes - MARKS
    spread = exact_dot(part, sequence_lanes(score_lanes, count, seqs))
    at_device = iota((n_dev, score_lanes), 0) == iota((n_dev, score_lanes), 1) // seqs
    row = jnp.sum(jnp.where(at_device, spread, 0.0), axis=0, keepdims=True)
    row = jnp.concatenate([row, jnp.zeros((1, MARKS), F32)], axis=1) + own_ref[...]
    told_ref[...] = jnp.broadcast_to(row[None], told_ref.shape)


def score(own, got, down, up, count, seqs, rank_size, n_dev):
    slots = got.shape[0]
    lanes, width = down.shape
    columns = up.shape[1]
    n_parts = len(column_parts(width, columns))
    vmem, hbm = pl.BlockSpec(memory_space=pltpu.VMEM), pl.BlockSpec(memory_space=pl.ANY)
    return pl.pallas_call(
        functools.partial(score_kernel, count, seqs, rank_size, slots // n_dev, columns),
        out_shape=[
            jax.ShapeDtypeStruct((slots, lanes), BF16),
            jax.ShapeDtypeStruct((slots, lanes), BF16),
            jax.ShapeDtypeStruct((n_dev,) + own.shape, F32),
        ],
        in_specs=[vmem, hbm, hbm, hbm],
        out_specs=[vmem] * 3,
        scratch_shapes=[
            pltpu.VMEM(got.shape, BF16),
            pltpu.VMEM(down.shape, BF16),
            pltpu.VMEM(up.shape, BF16),
            pltpu.SemaphoreType.DMA((n_parts + 1,)),
            pltpu.SemaphoreType.DMA((n_parts,)),
            pltpu.SemaphoreType.DMA,
        ],
        compiler_params=pltpu.CompilerParams(vmem_limit_bytes=16 * 2**20),
        cost_estimate=pl.CostEstimate(
            flops=2 * slots * lanes * (width + columns),
            bytes_accessed=2 * (slots + lanes) * (width + columns),
            transcendentals=0,
        ),
        name="score",
    )(own, got, down, up)


def weights(total, count, seqs):
    lane = iota(total.shape, 1)

    def column(at):
        return total[:, at : at + 1]

    pick = [[column(count + seqs + i * seqs + s) for s in range(seqs)] for i in range(seqs)]
    ordered = [sum(pick[i][s] * column(count + s) for s in range(seqs)) for i in range(seqs)]
    losses, by_order = jnp.zeros(total.shape, F32), []
    for pair in range(seqs // 2):
        margin = BETA * (ordered[2 * pair] - ordered[2 * pair + 1])
        loss = jnp.maximum(-margin, 0.0) + jnp.log1p(jnp.exp(-jnp.abs(margin)))
        losses = jnp.where(lane == pair, loss, losses)
        lean = 1.0 / (1.0 + jnp.exp(margin))
        by_order += [-BETA * lean, BETA * lean]
    table = jnp.zeros(total.shape, F32)
    for s in range(seqs):
        weight = LOSS_SCALE * sum(pick[i][s] * by_order[i] for i in range(seqs))
        table = jnp.where(lane == count + s, weight, table)
    return losses, table


def finish_kernel(count, seqs, capacity, columns, used, me_ref, told_ref, *refs):
    hidden_ref, pulled_ref, row_marks, got_hbm, *refs = refs
    if used:
        pick, *refs = refs
    block_hbms, refs = refs[: len(used)], refs[len(used) :]
    losses_ref, row_weight, up_hbm, down_hbm, *refs = refs
    if used:
        input_hbm, got, grad_up, grad_down, rows, input_grad, *sems = refs
        got_sems, up_sem, down_sems, block_sems, input_sems = sems
    else:
        got, grad_up, grad_down, got_sems, up_sem, down_sems = refs
    width, out_width = grad_down.shape[1], grad_up.shape[1]
    parts = column_parts(width, columns)
    tail = slice(width, got.shape[1])
    tail_copy = pltpu.make_async_copy(got_hbm.at[:, tail], got.at[:, tail], got_sems.at[len(parts)])
    copies = [
        pltpu.make_async_copy(got_hbm.at[:, part], got.at[:, part], got_sems.at[at])
        for at, part in enumerate(parts)
    ]
    first, block_copies = 0, []
    for at, size in enumerate(used):
        block_copies.append(
            pltpu.make_async_copy(
                block_hbms[at].at[pl.ds(0, size)], rows.at[pl.ds(first, size)], block_sems.at[at]
            )
        )
        first += size
    tail_copy.start()
    for copy in copies + block_copies:
        copy.start()

    told = jnp.concatenate([told_ref[at] for at in range(told_ref.shape[0])], axis=0)
    score_lanes = told.shape[1] - MARKS
    sums = jnp.sum(told[:, :score_lanes], axis=0, keepdims=True)
    shape = (told.shape[0], score_lanes)
    spread = jnp.where(iota(shape, 0) == iota(shape, 1) // seqs, sums, 0.0)
    total = told[:, score_lanes:] + lax.dot_general(
        spread,
        sequence_lanes(score_lanes, count, seqs),
        (((1,), (1,)), ((), ())),
        precision=lax.Precision.HIGHEST,
        preferred_element_type=F32,
    )
    losses, table = weights(total, count, seqs)
    n_dev, slots = total.shape[0], got.shape[0]
    mine = iota(total.shape, 0) == me_ref[0]
    pair_lane = iota(losses.shape, 1)
    for pair in range(seqs // 2):
        losses_ref[pair] = jnp.sum(jnp.where(mine & (pair_lane == pair), losses, 0.0))
    my_table = jnp.sum(jnp.where(mine, table, 0.0), axis=0, keepdims=True)
    my_weight = SCALE * jnp.sum(row_marks[...] * my_table, axis=1, keepdims=True)
    row_weight[...] = my_weight
    hot = iota((slots, n_dev), 0) // capacity == iota((slots, n_dev), 1)
    slot_table = exact_dot(hot.astype(F32), table)
    tail_copy.wait()
    marks = got[:, width + out_width :].astype(F32)
    weight = jnp.sum(marks * slot_table, axis=1, keepdims=True)
    lower = (weight * pulled_ref[...].astype(F32)).astype(BF16)
    upper = (weight * hidden_ref[...].astype(F32)).astype(BF16)
    contract = (((0,), (0,)), ((), ()))
    made = lax.dot_general(
        upper, got[:, width : width + out_width], contract, preferred_element_type=F32
    )
    grad_up[...] = (SCALE * made).astype(BF16)
    outs = [pltpu.make_async_copy(grad_up, up_hbm, up_sem)]
    outs[0].start()
    for at, part in enumerate(parts):
        copies[at].wait()
        made = lax.dot_general(lower, got[:, part], contract, preferred_element_type=F32)
        grad_down[:, part] = (SCALE * made).astype(BF16)
        outs.append(
            pltpu.make_async_copy(grad_down.at[:, part], down_hbm.at[:, part], down_sems.at[at])
        )
        outs[-1].start()
    if used:
        for copy in block_copies:
            copy.wait()
        for at, part in enumerate(parts):
            picked = jnp.dot(pick[...], rows[:, part], preferred_element_type=F32)
            input_grad[:, part] = (my_weight * picked).astype(BF16)
            outs.append(
                pltpu.make_async_copy(
                    input_grad.at[:, part], input_hbm.at[:, part], input_sems.at[at]
                )
            )
            outs[-1].start()
    for copy in outs:
        copy.wait()


def finish(
    me, told, got, hidden_rows, pulled_rows, row_marks, count, seqs, width, pick, blocks, used
):
    slots, lanes = hidden_rows.shape
    rows = row_marks.shape[0]
    n_dev = told.shape[0]
    columns = got.shape[1] - width - MARKS
    n_parts = len(column_parts(width, columns))
    together = not any(size % 16 for size in used)
    vmem, hbm = pl.BlockSpec(memory_space=pltpu.VMEM), pl.BlockSpec(memory_space=pl.ANY)
    sems = pltpu.SemaphoreType.DMA
    out_shape = [
        jax.ShapeDtypeStruct((seqs // 2,), F32),
        jax.ShapeDtypeStruct((rows, 1), F32),
        jax.ShapeDtypeStruct((lanes, columns), BF16),
        jax.ShapeDtypeStruct((lanes, width), BF16),
    ]
    in_specs = [pl.BlockSpec(memory_space=pltpu.SMEM)] + [vmem] * 4 + [hbm]
    operands = [me.reshape(1), told, hidden_rows, pulled_rows, row_marks, got]
    scratch = [
        pltpu.VMEM(got.shape, BF16),
        pltpu.VMEM((lanes, columns), BF16),
        pltpu.VMEM((lanes, width), BF16),
    ]
    scratch_sems = [sems((n_parts + 1,)), sems, sems((n_parts,))]
    if together:
        out_shape.append(jax.ShapeDtypeStruct((rows, width), BF16))
        in_specs += [vmem] + [hbm] * len(blocks)
        operands += [pick, *blocks]
        scratch += [pltpu.VMEM((slots, width), BF16), pltpu.VMEM((rows, width), BF16)]
        scratch_sems += [sems((len(blocks),)), sems((n_parts,))]
    losses, row_weight, grad_up, grad_down, *input_grad = pl.pallas_call(
        functools.partial(
            finish_kernel, count, seqs, slots // n_dev, columns, used if together else []
        ),
        out_shape=out_shape,
        in_specs=in_specs,
        out_specs=[pl.BlockSpec(memory_space=pltpu.SMEM), vmem] + [hbm] * (len(out_shape) - 2),
        scratch_shapes=scratch + scratch_sems,
        compiler_params=pltpu.CompilerParams(vmem_limit_bytes=24 * 2**20),
        cost_estimate=pl.CostEstimate(
            flops=4 * slots * lanes * width,
            bytes_accessed=2 * (2 * slots + lanes + rows) * width,
            transcendentals=0,
        ),
        name="finish",
    )(*operands)
    if not together:
        blocks = jnp.concatenate([block[:size] for block, size in zip(blocks, used)])
        picked = jnp.dot(pick, blocks, preferred_element_type=F32)
        input_grad = [(row_weight * picked).astype(BF16)]
    return input_grad[0], grad_down, grad_up, losses


def slots_kernel(
    count, capacity, half_size, half_ref, owner_ref, adapter_ref, segment_ref, g_ref, *refs
):
    to_slot, to_half, marks_ref, sent_g = refs
    slots, rows = to_slot.shape
    out_width = g_ref.shape[1]
    eye = (iota((rows, rows), 0) == iota((rows, rows), 1)).astype(BF16)
    owner = lax.dot_general(
        owner_ref[...].astype(F32).astype(BF16),
        eye,
        (((0,), (0,)), ((), ())),
        preferred_element_type=F32,
    ).astype(jnp.int32)
    n_dev = 2 * half_size
    hot = (iota((n_dev, rows), 0) == owner).astype(F32)
    earlier = (iota((rows, rows), 0) < iota((rows, rows), 1)).astype(BF16)
    before = jnp.dot(hot.astype(BF16), earlier, preferred_element_type=F32)
    rank = jnp.sum(before * hot, axis=0, keepdims=True).astype(jnp.int32)
    at_slot = iota((slots, rows), 0)
    to_slot[...] = (at_slot == owner * capacity + rank).astype(BF16)
    far = owner // half_size != half_ref[0]
    position = (owner % half_size * 2 + far.astype(jnp.int32)) * capacity + rank
    hot_half = (at_slot == position).astype(BF16)
    to_half[...] = hot_half
    lane = iota((MARKS, rows), 0)
    marks = ((lane == adapter_ref[...]) | (lane == segment_ref[...] + count)).astype(BF16)
    marks_ref[...] = marks
    sent_g[:, :out_width] = jnp.dot(hot_half, g_ref[...], preferred_element_type=F32).astype(BF16)
    sent_g[:, out_width:] = lax.dot_general(
        hot_half, marks, (((1,), (1,)), ((), ())), preferred_element_type=F32
    ).astype(BF16)


def slot_rows(half_at, owner, adapter, segment, cotangent, count, capacity, half_size):
    rows, out_width = cotangent.shape
    slots = 2 * half_size * capacity
    vmem = pl.BlockSpec(memory_space=pltpu.VMEM)
    return pl.pallas_call(
        functools.partial(slots_kernel, count, capacity, half_size),
        out_shape=[
            jax.ShapeDtypeStruct((slots, rows), BF16),
            jax.ShapeDtypeStruct((slots, rows), BF16),
            jax.ShapeDtypeStruct((MARKS, rows), BF16),
            jax.ShapeDtypeStruct((slots, out_width + MARKS), BF16),
        ],
        in_specs=[pl.BlockSpec(memory_space=pltpu.SMEM)] + [vmem] * 4,
        out_specs=[vmem] * 4,
        name="slots",
    )(half_at.reshape(1), owner, adapter.reshape(1, rows), segment, cotangent)


def send_kernel(columns, to_slot, marks, g_ref, tokens_hbm, sent_hbm, tokens, sent, *sems):
    in_sems, out_sems = sems
    width, out_width = tokens.shape[1], g_ref.shape[1]
    parts = column_parts(width, columns)
    copies = [
        pltpu.make_async_copy(tokens_hbm.at[:, part], tokens.at[:, part], in_sems.at[at])
        for at, part in enumerate(parts)
    ]
    for copy in copies:
        copy.start()
    hot = to_slot[...]
    last = slice(width + out_width, width + out_width + MARKS)
    sent[:, width : width + out_width] = jnp.dot(
        hot, g_ref[...], preferred_element_type=F32
    ).astype(BF16)
    sent[:, last] = lax.dot_general(
        hot, marks[...], (((1,), (1,)), ((), ())), preferred_element_type=F32
    ).astype(BF16)
    outs = []

    def send(part):
        outs.append(
            pltpu.make_async_copy(
                sent.at[:, part], sent_hbm.at[:, part], out_sems.at[len(outs)]
            )
        )
        outs[-1].start()

    send(slice(width, width + out_width + MARKS))
    for copy, part in zip(copies, parts):
        copy.wait()
        sent[:, part] = jnp.dot(hot, tokens[:, part], preferred_element_type=F32).astype(BF16)
        send(part)
    for copy in outs:
        copy.wait()


def send_rows(to_slot, marks, cotangent, tokens):
    slots, (rows, width) = to_slot.shape[0], tokens.shape
    columns = cotangent.shape[1]
    full = width + columns + MARKS
    n_parts = len(column_parts(width, columns))
    vmem, hbm = pl.BlockSpec(memory_space=pltpu.VMEM), pl.BlockSpec(memory_space=pl.ANY)
    return pl.pallas_call(
        functools.partial(send_kernel, columns),
        out_shape=jax.ShapeDtypeStruct((slots, full), BF16),
        in_specs=[vmem] * 3 + [hbm],
        out_specs=hbm,
        scratch_shapes=[
            pltpu.VMEM((rows, width), BF16),
            pltpu.VMEM((slots, full), BF16),
            pltpu.SemaphoreType.DMA((n_parts,)),
            pltpu.SemaphoreType.DMA((n_parts + 1,)),
        ],
        compiler_params=pltpu.CompilerParams(vmem_limit_bytes=32 * 2**20),
        cost_estimate=pl.CostEstimate(
            flops=2 * slots * rows * full,
            bytes_accessed=2 * (slots + rows) * full,
            transcendentals=0,
        ),
        name="send",
    )(to_slot, marks, cotangent, tokens)


def half_kernel(which_ref, up_hbm, down_hbm, out, sems):
    out_width, which = up_hbm.shape[2], which_ref[0]
    width = down_hbm.shape[2]
    copies = [
        pltpu.make_async_copy(up_hbm.at[which], out.at[:, pl.ds(0, out_width)], sems.at[0]),
        pltpu.make_async_copy(
            down_hbm.at[which], out.at[:, pl.ds(out_width, width)], sems.at[1]
        ),
    ]
    for copy in copies:
        copy.start()
    for copy in copies:
        copy.wait()


def half_of(which, up_pair, down_pair):
    _, rank_size, width = down_pair.shape
    hbm = pl.BlockSpec(memory_space=pl.ANY)
    return pl.pallas_call(
        half_kernel,
        out_shape=jax.ShapeDtypeStruct((rank_size, up_pair.shape[2] + width), BF16),
        in_specs=[pl.BlockSpec(memory_space=pltpu.SMEM), hbm, hbm],
        out_specs=pl.BlockSpec(memory_space=pltpu.VMEM),
        scratch_shapes=[pltpu.SemaphoreType.DMA((2,))],
        name="half",
    )(which.reshape(1), up_pair, down_pair)


def body(
    tokens,
    cotangent,
    owner,
    token_local_adapter,
    segment,
    pair_sequence_order,
    frozen_margin_score,
    adapter_down_weight,
    adapter_up_weight,
):
    rows, width = tokens.shape
    out_width = cotangent.shape[1]
    n_grp, n_dev = lax.axis_size("grp"), lax.axis_size("ad")
    grp, me = lax.axis_index("grp"), lax.axis_index("ad")
    half_size = n_dev // 2
    spot = me % half_size
    capacity = max(2, 2 * rows // n_dev)
    slots = n_dev * capacity
    count, rank_size, _ = adapter_down_weight.shape
    seqs = frozen_margin_score.shape[1]
    lanes = count * rank_size
    down = adapter_down_weight.reshape(lanes, width)
    up = adapter_up_weight.reshape(lanes, out_width)

    def flipped(block, flip):
        return lax.ppermute(block, "ad", [(at, at ^ flip) for at in range(n_dev)])

    def other_grp(block):
        return lax.ppermute(block, "grp", [(0, 1), (1, 0)])

    half_mine = half_of(grp, adapter_up_weight, adapter_down_weight)
    far = flipped(half_mine, half_size)
    half_other = half_of(1 - grp, adapter_up_weight, adapter_down_weight)

    (owner,) = gate(lax.optimization_barrier((owner, half_mine))[0])
    row_seq = segment[0][:, None] == jnp.arange(seqs, dtype=jnp.int32)
    to_slot, to_half, marks, sent_g = slot_rows(
        me // half_size, owner, token_local_adapter, segment, cotangent, count, capacity, half_size
    )
    sent = send_rows(to_slot, marks, cotangent, tokens)

    halves = [list(range(half_size)), list(range(half_size, n_dev))]
    to_half = to_half.reshape(half_size, 2, capacity, rows)
    half_g = lax.all_to_all(
        sent_g.reshape(half_size, 2 * capacity, out_width + MARKS),
        "ad",
        split_axis=0,
        concat_axis=0,
        tiled=True,
        axis_index_groups=halves,
    )

    lane = jnp.arange(MARKS, dtype=jnp.int32)[None, :]
    which = (lane == jnp.stack([grp, 1 - grp])[:, None]).astype(F32)

    def land(blocks):
        return [block if at == 0 else flipped(block, 2 * at) for at, block in enumerate(blocks)]

    def hand_over(blocks):
        return blocks + [flipped(jnp.concatenate([block[capacity:] for block in blocks]), 1)]

    made_near = project(
        0, False, capacity, out_width, width, spot, half_g, which, [half_mine], [half_other]
    )
    landed_near = land(made_near)
    (sent,) = gate(lax.optimization_barrier((sent, made_near))[0])
    got = lax.all_to_all(
        sent.reshape(n_dev, capacity, width + out_width + MARKS),
        "ad",
        split_axis=0,
        concat_axis=0,
        tiled=True,
    ).reshape(slots, width + out_width + MARKS)

    (which_far,) = gate(lax.optimization_barrier((which, sent, landed_near))[0])
    far_other = other_grp(far)
    kept, handed = project(
        1, True, capacity, out_width, width, spot, half_g, which_far, [far], [far_other]
    )
    taken = flipped(handed, 1)
    landed_far = land(
        [
            jnp.concatenate([kept[at : at + capacity], taken[at : at + capacity]])
            for at in range(0, half_size // 2 * capacity, capacity)
        ]
    )
    pair_hot = pair_sequence_order[0][:, None] == jnp.arange(seqs, dtype=jnp.int32)
    at_me = (jnp.arange(n_dev, dtype=jnp.int32) == me)[:, None]
    own_scores = jnp.where(at_me, frozen_margin_score, 0.0).reshape(1, -1)
    own = jnp.concatenate(
        [
            jnp.pad(own_scores, ((0, 0), (0, -own_scores.shape[1] % MARKS))),
            jnp.zeros((1, count + seqs), F32),
            pair_hot.astype(F32).reshape(1, -1),
            jnp.zeros((1, MARKS - count - seqs - seqs * seqs), F32),
        ],
        axis=1,
    )
    hidden_rows, pulled_rows, part = score(own, got, down, up, count, seqs, rank_size, n_dev)
    told = lax.all_to_all(part, "ad", split_axis=0, concat_axis=0, tiled=True)

    chips = half_size // 2
    order = [2 * at for at in range(chips)] + [2 * at + 1 for at in range(chips)]
    near_flips = spot ^ jnp.array(order, dtype=jnp.int32)
    far_flips = spot ^ jnp.arange(half_size, dtype=jnp.int32)
    pick = jnp.concatenate([to_half[near_flips, 0], to_half[far_flips, 1]])
    pick = pick.reshape(slots, rows).T
    landed_far = lax.optimization_barrier((landed_far, told))[0]
    landed = hand_over(landed_near) + landed_far
    row_marks = jnp.pad(row_seq.astype(F32), ((0, 0), (count, MARKS - count - seqs)))
    input_grad, grad_down, grad_up, losses = finish(
        me,
        told,
        got,
        hidden_rows,
        pulled_rows,
        row_marks,
        count,
        seqs,
        width,
        pick,
        landed,
        [capacity] * chips + [chips * capacity] + [2 * capacity] * chips,
    )
    return (
        input_grad,
        grad_down.reshape(count, rank_size, width),
        grad_up.reshape(count, rank_size, out_width),
        losses,
    )


def solution(mesh):
    placed = (
        P(("grp", "ad"), None),
        P(("grp", "ad"), None),
        P(("grp", "ad"), None),
        P(("grp", "ad")),
        P(("grp", "ad"), None),
        P(("grp", "ad"), None),
        P(("grp", "ad"), None),
        P("ad", None, None),
        P("ad", None, None),
    )
    return jax.shard_map(
        body,
        mesh=mesh,
        in_specs=placed,
        out_specs=(
            P(("grp", "ad"), None),
            P(("grp", "ad"), None, None),
            P(("grp", "ad"), None, None),
            P(("grp", "ad")),
        ),
        check_vma=False,
    )
```

```python
import functools

import jax
import jax.numpy as jnp
from jax import lax
from jax.experimental import pallas as pl
from jax.experimental.pallas import tpu as pltpu
from jax.sharding import PartitionSpec as P

SCALE = 2.0
BETA = 0.1
LOSS_SCALE = 256.0
MARKS = 128
GATE_FLOPS = 2 * 10**11

F32 = jnp.float32
BF16 = jnp.bfloat16


def gate(*arrays):
    return pl.pallas_call(
        lambda *refs: None,
        out_shape=[jax.ShapeDtypeStruct(array.shape, array.dtype) for array in arrays],
        in_specs=[pl.BlockSpec(memory_space=pl.ANY)] * len(arrays),
        out_specs=[pl.BlockSpec(memory_space=pl.ANY)] * len(arrays),
        input_output_aliases={at: at for at in range(len(arrays))},
        cost_estimate=pl.CostEstimate(flops=GATE_FLOPS, bytes_accessed=0, transcendentals=0),
        name="gate",
    )(*arrays)


def project_kernel(side, split, capacity, out_width, n_outs, spot_ref, g_ref, which, *refs):
    n_spots = g_ref.shape[0]
    n_parts = (len(refs) - n_outs) // 2
    mine, other, outs = refs[:n_parts], refs[n_parts : 2 * n_parts], refs[2 * n_parts :]
    first = side * capacity
    spot = spot_ref[0]
    rows = jnp.concatenate(
        [g_ref[spot ^ flip, first : first + capacity, :] for flip in range(n_spots)], axis=0
    )
    marks = rows[:, out_width:].astype(F32)
    contract = (((1,), (1,)), ((), ()))
    pulls = []
    for at, parts in enumerate((mine, other)):
        member = jnp.sum(marks * which[at : at + 1, :], axis=1, keepdims=True)
        pull = lax.dot_general(
            rows[:, :out_width], parts[0][:, :out_width], contract, preferred_element_type=F32
        )
        pulls.append((member * pull).astype(BF16))
    done = 0
    for at in range(n_parts):
        start, end = (out_width if at == 0 else 0), mine[at].shape[1]
        while start < end:
            size = min(1024, end - start)
            columns = slice(start, start + size)
            made = jnp.dot(pulls[0], mine[at][:, columns], preferred_element_type=F32)
            made = made + jnp.dot(pulls[1], other[at][:, columns], preferred_element_type=F32)
            made = made.astype(BF16)
            for flip in range(n_spots):
                row = made[flip * capacity : (flip + 1) * capacity]
                if split:
                    chip = flip // 2 * capacity
                    outs[flip % 2][chip : chip + capacity, done : done + size] = row
                else:
                    core = flip % 2 * capacity
                    outs[flip // 2][core : core + capacity, done : done + size] = row
            start, done = start + size, done + size


def project(side, split, capacity, out_width, width, spot, got_g, which, mine, other):
    n_spots = got_g.shape[0]
    chips = n_spots // 2
    blocks = [(chips * capacity, width)] * 2 if split else [(2 * capacity, width)] * chips
    if capacity % 16 == 0:
        return pl.pallas_call(
            functools.partial(project_kernel, side, split, capacity, out_width, len(blocks)),
            out_shape=[jax.ShapeDtypeStruct(block, BF16) for block in blocks],
            in_specs=[pl.BlockSpec(memory_space=pltpu.SMEM)]
            + [pl.BlockSpec(memory_space=pltpu.VMEM)] * (2 + len(mine) + len(other)),
            cost_estimate=pl.CostEstimate(flops=1000, bytes_accessed=1000, transcendentals=0),
            name="project",
        )(spot.reshape(1), got_g, which, *mine, *other)
    order = spot ^ jnp.arange(n_spots, dtype=jnp.int32)
    rows = got_g[order, side * capacity : (side + 1) * capacity].reshape(n_spots * capacity, -1)
    marks = rows[:, out_width:].astype(F32)
    made = 0.0
    for at, parts in enumerate((mine, other)):
        whole = jnp.concatenate(parts, axis=1)
        pull = jnp.dot(rows[:, :out_width], whole[:, :out_width].T, preferred_element_type=F32)
        pull = (jnp.sum(marks * which[at], axis=1, keepdims=True) * pull).astype(BF16)
        made = made + jnp.dot(pull, whole[:, out_width:], preferred_element_type=F32)
    made = made.astype(BF16).reshape(chips, 2, capacity, width)
    if split:
        return [made[:, core].reshape(chips * capacity, width) for core in range(2)]
    return list(made.reshape(chips, 2 * capacity, width))


def iota(shape, axis):
    return lax.broadcasted_iota(jnp.int32, shape, axis)


def exact_dot(hot, values):
    return jnp.dot(hot, values, precision=lax.Precision.HIGHEST, preferred_element_type=F32)


def column_parts(width, columns):
    return [slice(start, min(start + columns, width)) for start in range(0, width, columns)]


def sequence_lanes(score_lanes, count, seqs):
    shape = (MARKS, score_lanes)
    return (iota(shape, 0) == count + iota(shape, 1) % seqs).astype(F32)


def score_kernel(
    count, seqs, rank_size, capacity, columns, own_ref, got_hbm, down, up, *refs
):
    told_ref, rows_hbm, got, rank_rows, got_sems, rows_sem = refs
    width, out_width = down.shape[1], up.shape[1]
    parts = column_parts(width, columns)
    tail = slice(width, got.shape[1])
    copies = []
    for at, part in enumerate(parts):
        copies.append(
            (pltpu.make_async_copy(got_hbm.at[:, part], got.at[:, part], got_sems.at[at]),)
        )
    tail_copy = pltpu.make_async_copy(got_hbm.at[:, tail], got.at[:, tail], got_sems.at[len(parts)])
    tail_copy.start()
    for pair in copies:
        for copy in pair:
            copy.start()
    contract = (((1,), (1,)), ((), ()))
    tail_copy.wait()
    marks = got[:, width + out_width :].astype(F32)
    slots, lanes = got.shape[0], down.shape[0]
    lane = iota((slots, lanes), 1) // rank_size
    member = jnp.zeros((slots, lanes), F32)
    for which in range(count):
        member = jnp.where(lane == which, marks[:, which : which + 1], member)
    pulled = member * lax.dot_general(
        got[:, width : width + out_width], up[...], contract, preferred_element_type=F32
    )
    rank_rows[:, lanes:] = pulled.astype(BF16)
    total = jnp.zeros((slots, lanes), F32)
    for pair, part in zip(copies, parts):
        for copy in pair:
            copy.wait()
        total = total + lax.dot_general(
            got[:, part], down[:, part], contract, preferred_element_type=F32
        )
    hidden = (member * total).astype(BF16)
    rank_rows[:, :lanes] = hidden
    rows_copy = pltpu.make_async_copy(rank_rows, rows_hbm, rows_sem)
    rows_copy.start()
    inner = SCALE * jnp.sum(hidden.astype(F32) * pulled, axis=1, keepdims=True)
    n_dev, _, all_lanes = told_ref.shape
    hot = iota((n_dev, slots), 1) // capacity == iota((n_dev, slots), 0)
    part = exact_dot(hot.astype(F32), marks * inner)
    score_lanes = all_lanes - MARKS
    spread = exact_dot(part, sequence_lanes(score_lanes, count, seqs))
    at_device = iota((n_dev, score_lanes), 0) == iota((n_dev, score_lanes), 1) // seqs
    row = jnp.sum(jnp.where(at_device, spread, 0.0), axis=0, keepdims=True)
    row = jnp.concatenate([row, jnp.zeros((1, MARKS), F32)], axis=1) + own_ref[...]
    told_ref[...] = jnp.broadcast_to(row[None], told_ref.shape)
    rows_copy.wait()


def score(own, got, down, up, count, seqs, rank_size, n_dev):
    slots = got.shape[0]
    lanes, width = down.shape
    columns = up.shape[1]
    n_parts = len(column_parts(width, columns))
    vmem, hbm = pl.BlockSpec(memory_space=pltpu.VMEM), pl.BlockSpec(memory_space=pl.ANY)
    return pl.pallas_call(
        functools.partial(score_kernel, count, seqs, rank_size, slots // n_dev, columns),
        out_shape=[
            jax.ShapeDtypeStruct((n_dev,) + own.shape, F32),
            pltpu.HBM((slots, 2 * lanes), BF16),
        ],
        in_specs=[vmem, hbm, vmem, vmem],
        out_specs=[vmem, pl.BlockSpec(memory_space=pltpu.HBM)],
        scratch_shapes=[
            pltpu.VMEM(got.shape, BF16),
            pltpu.VMEM((slots, 2 * lanes), BF16),
            pltpu.SemaphoreType.DMA((n_parts + 1,)),
            pltpu.SemaphoreType.DMA,
        ],
        compiler_params=pltpu.CompilerParams(vmem_limit_bytes=16 * 2**20),
        cost_estimate=pl.CostEstimate(
            flops=2 * slots * lanes * (width + columns),
            bytes_accessed=2 * (slots + lanes) * (width + columns),
            transcendentals=0,
        ),
        name="score",
    )(own, got, down, up)


def weights(total, count, seqs):
    lane = iota(total.shape, 1)

    def column(at):
        return total[:, at : at + 1]

    pick = [[column(count + seqs + i * seqs + s) for s in range(seqs)] for i in range(seqs)]
    ordered = [sum(pick[i][s] * column(count + s) for s in range(seqs)) for i in range(seqs)]
    losses, by_order = jnp.zeros(total.shape, F32), []
    for pair in range(seqs // 2):
        margin = BETA * (ordered[2 * pair] - ordered[2 * pair + 1])
        loss = jnp.maximum(-margin, 0.0) + jnp.log1p(jnp.exp(-jnp.abs(margin)))
        losses = jnp.where(lane == pair, loss, losses)
        lean = 1.0 / (1.0 + jnp.exp(margin))
        by_order += [-BETA * lean, BETA * lean]
    table = jnp.zeros(total.shape, F32)
    for s in range(seqs):
        weight = LOSS_SCALE * sum(pick[i][s] * by_order[i] for i in range(seqs))
        table = jnp.where(lane == count + s, weight, table)
    return losses, table


def finish_kernel(count, seqs, capacity, columns, used, me_ref, told_ref, *refs):
    row_marks, rank_hbm, got_hbm, *refs = refs
    if used:
        pick, *refs = refs
    block_hbms, refs = refs[: len(used)], refs[len(used) :]
    losses_ref, row_weight, up_hbm, down_hbm, *refs = refs
    if used:
        input_hbm, rank_rows, got, grad_up, grad_down, rows, input_grad, *sems = refs
        rank_sem, got_sems, up_sem, down_sems, block_sems, input_sems = sems
    else:
        rank_rows, got, grad_up, grad_down, rank_sem, got_sems, up_sem, down_sems = refs
    width, out_width = grad_down.shape[1], grad_up.shape[1]
    parts = column_parts(width, columns)
    tail = slice(width, got.shape[1])
    tail_copy = pltpu.make_async_copy(got_hbm.at[:, tail], got.at[:, tail], got_sems.at[len(parts)])
    copies = [
        pltpu.make_async_copy(got_hbm.at[:, part], got.at[:, part], got_sems.at[at])
        for at, part in enumerate(parts)
    ]
    first, block_copies = 0, []
    for at, size in enumerate(used):
        block_copies.append(
            pltpu.make_async_copy(
                block_hbms[at].at[pl.ds(0, size)], rows.at[pl.ds(first, size)], block_sems.at[at]
            )
        )
        first += size
    rank_copy = pltpu.make_async_copy(rank_hbm, rank_rows, rank_sem)
    rank_copy.start()
    tail_copy.start()
    for copy in copies + block_copies:
        copy.start()

    told = jnp.concatenate([told_ref[at] for at in range(told_ref.shape[0])], axis=0)
    score_lanes = told.shape[1] - MARKS
    sums = jnp.sum(told[:, :score_lanes], axis=0, keepdims=True)
    shape = (told.shape[0], score_lanes)
    spread = jnp.where(iota(shape, 0) == iota(shape, 1) // seqs, sums, 0.0)
    total = told[:, score_lanes:] + lax.dot_general(
        spread,
        sequence_lanes(score_lanes, count, seqs),
        (((1,), (1,)), ((), ())),
        precision=lax.Precision.HIGHEST,
        preferred_element_type=F32,
    )
    losses, table = weights(total, count, seqs)
    n_dev, slots = total.shape[0], got.shape[0]
    mine = iota(total.shape, 0) == me_ref[0]
    pair_lane = iota(losses.shape, 1)
    for pair in range(seqs // 2):
        losses_ref[pair] = jnp.sum(jnp.where(mine & (pair_lane == pair), losses, 0.0))
    my_table = jnp.sum(jnp.where(mine, table, 0.0), axis=0, keepdims=True)
    my_weight = SCALE * jnp.sum(row_marks[...] * my_table, axis=1, keepdims=True)
    row_weight[...] = my_weight
    hot = iota((slots, n_dev), 0) // capacity == iota((slots, n_dev), 1)
    slot_table = exact_dot(hot.astype(F32), table)
    tail_copy.wait()
    marks = got[:, width + out_width :].astype(F32)
    weight = jnp.sum(marks * slot_table, axis=1, keepdims=True)
    rank_copy.wait()
    lanes = grad_up.shape[0]
    upper = (weight * rank_rows[:, :lanes].astype(F32)).astype(BF16)
    lower = (weight * rank_rows[:, lanes:].astype(F32)).astype(BF16)
    contract = (((0,), (0,)), ((), ()))
    made = lax.dot_general(
        upper, got[:, width : width + out_width], contract, preferred_element_type=F32
    )
    grad_up[...] = (SCALE * made).astype(BF16)
    outs = [pltpu.make_async_copy(grad_up, up_hbm, up_sem)]
    outs[0].start()
    for at, part in enumerate(parts):
        copies[at].wait()
        made = lax.dot_general(lower, got[:, part], contract, preferred_element_type=F32)
        grad_down[:, part] = (SCALE * made).astype(BF16)
        outs.append(
            pltpu.make_async_copy(grad_down.at[:, part], down_hbm.at[:, part], down_sems.at[at])
        )
        outs[-1].start()
    if used:
        for copy in block_copies:
            copy.wait()
        for at, part in enumerate(parts):
            picked = jnp.dot(pick[...], rows[:, part], preferred_element_type=F32)
            input_grad[:, part] = (my_weight * picked).astype(BF16)
            outs.append(
                pltpu.make_async_copy(
                    input_grad.at[:, part], input_hbm.at[:, part], input_sems.at[at]
                )
            )
            outs[-1].start()
    for copy in outs:
        copy.wait()


def finish(
    me, told, got, rank_rows, row_marks, count, seqs, width, pick, blocks, used
):
    slots, lanes = rank_rows.shape[0], rank_rows.shape[1] // 2
    rows = row_marks.shape[0]
    n_dev = told.shape[0]
    columns = got.shape[1] - width - MARKS
    n_parts = len(column_parts(width, columns))
    together = not any(size % 16 for size in used)
    vmem, hbm = pl.BlockSpec(memory_space=pltpu.VMEM), pl.BlockSpec(memory_space=pltpu.HBM)
    sems = pltpu.SemaphoreType.DMA
    out_shape = [
        jax.ShapeDtypeStruct((seqs // 2,), F32),
        jax.ShapeDtypeStruct((rows, 1), F32),
        jax.ShapeDtypeStruct((lanes, columns), BF16),
        jax.ShapeDtypeStruct((lanes, width), BF16),
    ]
    in_specs = [pl.BlockSpec(memory_space=pltpu.SMEM)] + [vmem] * 2 + [hbm] * 2
    rank_rows = pltpu.with_memory_space_constraint(rank_rows, pltpu.HBM)
    operands = [me.reshape(1), told, row_marks, rank_rows, got]
    scratch = [
        pltpu.VMEM(rank_rows.shape, BF16),
        pltpu.VMEM(got.shape, BF16),
        pltpu.VMEM((lanes, columns), BF16),
        pltpu.VMEM((lanes, width), BF16),
    ]
    scratch_sems = [sems, sems((n_parts + 1,)), sems, sems((n_parts,))]
    if together:
        out_shape.append(jax.ShapeDtypeStruct((rows, width), BF16))
        in_specs += [vmem] + [hbm] * len(blocks)
        operands += [pick, *blocks]
        scratch += [pltpu.VMEM((slots, width), BF16), pltpu.VMEM((rows, width), BF16)]
        scratch_sems += [sems((len(blocks),)), sems((n_parts,))]
    losses, row_weight, grad_up, grad_down, *input_grad = pl.pallas_call(
        functools.partial(
            finish_kernel, count, seqs, slots // n_dev, columns, used if together else []
        ),
        out_shape=out_shape,
        in_specs=in_specs,
        out_specs=[pl.BlockSpec(memory_space=pltpu.SMEM), vmem] + [hbm] * (len(out_shape) - 2),
        scratch_shapes=scratch + scratch_sems,
        compiler_params=pltpu.CompilerParams(vmem_limit_bytes=24 * 2**20),
        cost_estimate=pl.CostEstimate(
            flops=4 * slots * lanes * width,
            bytes_accessed=2 * (2 * slots + lanes + rows) * width,
            transcendentals=0,
        ),
        name="finish",
    )(*operands)
    if not together:
        blocks = jnp.concatenate([block[:size] for block, size in zip(blocks, used)])
        picked = jnp.dot(pick, blocks, preferred_element_type=F32)
        input_grad = [(row_weight * picked).astype(BF16)]
    return input_grad[0], grad_down, grad_up, losses


def slots_kernel(
    count, capacity, half_size, half_ref, owner_ref, adapter_ref, segment_ref, g_ref, *refs
):
    to_slot, to_half, marks_ref, sent_g = refs
    slots, rows = to_slot.shape
    out_width = g_ref.shape[1]
    eye = (iota((rows, rows), 0) == iota((rows, rows), 1)).astype(BF16)
    owner = lax.dot_general(
        owner_ref[...].astype(F32).astype(BF16),
        eye,
        (((0,), (0,)), ((), ())),
        preferred_element_type=F32,
    ).astype(jnp.int32)
    n_dev = 2 * half_size
    hot = (iota((n_dev, rows), 0) == owner).astype(F32)
    earlier = (iota((rows, rows), 0) < iota((rows, rows), 1)).astype(BF16)
    before = jnp.dot(hot.astype(BF16), earlier, preferred_element_type=F32)
    rank = jnp.sum(before * hot, axis=0, keepdims=True).astype(jnp.int32)
    at_slot = iota((slots, rows), 0)
    to_slot[...] = (at_slot == owner * capacity + rank).astype(BF16)
    far = owner // half_size != half_ref[0]
    position = (owner % half_size * 2 + far.astype(jnp.int32)) * capacity + rank
    hot_half = (at_slot == position).astype(BF16)
    to_half[...] = hot_half
    lane = iota((MARKS, rows), 0)
    marks = ((lane == adapter_ref[...]) | (lane == segment_ref[...] + count)).astype(BF16)
    marks_ref[...] = marks
    sent_g[:, :out_width] = jnp.dot(hot_half, g_ref[...], preferred_element_type=F32).astype(BF16)
    sent_g[:, out_width:] = lax.dot_general(
        hot_half, marks, (((1,), (1,)), ((), ())), preferred_element_type=F32
    ).astype(BF16)


def slot_rows(half_at, owner, adapter, segment, cotangent, count, capacity, half_size):
    rows, out_width = cotangent.shape
    slots = 2 * half_size * capacity
    vmem = pl.BlockSpec(memory_space=pltpu.VMEM)
    return pl.pallas_call(
        functools.partial(slots_kernel, count, capacity, half_size),
        out_shape=[
            jax.ShapeDtypeStruct((slots, rows), BF16),
            jax.ShapeDtypeStruct((slots, rows), BF16),
            jax.ShapeDtypeStruct((MARKS, rows), BF16),
            jax.ShapeDtypeStruct((slots, out_width + MARKS), BF16),
        ],
        in_specs=[pl.BlockSpec(memory_space=pltpu.SMEM)] + [vmem] * 4,
        out_specs=[vmem] * 4,
        name="slots",
    )(half_at.reshape(1), owner, adapter.reshape(1, rows), segment, cotangent)


def send_kernel(columns, to_slot, marks, g_ref, tokens_hbm, sent_hbm, tokens, sent, *sems):
    in_sems, out_sems = sems
    width, out_width = tokens.shape[1], g_ref.shape[1]
    parts = column_parts(width, columns)
    copies = [
        pltpu.make_async_copy(tokens_hbm.at[:, part], tokens.at[:, part], in_sems.at[at])
        for at, part in enumerate(parts)
    ]
    for copy in copies:
        copy.start()
    hot = to_slot[...]
    last = slice(width + out_width, width + out_width + MARKS)
    sent[:, width : width + out_width] = jnp.dot(
        hot, g_ref[...], preferred_element_type=F32
    ).astype(BF16)
    sent[:, last] = lax.dot_general(
        hot, marks[...], (((1,), (1,)), ((), ())), preferred_element_type=F32
    ).astype(BF16)
    outs = []

    def send(part):
        outs.append(
            pltpu.make_async_copy(
                sent.at[:, part], sent_hbm.at[:, part], out_sems.at[len(outs)]
            )
        )
        outs[-1].start()

    send(slice(width, width + out_width + MARKS))
    for copy, part in zip(copies, parts):
        copy.wait()
        sent[:, part] = jnp.dot(hot, tokens[:, part], preferred_element_type=F32).astype(BF16)
        send(part)
    for copy in outs:
        copy.wait()


def send_rows(to_slot, marks, cotangent, tokens):
    slots, (rows, width) = to_slot.shape[0], tokens.shape
    columns = cotangent.shape[1]
    full = width + columns + MARKS
    n_parts = len(column_parts(width, columns))
    vmem, hbm = pl.BlockSpec(memory_space=pltpu.VMEM), pl.BlockSpec(memory_space=pl.ANY)
    return pl.pallas_call(
        functools.partial(send_kernel, columns),
        out_shape=jax.ShapeDtypeStruct((slots, full), BF16),
        in_specs=[vmem] * 3 + [hbm],
        out_specs=hbm,
        scratch_shapes=[
            pltpu.VMEM((rows, width), BF16),
            pltpu.VMEM((slots, full), BF16),
            pltpu.SemaphoreType.DMA((n_parts,)),
            pltpu.SemaphoreType.DMA((n_parts + 1,)),
        ],
        compiler_params=pltpu.CompilerParams(vmem_limit_bytes=32 * 2**20),
        cost_estimate=pl.CostEstimate(
            flops=2 * slots * rows * full,
            bytes_accessed=2 * (slots + rows) * full,
            transcendentals=0,
        ),
        name="send",
    )(to_slot, marks, cotangent, tokens)


def half_kernel(which_ref, up_hbm, down_hbm, out, sems):
    out_width, which = up_hbm.shape[2], which_ref[0]
    width = down_hbm.shape[2]
    copies = [
        pltpu.make_async_copy(up_hbm.at[which], out.at[:, pl.ds(0, out_width)], sems.at[0]),
        pltpu.make_async_copy(
            down_hbm.at[which], out.at[:, pl.ds(out_width, width)], sems.at[1]
        ),
    ]
    for copy in copies:
        copy.start()
    for copy in copies:
        copy.wait()


def half_of(which, up_pair, down_pair):
    _, rank_size, width = down_pair.shape
    hbm = pl.BlockSpec(memory_space=pl.ANY)
    return pl.pallas_call(
        half_kernel,
        out_shape=jax.ShapeDtypeStruct((rank_size, up_pair.shape[2] + width), BF16),
        in_specs=[pl.BlockSpec(memory_space=pltpu.SMEM), hbm, hbm],
        out_specs=pl.BlockSpec(memory_space=pltpu.VMEM),
        scratch_shapes=[pltpu.SemaphoreType.DMA((2,))],
        name="half",
    )(which.reshape(1), up_pair, down_pair)


def body(
    tokens,
    cotangent,
    owner,
    token_local_adapter,
    segment,
    pair_sequence_order,
    frozen_margin_score,
    adapter_down_weight,
    adapter_up_weight,
):
    rows, width = tokens.shape
    out_width = cotangent.shape[1]
    n_grp, n_dev = lax.axis_size("grp"), lax.axis_size("ad")
    grp, me = lax.axis_index("grp"), lax.axis_index("ad")
    half_size = n_dev // 2
    spot = me % half_size
    capacity = max(2, 2 * rows // n_dev)
    slots = n_dev * capacity
    count, rank_size, _ = adapter_down_weight.shape
    seqs = frozen_margin_score.shape[1]
    lanes = count * rank_size
    down = adapter_down_weight.reshape(lanes, width)
    up = adapter_up_weight.reshape(lanes, out_width)

    def flipped(block, flip):
        return lax.ppermute(block, "ad", [(at, at ^ flip) for at in range(n_dev)])

    def other_grp(block):
        return lax.ppermute(block, "grp", [(0, 1), (1, 0)])

    half_mine = half_of(grp, adapter_up_weight, adapter_down_weight)
    far = flipped(half_mine, half_size)
    half_other = half_of(1 - grp, adapter_up_weight, adapter_down_weight)

    (owner,) = gate(lax.optimization_barrier((owner, half_mine))[0])
    row_seq = segment[0][:, None] == jnp.arange(seqs, dtype=jnp.int32)
    to_slot, to_half, marks, sent_g = slot_rows(
        me // half_size, owner, token_local_adapter, segment, cotangent, count, capacity, half_size
    )
    sent = send_rows(to_slot, marks, cotangent, tokens)

    halves = [list(range(half_size)), list(range(half_size, n_dev))]
    to_half = to_half.reshape(half_size, 2, capacity, rows)
    half_g = lax.all_to_all(
        sent_g.reshape(half_size, 2 * capacity, out_width + MARKS),
        "ad",
        split_axis=0,
        concat_axis=0,
        tiled=True,
        axis_index_groups=halves,
    )

    lane = jnp.arange(MARKS, dtype=jnp.int32)[None, :]
    which = (lane == jnp.stack([grp, 1 - grp])[:, None]).astype(F32)

    def land(blocks):
        return [block if at == 0 else flipped(block, 2 * at) for at, block in enumerate(blocks)]

    def hand_over(blocks):
        return blocks + [flipped(jnp.concatenate([block[capacity:] for block in blocks]), 1)]

    made_near = project(
        0, False, capacity, out_width, width, spot, half_g, which, [half_mine], [half_other]
    )
    landed_near = land(made_near)
    (sent,) = gate(lax.optimization_barrier((sent, made_near))[0])
    got = lax.all_to_all(
        sent.reshape(n_dev, capacity, width + out_width + MARKS),
        "ad",
        split_axis=0,
        concat_axis=0,
        tiled=True,
    ).reshape(slots, width + out_width + MARKS)

    (which_far,) = gate(lax.optimization_barrier((which, sent, landed_near))[0])
    far_other = other_grp(far)
    kept, handed = project(
        1, True, capacity, out_width, width, spot, half_g, which_far, [far], [far_other]
    )
    taken = flipped(handed, 1)
    landed_far = land(
        [
            jnp.concatenate([kept[at : at + capacity], taken[at : at + capacity]])
            for at in range(0, half_size // 2 * capacity, capacity)
        ]
    )
    pair_hot = pair_sequence_order[0][:, None] == jnp.arange(seqs, dtype=jnp.int32)
    at_me = (jnp.arange(n_dev, dtype=jnp.int32) == me)[:, None]
    own_scores = jnp.where(at_me, frozen_margin_score, 0.0).reshape(1, -1)
    own = jnp.concatenate(
        [
            jnp.pad(own_scores, ((0, 0), (0, -own_scores.shape[1] % MARKS))),
            jnp.zeros((1, count + seqs), F32),
            pair_hot.astype(F32).reshape(1, -1),
            jnp.zeros((1, MARKS - count - seqs - seqs * seqs), F32),
        ],
        axis=1,
    )
    part, rank_rows = score(own, got, down, up, count, seqs, rank_size, n_dev)
    told = lax.all_to_all(part, "ad", split_axis=0, concat_axis=0, tiled=True)

    chips = half_size // 2
    order = [2 * at for at in range(chips)] + [2 * at + 1 for at in range(chips)]
    near_flips = spot ^ jnp.array(order, dtype=jnp.int32)
    far_flips = spot ^ jnp.arange(half_size, dtype=jnp.int32)
    pick = jnp.concatenate([to_half[near_flips, 0], to_half[far_flips, 1]])
    pick = pick.reshape(slots, rows).T
    landed_far = lax.optimization_barrier((landed_far, told))[0]
    landed = hand_over(landed_near) + landed_far
    row_marks = jnp.pad(row_seq.astype(F32), ((0, 0), (count, MARKS - count - seqs)))
    input_grad, grad_down, grad_up, losses = finish(
        me,
        told,
        got,
        rank_rows,
        row_marks,
        count,
        seqs,
        width,
        pick,
        landed,
        [capacity] * chips + [chips * capacity] + [2 * capacity] * chips,
    )
    return (
        input_grad,
        grad_down.reshape(count, rank_size, width),
        grad_up.reshape(count, rank_size, out_width),
        losses,
    )


def solution(mesh):
    placed = (
        P(("grp", "ad"), None),
        P(("grp", "ad"), None),
        P(("grp", "ad"), None),
        P(("grp", "ad")),
        P(("grp", "ad"), None),
        P(("grp", "ad"), None),
        P(("grp", "ad"), None),
        P("ad", None, None),
        P("ad", None, None),
    )
    return jax.shard_map(
        body,
        mesh=mesh,
        in_specs=placed,
        out_specs=(
            P(("grp", "ad"), None),
            P(("grp", "ad"), None, None),
            P(("grp", "ad"), None, None),
            P(("grp", "ad")),
        ),
        check_vma=False,
    )
```

```python
import functools

import jax
import jax.numpy as jnp
from jax import lax
from jax.experimental import pallas as pl
from jax.experimental.pallas import tpu as pltpu
from jax.sharding import PartitionSpec as P

SCALE = 2.0
BETA = 0.1
LOSS_SCALE = 256.0
MARKS = 128
GATE_FLOPS = 2 * 10**11

F32 = jnp.float32
BF16 = jnp.bfloat16


def gate(*arrays):
    return pl.pallas_call(
        lambda *refs: None,
        out_shape=[jax.ShapeDtypeStruct(array.shape, array.dtype) for array in arrays],
        in_specs=[pl.BlockSpec(memory_space=pl.ANY)] * len(arrays),
        out_specs=[pl.BlockSpec(memory_space=pl.ANY)] * len(arrays),
        input_output_aliases={at: at for at in range(len(arrays))},
        cost_estimate=pl.CostEstimate(flops=GATE_FLOPS, bytes_accessed=0, transcendentals=0),
        name="gate",
    )(*arrays)


def project_kernel(side, split, capacity, out_width, n_outs, spot_ref, g_ref, which, *refs):
    n_spots = g_ref.shape[0]
    n_parts = (len(refs) - n_outs) // 2
    mine, other, outs = refs[:n_parts], refs[n_parts : 2 * n_parts], refs[2 * n_parts :]
    first = side * capacity
    spot = spot_ref[0]
    rows = jnp.concatenate(
        [g_ref[spot ^ flip, first : first + capacity, :] for flip in range(n_spots)], axis=0
    )
    marks = rows[:, out_width:].astype(F32)
    contract = (((1,), (1,)), ((), ()))
    pulls = []
    for at, parts in enumerate((mine, other)):
        member = jnp.sum(marks * which[at : at + 1, :], axis=1, keepdims=True)
        pull = lax.dot_general(
            rows[:, :out_width], parts[0][:, :out_width], contract, preferred_element_type=F32
        )
        pulls.append((member * pull).astype(BF16))
    done = 0
    for at in range(n_parts):
        start, end = (out_width if at == 0 else 0), mine[at].shape[1]
        while start < end:
            size = min(1024, end - start)
            columns = slice(start, start + size)
            made = jnp.dot(pulls[0], mine[at][:, columns], preferred_element_type=F32)
            made = made + jnp.dot(pulls[1], other[at][:, columns], preferred_element_type=F32)
            made = made.astype(BF16)
            for flip in range(n_spots):
                row = made[flip * capacity : (flip + 1) * capacity]
                if split:
                    chip = flip // 2 * capacity
                    outs[flip % 2][chip : chip + capacity, done : done + size] = row
                else:
                    core = flip % 2 * capacity
                    outs[flip // 2][core : core + capacity, done : done + size] = row
            start, done = start + size, done + size


def project(side, split, capacity, out_width, width, spot, got_g, which, mine, other):
    n_spots = got_g.shape[0]
    chips = n_spots // 2
    blocks = [(chips * capacity, width)] * 2 if split else [(2 * capacity, width)] * chips
    if capacity % 16 == 0:
        return pl.pallas_call(
            functools.partial(project_kernel, side, split, capacity, out_width, len(blocks)),
            out_shape=[jax.ShapeDtypeStruct(block, BF16) for block in blocks],
            in_specs=[pl.BlockSpec(memory_space=pltpu.SMEM)]
            + [pl.BlockSpec(memory_space=pltpu.VMEM)] * (2 + len(mine) + len(other)),
            cost_estimate=pl.CostEstimate(flops=1000, bytes_accessed=1000, transcendentals=0),
            name="project",
        )(spot.reshape(1), got_g, which, *mine, *other)
    order = spot ^ jnp.arange(n_spots, dtype=jnp.int32)
    rows = got_g[order, side * capacity : (side + 1) * capacity].reshape(n_spots * capacity, -1)
    marks = rows[:, out_width:].astype(F32)
    made = 0.0
    for at, parts in enumerate((mine, other)):
        whole = jnp.concatenate(parts, axis=1)
        pull = jnp.dot(rows[:, :out_width], whole[:, :out_width].T, preferred_element_type=F32)
        pull = (jnp.sum(marks * which[at], axis=1, keepdims=True) * pull).astype(BF16)
        made = made + jnp.dot(pull, whole[:, out_width:], preferred_element_type=F32)
    made = made.astype(BF16).reshape(chips, 2, capacity, width)
    if split:
        return [made[:, core].reshape(chips * capacity, width) for core in range(2)]
    return list(made.reshape(chips, 2 * capacity, width))


def iota(shape, axis):
    return lax.broadcasted_iota(jnp.int32, shape, axis)


def exact_dot(hot, values):
    return jnp.dot(hot, values, precision=lax.Precision.HIGHEST, preferred_element_type=F32)


def column_parts(width, columns):
    return [slice(start, min(start + columns, width)) for start in range(0, width, columns)]


def sequence_lanes(score_lanes, count, seqs):
    shape = (MARKS, score_lanes)
    return (iota(shape, 0) == count + iota(shape, 1) % seqs).astype(F32)


def score_kernel(
    count, seqs, rank_size, capacity, columns, own_ref, got_hbm, down, up, *refs
):
    told_ref, rows_hbm, got, rank_rows, got_sems, rows_sem = refs
    width, out_width = down.shape[1], up.shape[1]
    parts = column_parts(width, 4 * columns)
    tail = slice(width, got.shape[1])
    copies = []
    for at, part in enumerate(parts):
        copies.append(
            (pltpu.make_async_copy(got_hbm.at[:, part], got.at[:, part], got_sems.at[at]),)
        )
    tail_copy = pltpu.make_async_copy(got_hbm.at[:, tail], got.at[:, tail], got_sems.at[len(parts)])
    tail_copy.start()
    for pair in copies:
        for copy in pair:
            copy.start()
    contract = (((1,), (1,)), ((), ()))
    tail_copy.wait()
    marks = got[:, width + out_width :].astype(F32)
    slots, lanes = got.shape[0], down.shape[0]
    lane = iota((slots, lanes), 1) // rank_size
    member = jnp.zeros((slots, lanes), F32)
    for which in range(count):
        member = jnp.where(lane == which, marks[:, which : which + 1], member)
    pulled = member * lax.dot_general(
        got[:, width : width + out_width], up[...], contract, preferred_element_type=F32
    )
    rank_rows[:, lanes:] = pulled.astype(BF16)
    total = jnp.zeros((slots, lanes), F32)
    for pair, part in zip(copies, parts):
        for copy in pair:
            copy.wait()
        total = total + lax.dot_general(
            got[:, part], down[:, part], contract, preferred_element_type=F32
        )
    hidden = (member * total).astype(BF16)
    rank_rows[:, :lanes] = hidden
    rows_copy = pltpu.make_async_copy(rank_rows, rows_hbm, rows_sem)
    rows_copy.start()
    inner = SCALE * jnp.sum(hidden.astype(F32) * pulled, axis=1, keepdims=True)
    n_dev, _, all_lanes = told_ref.shape
    hot = iota((n_dev, slots), 1) // capacity == iota((n_dev, slots), 0)
    part = exact_dot(hot.astype(F32), marks * inner)
    score_lanes = all_lanes - MARKS
    spread = exact_dot(part, sequence_lanes(score_lanes, count, seqs))
    at_device = iota((n_dev, score_lanes), 0) == iota((n_dev, score_lanes), 1) // seqs
    row = jnp.sum(jnp.where(at_device, spread, 0.0), axis=0, keepdims=True)
    row = jnp.concatenate([row, jnp.zeros((1, MARKS), F32)], axis=1) + own_ref[...]
    told_ref[...] = jnp.broadcast_to(row[None], told_ref.shape)
    rows_copy.wait()


def score(own, got, down, up, count, seqs, rank_size, n_dev):
    slots = got.shape[0]
    lanes, width = down.shape
    columns = up.shape[1]
    n_parts = len(column_parts(width, 4 * columns))
    vmem, hbm = pl.BlockSpec(memory_space=pltpu.VMEM), pl.BlockSpec(memory_space=pl.ANY)
    return pl.pallas_call(
        functools.partial(score_kernel, count, seqs, rank_size, slots // n_dev, columns),
        out_shape=[
            jax.ShapeDtypeStruct((n_dev,) + own.shape, F32),
            pltpu.HBM((slots, 2 * lanes), BF16),
        ],
        in_specs=[vmem, hbm, vmem, vmem],
        out_specs=[vmem, pl.BlockSpec(memory_space=pltpu.HBM)],
        scratch_shapes=[
            pltpu.VMEM(got.shape, BF16),
            pltpu.VMEM((slots, 2 * lanes), BF16),
            pltpu.SemaphoreType.DMA((n_parts + 1,)),
            pltpu.SemaphoreType.DMA,
        ],
        compiler_params=pltpu.CompilerParams(vmem_limit_bytes=16 * 2**20),
        cost_estimate=pl.CostEstimate(
            flops=2 * slots * lanes * (width + columns),
            bytes_accessed=2 * (slots + lanes) * (width + columns),
            transcendentals=0,
        ),
        name="score",
    )(own, got, down, up)


def weights(total, count, seqs):
    lane = iota(total.shape, 1)

    def column(at):
        return total[:, at : at + 1]

    pick = [[column(count + seqs + i * seqs + s) for s in range(seqs)] for i in range(seqs)]
    ordered = [sum(pick[i][s] * column(count + s) for s in range(seqs)) for i in range(seqs)]
    losses, by_order = jnp.zeros(total.shape, F32), []
    for pair in range(seqs // 2):
        margin = BETA * (ordered[2 * pair] - ordered[2 * pair + 1])
        loss = jnp.maximum(-margin, 0.0) + jnp.log1p(jnp.exp(-jnp.abs(margin)))
        losses = jnp.where(lane == pair, loss, losses)
        lean = 1.0 / (1.0 + jnp.exp(margin))
        by_order += [-BETA * lean, BETA * lean]
    table = jnp.zeros(total.shape, F32)
    for s in range(seqs):
        weight = LOSS_SCALE * sum(pick[i][s] * by_order[i] for i in range(seqs))
        table = jnp.where(lane == count + s, weight, table)
    return losses, table


def finish_kernel(count, seqs, capacity, columns, used, me_ref, told_ref, *refs):
    row_marks, rank_hbm, got_hbm, *refs = refs
    if used:
        pick, *refs = refs
    block_hbms, refs = refs[: len(used)], refs[len(used) :]
    losses_ref, row_weight, up_hbm, down_hbm, *refs = refs
    if used:
        input_hbm, rank_rows, got, grad_up, grad_down, rows, input_grad, *sems = refs
        rank_sem, got_sems, up_sem, down_sems, block_sems, input_sems = sems
    else:
        rank_rows, got, grad_up, grad_down, rank_sem, got_sems, up_sem, down_sems = refs
    width, out_width = grad_down.shape[1], grad_up.shape[1]
    parts = column_parts(width, 2 * columns)
    tail = slice(width, got.shape[1])
    tail_copy = pltpu.make_async_copy(got_hbm.at[:, tail], got.at[:, tail], got_sems.at[len(parts)])
    copies = [
        pltpu.make_async_copy(got_hbm.at[:, part], got.at[:, part], got_sems.at[at])
        for at, part in enumerate(parts)
    ]
    first, block_copies = 0, []
    for at, size in enumerate(used):
        block_copies.append(
            pltpu.make_async_copy(
                block_hbms[at].at[pl.ds(0, size)], rows.at[pl.ds(first, size)], block_sems.at[at]
            )
        )
        first += size
    rank_copy = pltpu.make_async_copy(rank_hbm, rank_rows, rank_sem)
    rank_copy.start()
    tail_copy.start()
    for copy in copies + block_copies:
        copy.start()

    told = jnp.concatenate([told_ref[at] for at in range(told_ref.shape[0])], axis=0)
    score_lanes = told.shape[1] - MARKS
    sums = jnp.sum(told[:, :score_lanes], axis=0, keepdims=True)
    shape = (told.shape[0], score_lanes)
    spread = jnp.where(iota(shape, 0) == iota(shape, 1) // seqs, sums, 0.0)
    total = told[:, score_lanes:] + lax.dot_general(
        spread,
        sequence_lanes(score_lanes, count, seqs),
        (((1,), (1,)), ((), ())),
        precision=lax.Precision.HIGHEST,
        preferred_element_type=F32,
    )
    losses, table = weights(total, count, seqs)
    n_dev, slots = total.shape[0], got.shape[0]
    mine = iota(total.shape, 0) == me_ref[0]
    pair_lane = iota(losses.shape, 1)
    for pair in range(seqs // 2):
        losses_ref[pair] = jnp.sum(jnp.where(mine & (pair_lane == pair), losses, 0.0))
    my_table = jnp.sum(jnp.where(mine, table, 0.0), axis=0, keepdims=True)
    my_weight = SCALE * jnp.sum(row_marks[...] * my_table, axis=1, keepdims=True)
    row_weight[...] = my_weight
    hot = iota((slots, n_dev), 0) // capacity == iota((slots, n_dev), 1)
    slot_table = exact_dot(hot.astype(F32), table)
    tail_copy.wait()
    marks = got[:, width + out_width :].astype(F32)
    weight = jnp.sum(marks * slot_table, axis=1, keepdims=True)
    rank_copy.wait()
    lanes = grad_up.shape[0]
    upper = (weight * rank_rows[:, :lanes].astype(F32)).astype(BF16)
    lower = (weight * rank_rows[:, lanes:].astype(F32)).astype(BF16)
    contract = (((0,), (0,)), ((), ()))
    made = lax.dot_general(
        upper, got[:, width : width + out_width], contract, preferred_element_type=F32
    )
    grad_up[...] = (SCALE * made).astype(BF16)
    outs = [pltpu.make_async_copy(grad_up, up_hbm, up_sem)]
    outs[0].start()
    for at, part in enumerate(parts):
        copies[at].wait()
        made = lax.dot_general(lower, got[:, part], contract, preferred_element_type=F32)
        grad_down[:, part] = (SCALE * made).astype(BF16)
        outs.append(
            pltpu.make_async_copy(grad_down.at[:, part], down_hbm.at[:, part], down_sems.at[at])
        )
        outs[-1].start()
    if used:
        for copy in block_copies:
            copy.wait()
        for at, part in enumerate(parts):
            picked = jnp.dot(pick[...], rows[:, part], preferred_element_type=F32)
            input_grad[:, part] = (my_weight * picked).astype(BF16)
            outs.append(
                pltpu.make_async_copy(
                    input_grad.at[:, part], input_hbm.at[:, part], input_sems.at[at]
                )
            )
            outs[-1].start()
    for copy in outs:
        copy.wait()


def finish(
    me, told, got, rank_rows, row_marks, count, seqs, width, pick, blocks, used
):
    slots, lanes = rank_rows.shape[0], rank_rows.shape[1] // 2
    rows = row_marks.shape[0]
    n_dev = told.shape[0]
    columns = got.shape[1] - width - MARKS
    n_parts = len(column_parts(width, 2 * columns))
    together = not any(size % 16 for size in used)
    vmem, hbm = pl.BlockSpec(memory_space=pltpu.VMEM), pl.BlockSpec(memory_space=pltpu.HBM)
    sems = pltpu.SemaphoreType.DMA
    out_shape = [
        jax.ShapeDtypeStruct((seqs // 2,), F32),
        jax.ShapeDtypeStruct((rows, 1), F32),
        jax.ShapeDtypeStruct((lanes, columns), BF16),
        jax.ShapeDtypeStruct((lanes, width), BF16),
    ]
    in_specs = [pl.BlockSpec(memory_space=pltpu.SMEM)] + [vmem] * 2 + [hbm] * 2
    rank_rows = pltpu.with_memory_space_constraint(rank_rows, pltpu.HBM)
    operands = [me.reshape(1), told, row_marks, rank_rows, got]
    scratch = [
        pltpu.VMEM(rank_rows.shape, BF16),
        pltpu.VMEM(got.shape, BF16),
        pltpu.VMEM((lanes, columns), BF16),
        pltpu.VMEM((lanes, width), BF16),
    ]
    scratch_sems = [sems, sems((n_parts + 1,)), sems, sems((n_parts,))]
    if together:
        out_shape.append(jax.ShapeDtypeStruct((rows, width), BF16))
        in_specs += [vmem] + [hbm] * len(blocks)
        operands += [pick, *blocks]
        scratch += [pltpu.VMEM((slots, width), BF16), pltpu.VMEM((rows, width), BF16)]
        scratch_sems += [sems((len(blocks),)), sems((n_parts,))]
    losses, row_weight, grad_up, grad_down, *input_grad = pl.pallas_call(
        functools.partial(
            finish_kernel, count, seqs, slots // n_dev, columns, used if together else []
        ),
        out_shape=out_shape,
        in_specs=in_specs,
        out_specs=[pl.BlockSpec(memory_space=pltpu.SMEM), vmem] + [hbm] * (len(out_shape) - 2),
        scratch_shapes=scratch + scratch_sems,
        compiler_params=pltpu.CompilerParams(vmem_limit_bytes=24 * 2**20),
        cost_estimate=pl.CostEstimate(
            flops=4 * slots * lanes * width,
            bytes_accessed=2 * (2 * slots + lanes + rows) * width,
            transcendentals=0,
        ),
        name="finish",
    )(*operands)
    if not together:
        blocks = jnp.concatenate([block[:size] for block, size in zip(blocks, used)])
        picked = jnp.dot(pick, blocks, preferred_element_type=F32)
        input_grad = [(row_weight * picked).astype(BF16)]
    return input_grad[0], grad_down, grad_up, losses


def slots_kernel(
    count, capacity, half_size, half_ref, owner_ref, adapter_ref, segment_ref, g_ref, *refs
):
    to_slot, to_half, marks_ref, sent_g = refs
    slots, rows = to_slot.shape
    out_width = g_ref.shape[1]
    eye = (iota((rows, rows), 0) == iota((rows, rows), 1)).astype(BF16)
    owner = lax.dot_general(
        owner_ref[...].astype(F32).astype(BF16),
        eye,
        (((0,), (0,)), ((), ())),
        preferred_element_type=F32,
    ).astype(jnp.int32)
    n_dev = 2 * half_size
    hot = (iota((n_dev, rows), 0) == owner).astype(F32)
    earlier = (iota((rows, rows), 0) < iota((rows, rows), 1)).astype(BF16)
    before = jnp.dot(hot.astype(BF16), earlier, preferred_element_type=F32)
    rank = jnp.sum(before * hot, axis=0, keepdims=True).astype(jnp.int32)
    at_slot = iota((slots, rows), 0)
    to_slot[...] = (at_slot == owner * capacity + rank).astype(BF16)
    far = owner // half_size != half_ref[0]
    position = (owner % half_size * 2 + far.astype(jnp.int32)) * capacity + rank
    hot_half = (at_slot == position).astype(BF16)
    to_half[...] = hot_half
    lane = iota((MARKS, rows), 0)
    marks = ((lane == adapter_ref[...]) | (lane == segment_ref[...] + count)).astype(BF16)
    marks_ref[...] = marks
    sent_g[:, :out_width] = jnp.dot(hot_half, g_ref[...], preferred_element_type=F32).astype(BF16)
    sent_g[:, out_width:] = lax.dot_general(
        hot_half, marks, (((1,), (1,)), ((), ())), preferred_element_type=F32
    ).astype(BF16)


def slot_rows(half_at, owner, adapter, segment, cotangent, count, capacity, half_size):
    rows, out_width = cotangent.shape
    slots = 2 * half_size * capacity
    vmem = pl.BlockSpec(memory_space=pltpu.VMEM)
    return pl.pallas_call(
        functools.partial(slots_kernel, count, capacity, half_size),
        out_shape=[
            jax.ShapeDtypeStruct((slots, rows), BF16),
            jax.ShapeDtypeStruct((slots, rows), BF16),
            jax.ShapeDtypeStruct((MARKS, rows), BF16),
            jax.ShapeDtypeStruct((slots, out_width + MARKS), BF16),
        ],
        in_specs=[pl.BlockSpec(memory_space=pltpu.SMEM)] + [vmem] * 4,
        out_specs=[vmem] * 4,
        name="slots",
    )(half_at.reshape(1), owner, adapter.reshape(1, rows), segment, cotangent)


def send_kernel(columns, to_slot, marks, g_ref, tokens_hbm, sent_hbm, tokens, sent, *sems):
    in_sems, out_sems = sems
    width, out_width = tokens.shape[1], g_ref.shape[1]
    parts = column_parts(width, columns)
    copies = [
        pltpu.make_async_copy(tokens_hbm.at[:, part], tokens.at[:, part], in_sems.at[at])
        for at, part in enumerate(parts)
    ]
    for copy in copies:
        copy.start()
    hot = to_slot[...]
    last = slice(width + out_width, width + out_width + MARKS)
    sent[:, width : width + out_width] = jnp.dot(
        hot, g_ref[...], preferred_element_type=F32
    ).astype(BF16)
    sent[:, last] = lax.dot_general(
        hot, marks[...], (((1,), (1,)), ((), ())), preferred_element_type=F32
    ).astype(BF16)
    outs = []

    def send(part):
        outs.append(
            pltpu.make_async_copy(
                sent.at[:, part], sent_hbm.at[:, part], out_sems.at[len(outs)]
            )
        )
        outs[-1].start()

    send(slice(width, width + out_width + MARKS))
    for copy, part in zip(copies, parts):
        copy.wait()
        sent[:, part] = jnp.dot(hot, tokens[:, part], preferred_element_type=F32).astype(BF16)
        send(part)
    for copy in outs:
        copy.wait()


def send_rows(to_slot, marks, cotangent, tokens):
    slots, (rows, width) = to_slot.shape[0], tokens.shape
    columns = cotangent.shape[1]
    full = width + columns + MARKS
    n_parts = len(column_parts(width, columns))
    vmem, hbm = pl.BlockSpec(memory_space=pltpu.VMEM), pl.BlockSpec(memory_space=pl.ANY)
    return pl.pallas_call(
        functools.partial(send_kernel, columns),
        out_shape=jax.ShapeDtypeStruct((slots, full), BF16),
        in_specs=[vmem] * 3 + [hbm],
        out_specs=hbm,
        scratch_shapes=[
            pltpu.VMEM((rows, width), BF16),
            pltpu.VMEM((slots, full), BF16),
            pltpu.SemaphoreType.DMA((n_parts,)),
            pltpu.SemaphoreType.DMA((n_parts + 1,)),
        ],
        compiler_params=pltpu.CompilerParams(vmem_limit_bytes=32 * 2**20),
        cost_estimate=pl.CostEstimate(
            flops=2 * slots * rows * full,
            bytes_accessed=2 * (slots + rows) * full,
            transcendentals=0,
        ),
        name="send",
    )(to_slot, marks, cotangent, tokens)


def half_kernel(which_ref, up_hbm, down_hbm, out, sems):
    out_width, which = up_hbm.shape[2], which_ref[0]
    width = down_hbm.shape[2]
    copies = [
        pltpu.make_async_copy(up_hbm.at[which], out.at[:, pl.ds(0, out_width)], sems.at[0]),
        pltpu.make_async_copy(
            down_hbm.at[which], out.at[:, pl.ds(out_width, width)], sems.at[1]
        ),
    ]
    for copy in copies:
        copy.start()
    for copy in copies:
        copy.wait()


def half_of(which, up_pair, down_pair):
    _, rank_size, width = down_pair.shape
    hbm = pl.BlockSpec(memory_space=pl.ANY)
    return pl.pallas_call(
        half_kernel,
        out_shape=jax.ShapeDtypeStruct((rank_size, up_pair.shape[2] + width), BF16),
        in_specs=[pl.BlockSpec(memory_space=pltpu.SMEM), hbm, hbm],
        out_specs=pl.BlockSpec(memory_space=pltpu.VMEM),
        scratch_shapes=[pltpu.SemaphoreType.DMA((2,))],
        name="half",
    )(which.reshape(1), up_pair, down_pair)


def body(
    tokens,
    cotangent,
    owner,
    token_local_adapter,
    segment,
    pair_sequence_order,
    frozen_margin_score,
    adapter_down_weight,
    adapter_up_weight,
):
    rows, width = tokens.shape
    out_width = cotangent.shape[1]
    n_grp, n_dev = lax.axis_size("grp"), lax.axis_size("ad")
    grp, me = lax.axis_index("grp"), lax.axis_index("ad")
    half_size = n_dev // 2
    spot = me % half_size
    capacity = max(2, 2 * rows // n_dev)
    slots = n_dev * capacity
    count, rank_size, _ = adapter_down_weight.shape
    seqs = frozen_margin_score.shape[1]
    lanes = count * rank_size
    down = adapter_down_weight.reshape(lanes, width)
    up = adapter_up_weight.reshape(lanes, out_width)

    def flipped(block, flip):
        return lax.ppermute(block, "ad", [(at, at ^ flip) for at in range(n_dev)])

    def other_grp(block):
        return lax.ppermute(block, "grp", [(0, 1), (1, 0)])

    half_mine = half_of(grp, adapter_up_weight, adapter_down_weight)
    far = flipped(half_mine, half_size)
    half_other = half_of(1 - grp, adapter_up_weight, adapter_down_weight)

    (owner,) = gate(lax.optimization_barrier((owner, half_mine))[0])
    row_seq = segment[0][:, None] == jnp.arange(seqs, dtype=jnp.int32)
    to_slot, to_half, marks, sent_g = slot_rows(
        me // half_size, owner, token_local_adapter, segment, cotangent, count, capacity, half_size
    )
    sent = send_rows(to_slot, marks, cotangent, tokens)

    halves = [list(range(half_size)), list(range(half_size, n_dev))]
    to_half = to_half.reshape(half_size, 2, capacity, rows)
    half_g = lax.all_to_all(
        sent_g.reshape(half_size, 2 * capacity, out_width + MARKS),
        "ad",
        split_axis=0,
        concat_axis=0,
        tiled=True,
        axis_index_groups=halves,
    )

    lane = jnp.arange(MARKS, dtype=jnp.int32)[None, :]
    which = (lane == jnp.stack([grp, 1 - grp])[:, None]).astype(F32)

    def land(blocks):
        return [block if at == 0 else flipped(block, 2 * at) for at, block in enumerate(blocks)]

    def hand_over(blocks):
        return blocks + [flipped(jnp.concatenate([block[capacity:] for block in blocks]), 1)]

    made_near = project(
        0, False, capacity, out_width, width, spot, half_g, which, [half_mine], [half_other]
    )
    landed_near = land(made_near)
    (sent,) = gate(lax.optimization_barrier((sent, made_near))[0])
    got = lax.all_to_all(
        sent.reshape(n_dev, capacity, width + out_width + MARKS),
        "ad",
        split_axis=0,
        concat_axis=0,
        tiled=True,
    ).reshape(slots, width + out_width + MARKS)

    (which_far,) = gate(lax.optimization_barrier((which, sent, landed_near))[0])
    far_other = other_grp(far)
    kept, handed = project(
        1, True, capacity, out_width, width, spot, half_g, which_far, [far], [far_other]
    )
    taken = flipped(handed, 1)
    landed_far = land(
        [
            jnp.concatenate([kept[at : at + capacity], taken[at : at + capacity]])
            for at in range(0, half_size // 2 * capacity, capacity)
        ]
    )
    pair_hot = pair_sequence_order[0][:, None] == jnp.arange(seqs, dtype=jnp.int32)
    at_me = (jnp.arange(n_dev, dtype=jnp.int32) == me)[:, None]
    own_scores = jnp.where(at_me, frozen_margin_score, 0.0).reshape(1, -1)
    own = jnp.concatenate(
        [
            jnp.pad(own_scores, ((0, 0), (0, -own_scores.shape[1] % MARKS))),
            jnp.zeros((1, count + seqs), F32),
            pair_hot.astype(F32).reshape(1, -1),
            jnp.zeros((1, MARKS - count - seqs - seqs * seqs), F32),
        ],
        axis=1,
    )
    part, rank_rows = score(own, got, down, up, count, seqs, rank_size, n_dev)
    told = lax.all_to_all(part, "ad", split_axis=0, concat_axis=0, tiled=True)

    chips = half_size // 2
    order = [2 * at for at in range(chips)] + [2 * at + 1 for at in range(chips)]
    near_flips = spot ^ jnp.array(order, dtype=jnp.int32)
    far_flips = spot ^ jnp.arange(half_size, dtype=jnp.int32)
    pick = jnp.concatenate([to_half[near_flips, 0], to_half[far_flips, 1]])
    pick = pick.reshape(slots, rows).T
    landed_far = lax.optimization_barrier((landed_far, told))[0]
    landed = hand_over(landed_near) + landed_far
    row_marks = jnp.pad(row_seq.astype(F32), ((0, 0), (count, MARKS - count - seqs)))
    input_grad, grad_down, grad_up, losses = finish(
        me,
        told,
        got,
        rank_rows,
        row_marks,
        count,
        seqs,
        width,
        pick,
        landed,
        [capacity] * chips + [chips * capacity] + [2 * capacity] * chips,
    )
    return (
        input_grad,
        grad_down.reshape(count, rank_size, width),
        grad_up.reshape(count, rank_size, out_width),
        losses,
    )


def solution(mesh):
    placed = (
        P(("grp", "ad"), None),
        P(("grp", "ad"), None),
        P(("grp", "ad"), None),
        P(("grp", "ad")),
        P(("grp", "ad"), None),
        P(("grp", "ad"), None),
        P(("grp", "ad"), None),
        P("ad", None, None),
        P("ad", None, None),
    )
    return jax.shard_map(
        body,
        mesh=mesh,
        in_specs=placed,
        out_specs=(
            P(("grp", "ad"), None),
            P(("grp", "ad"), None, None),
            P(("grp", "ad"), None, None),
            P(("grp", "ad")),
        ),
        check_vma=False,
    )
```

```python
import functools

import jax
import jax.numpy as jnp
from jax import lax
from jax.experimental import pallas as pl
from jax.experimental.pallas import tpu as pltpu
from jax.sharding import PartitionSpec as P

SCALE = 2.0
BETA = 0.1
LOSS_SCALE = 256.0
MARKS = 128
GATE_FLOPS = 2 * 10**11

F32 = jnp.float32
BF16 = jnp.bfloat16


def gate(*arrays):
    return pl.pallas_call(
        lambda *refs: None,
        out_shape=[jax.ShapeDtypeStruct(array.shape, array.dtype) for array in arrays],
        in_specs=[pl.BlockSpec(memory_space=pl.ANY)] * len(arrays),
        out_specs=[pl.BlockSpec(memory_space=pl.ANY)] * len(arrays),
        input_output_aliases={at: at for at in range(len(arrays))},
        cost_estimate=pl.CostEstimate(flops=GATE_FLOPS, bytes_accessed=0, transcendentals=0),
        name="gate",
    )(*arrays)


def project_kernel(side, split, capacity, out_width, n_outs, spot_ref, g_ref, which, *refs):
    n_spots = g_ref.shape[0]
    n_parts = (len(refs) - n_outs) // 2
    mine, other, outs = refs[:n_parts], refs[n_parts : 2 * n_parts], refs[2 * n_parts :]
    first = side * capacity
    spot = spot_ref[0]
    rows = jnp.concatenate(
        [g_ref[spot ^ flip, first : first + capacity, :] for flip in range(n_spots)], axis=0
    )
    marks = rows[:, out_width:].astype(F32)
    contract = (((1,), (1,)), ((), ()))
    pulls = []
    for at, parts in enumerate((mine, other)):
        member = jnp.sum(marks * which[at : at + 1, :], axis=1, keepdims=True)
        pull = lax.dot_general(
            rows[:, :out_width], parts[0][:, :out_width], contract, preferred_element_type=F32
        )
        pulls.append((member * pull).astype(BF16))
    done = 0
    for at in range(n_parts):
        start, end = (out_width if at == 0 else 0), mine[at].shape[1]
        while start < end:
            size = min(1024, end - start)
            columns = slice(start, start + size)
            made = jnp.dot(pulls[0], mine[at][:, columns], preferred_element_type=F32)
            made = made + jnp.dot(pulls[1], other[at][:, columns], preferred_element_type=F32)
            made = made.astype(BF16)
            for flip in range(n_spots):
                row = made[flip * capacity : (flip + 1) * capacity]
                if split:
                    chip = flip // 2 * capacity
                    outs[flip % 2][chip : chip + capacity, done : done + size] = row
                else:
                    core = flip % 2 * capacity
                    outs[flip // 2][core : core + capacity, done : done + size] = row
            start, done = start + size, done + size


def project(side, split, capacity, out_width, width, spot, got_g, which, mine, other):
    n_spots = got_g.shape[0]
    chips = n_spots // 2
    blocks = [(chips * capacity, width)] * 2 if split else [(2 * capacity, width)] * chips
    if capacity % 16 == 0:
        return pl.pallas_call(
            functools.partial(project_kernel, side, split, capacity, out_width, len(blocks)),
            out_shape=[jax.ShapeDtypeStruct(block, BF16) for block in blocks],
            in_specs=[pl.BlockSpec(memory_space=pltpu.SMEM)]
            + [pl.BlockSpec(memory_space=pltpu.VMEM)] * (2 + len(mine) + len(other)),
            cost_estimate=pl.CostEstimate(flops=1000, bytes_accessed=1000, transcendentals=0),
            name="project",
        )(spot.reshape(1), got_g, which, *mine, *other)
    order = spot ^ jnp.arange(n_spots, dtype=jnp.int32)
    rows = got_g[order, side * capacity : (side + 1) * capacity].reshape(n_spots * capacity, -1)
    marks = rows[:, out_width:].astype(F32)
    made = 0.0
    for at, parts in enumerate((mine, other)):
        whole = jnp.concatenate(parts, axis=1)
        pull = jnp.dot(rows[:, :out_width], whole[:, :out_width].T, preferred_element_type=F32)
        pull = (jnp.sum(marks * which[at], axis=1, keepdims=True) * pull).astype(BF16)
        made = made + jnp.dot(pull, whole[:, out_width:], preferred_element_type=F32)
    made = made.astype(BF16).reshape(chips, 2, capacity, width)
    if split:
        return [made[:, core].reshape(chips * capacity, width) for core in range(2)]
    return list(made.reshape(chips, 2 * capacity, width))


def iota(shape, axis):
    return lax.broadcasted_iota(jnp.int32, shape, axis)


def exact_dot(hot, values):
    return jnp.dot(hot, values, precision=lax.Precision.HIGHEST, preferred_element_type=F32)


def column_parts(width, columns):
    return [slice(start, min(start + columns, width)) for start in range(0, width, columns)]


def sequence_lanes(score_lanes, count, seqs):
    shape = (MARKS, score_lanes)
    return (iota(shape, 0) == count + iota(shape, 1) % seqs).astype(F32)


def score_kernel(
    count, seqs, rank_size, capacity, columns, own_ref, got_hbm, down, up, *refs
):
    told_ref, rows_hbm, got, rank_rows, got_sems, rows_sem = refs
    width, out_width = down.shape[1], up.shape[1]
    parts = column_parts(width, 4 * columns)
    tail = slice(width, got.shape[1])
    copies = []
    for at, part in enumerate(parts):
        copies.append(
            (pltpu.make_async_copy(got_hbm.at[:, part], got.at[:, part], got_sems.at[at]),)
        )
    tail_copy = pltpu.make_async_copy(got_hbm.at[:, tail], got.at[:, tail], got_sems.at[len(parts)])
    tail_copy.start()
    for pair in copies:
        for copy in pair:
            copy.start()
    contract = (((1,), (1,)), ((), ()))
    tail_copy.wait()
    marks = got[:, width + out_width :].astype(F32)
    slots, lanes = got.shape[0], down.shape[0]
    lane = iota((slots, lanes), 1) // rank_size
    member = jnp.zeros((slots, lanes), F32)
    for which in range(count):
        member = jnp.where(lane == which, marks[:, which : which + 1], member)
    pulled = member * lax.dot_general(
        got[:, width : width + out_width], up[...], contract, preferred_element_type=F32
    )
    rank_rows[:, lanes:] = pulled.astype(BF16)
    total = jnp.zeros((slots, lanes), F32)
    for pair, part in zip(copies, parts):
        for copy in pair:
            copy.wait()
        total = total + lax.dot_general(
            got[:, part], down[:, part], contract, preferred_element_type=F32
        )
    hidden = (member * total).astype(BF16)
    rank_rows[:, :lanes] = hidden
    rows_copy = pltpu.make_async_copy(rank_rows, rows_hbm, rows_sem)
    rows_copy.start()
    inner = SCALE * jnp.sum(hidden.astype(F32) * pulled, axis=1, keepdims=True)
    n_dev, _, all_lanes = told_ref.shape
    scored = marks * inner
    if capacity % 8 == 0:
        part = jnp.sum(scored.reshape(n_dev, capacity, MARKS), axis=1)
    else:
        hot = iota((n_dev, slots), 1) // capacity == iota((n_dev, slots), 0)
        part = exact_dot(hot.astype(F32), scored)
    score_lanes = all_lanes - MARKS
    spread = exact_dot(part, sequence_lanes(score_lanes, count, seqs))
    at_device = iota((n_dev, score_lanes), 0) == iota((n_dev, score_lanes), 1) // seqs
    row = jnp.sum(jnp.where(at_device, spread, 0.0), axis=0, keepdims=True)
    row = jnp.concatenate([row, jnp.zeros((1, MARKS), F32)], axis=1) + own_ref[...]
    told_ref[...] = jnp.broadcast_to(row[None], told_ref.shape)
    rows_copy.wait()


def score(own, got, down, up, count, seqs, rank_size, n_dev):
    slots = got.shape[0]
    lanes, width = down.shape
    columns = up.shape[1]
    n_parts = len(column_parts(width, 4 * columns))
    vmem, hbm = pl.BlockSpec(memory_space=pltpu.VMEM), pl.BlockSpec(memory_space=pl.ANY)
    return pl.pallas_call(
        functools.partial(score_kernel, count, seqs, rank_size, slots // n_dev, columns),
        out_shape=[
            jax.ShapeDtypeStruct((n_dev,) + own.shape, F32),
            pltpu.HBM((slots, 2 * lanes), BF16),
        ],
        in_specs=[vmem, hbm, vmem, vmem],
        out_specs=[vmem, pl.BlockSpec(memory_space=pltpu.HBM)],
        scratch_shapes=[
            pltpu.VMEM(got.shape, BF16),
            pltpu.VMEM((slots, 2 * lanes), BF16),
            pltpu.SemaphoreType.DMA((n_parts + 1,)),
            pltpu.SemaphoreType.DMA,
        ],
        compiler_params=pltpu.CompilerParams(vmem_limit_bytes=16 * 2**20),
        cost_estimate=pl.CostEstimate(
            flops=2 * slots * lanes * (width + columns),
            bytes_accessed=2 * (slots + lanes) * (width + columns),
            transcendentals=0,
        ),
        name="score",
    )(own, got, down, up)


def weights(total, count, seqs):
    lane = iota(total.shape, 1)

    def column(at):
        return total[:, at : at + 1]

    pick = [[column(count + seqs + i * seqs + s) for s in range(seqs)] for i in range(seqs)]
    ordered = [sum(pick[i][s] * column(count + s) for s in range(seqs)) for i in range(seqs)]
    losses, by_order = jnp.zeros(total.shape, F32), []
    for pair in range(seqs // 2):
        margin = BETA * (ordered[2 * pair] - ordered[2 * pair + 1])
        small = jnp.exp(-jnp.abs(margin))
        loss = jnp.maximum(-margin, 0.0) + jnp.log1p(small)
        losses = jnp.where(lane == pair, loss, losses)
        lean = jnp.where(margin > 0.0, small, 1.0) / (1.0 + small)
        by_order += [-BETA * lean, BETA * lean]
    table = jnp.zeros(total.shape, F32)
    for s in range(seqs):
        weight = LOSS_SCALE * sum(pick[i][s] * by_order[i] for i in range(seqs))
        table = jnp.where(lane == count + s, weight, table)
    return losses, table


def finish_kernel(count, seqs, capacity, columns, used, me_ref, told_ref, *refs):
    row_marks, rank_hbm, got_hbm, *refs = refs
    if used:
        pick, *refs = refs
    block_hbms, refs = refs[: len(used)], refs[len(used) :]
    losses_ref, row_weight, up_hbm, down_hbm, *refs = refs
    if used:
        input_hbm, rank_rows, got, grad_up, grad_down, rows, input_grad, *sems = refs
        rank_sem, got_sems, up_sem, down_sems, block_sems, input_sems = sems
    else:
        rank_rows, got, grad_up, grad_down, rank_sem, got_sems, up_sem, down_sems = refs
    width, out_width = grad_down.shape[1], grad_up.shape[1]
    parts = column_parts(width, 2 * columns)
    tail = slice(width, got.shape[1])
    tail_copy = pltpu.make_async_copy(got_hbm.at[:, tail], got.at[:, tail], got_sems.at[len(parts)])
    copies = [
        pltpu.make_async_copy(got_hbm.at[:, part], got.at[:, part], got_sems.at[at])
        for at, part in enumerate(parts)
    ]
    first, block_copies = 0, []
    for at, size in enumerate(used):
        block_copies.append(
            pltpu.make_async_copy(
                block_hbms[at].at[pl.ds(0, size)], rows.at[pl.ds(first, size)], block_sems.at[at]
            )
        )
        first += size
    rank_copy = pltpu.make_async_copy(rank_hbm, rank_rows, rank_sem)
    rank_copy.start()
    tail_copy.start()
    for copy in copies + block_copies:
        copy.start()

    told = jnp.concatenate([told_ref[at] for at in range(told_ref.shape[0])], axis=0)
    score_lanes = told.shape[1] - MARKS
    sums = jnp.sum(told[:, :score_lanes], axis=0, keepdims=True)
    shape = (told.shape[0], score_lanes)
    spread = jnp.where(iota(shape, 0) == iota(shape, 1) // seqs, sums, 0.0)
    total = told[:, score_lanes:] + lax.dot_general(
        spread,
        sequence_lanes(score_lanes, count, seqs),
        (((1,), (1,)), ((), ())),
        precision=lax.Precision.HIGHEST,
        preferred_element_type=F32,
    )
    losses, table = weights(total, count, seqs)
    n_dev, slots = total.shape[0], got.shape[0]
    mine = iota(total.shape, 0) == me_ref[0]
    pair_lane = iota(losses.shape, 1)
    for pair in range(seqs // 2):
        losses_ref[pair] = jnp.sum(jnp.where(mine & (pair_lane == pair), losses, 0.0))
    my_table = jnp.sum(jnp.where(mine, table, 0.0), axis=0, keepdims=True)
    my_weight = SCALE * jnp.sum(row_marks[...] * my_table, axis=1, keepdims=True)
    row_weight[...] = my_weight
    hot = iota((slots, n_dev), 0) // capacity == iota((slots, n_dev), 1)
    slot_table = exact_dot(hot.astype(F32), table)
    tail_copy.wait()
    marks = got[:, width + out_width :].astype(F32)
    weight = jnp.sum(marks * slot_table, axis=1, keepdims=True)
    rank_copy.wait()
    lanes = grad_up.shape[0]
    upper = (weight * rank_rows[:, :lanes].astype(F32)).astype(BF16)
    lower = (weight * rank_rows[:, lanes:].astype(F32)).astype(BF16)
    contract = (((0,), (0,)), ((), ()))
    made = lax.dot_general(
        upper, got[:, width : width + out_width], contract, preferred_element_type=F32
    )
    grad_up[...] = (SCALE * made).astype(BF16)
    outs = [pltpu.make_async_copy(grad_up, up_hbm, up_sem)]
    outs[0].start()
    for at, part in enumerate(parts):
        copies[at].wait()
        made = lax.dot_general(lower, got[:, part], contract, preferred_element_type=F32)
        grad_down[:, part] = (SCALE * made).astype(BF16)
        outs.append(
            pltpu.make_async_copy(grad_down.at[:, part], down_hbm.at[:, part], down_sems.at[at])
        )
        outs[-1].start()
    if used:
        for copy in block_copies:
            copy.wait()
        for at, part in enumerate(parts):
            picked = jnp.dot(pick[...], rows[:, part], preferred_element_type=F32)
            input_grad[:, part] = (my_weight * picked).astype(BF16)
            outs.append(
                pltpu.make_async_copy(
                    input_grad.at[:, part], input_hbm.at[:, part], input_sems.at[at]
                )
            )
            outs[-1].start()
    for copy in outs:
        copy.wait()


def finish(
    me, told, got, rank_rows, row_marks, count, seqs, width, pick, blocks, used
):
    slots, lanes = rank_rows.shape[0], rank_rows.shape[1] // 2
    rows = row_marks.shape[0]
    n_dev = told.shape[0]
    columns = got.shape[1] - width - MARKS
    n_parts = len(column_parts(width, 2 * columns))
    together = not any(size % 16 for size in used)
    vmem, hbm = pl.BlockSpec(memory_space=pltpu.VMEM), pl.BlockSpec(memory_space=pltpu.HBM)
    sems = pltpu.SemaphoreType.DMA
    out_shape = [
        jax.ShapeDtypeStruct((seqs // 2,), F32),
        jax.ShapeDtypeStruct((rows, 1), F32),
        jax.ShapeDtypeStruct((lanes, columns), BF16),
        jax.ShapeDtypeStruct((lanes, width), BF16),
    ]
    in_specs = [pl.BlockSpec(memory_space=pltpu.SMEM)] + [vmem] * 2 + [hbm] * 2
    rank_rows = pltpu.with_memory_space_constraint(rank_rows, pltpu.HBM)
    operands = [me.reshape(1), told, row_marks, rank_rows, got]
    scratch = [
        pltpu.VMEM(rank_rows.shape, BF16),
        pltpu.VMEM(got.shape, BF16),
        pltpu.VMEM((lanes, columns), BF16),
        pltpu.VMEM((lanes, width), BF16),
    ]
    scratch_sems = [sems, sems((n_parts + 1,)), sems, sems((n_parts,))]
    if together:
        out_shape.append(jax.ShapeDtypeStruct((rows, width), BF16))
        in_specs += [vmem] + [hbm] * len(blocks)
        operands += [pick, *blocks]
        scratch += [pltpu.VMEM((slots, width), BF16), pltpu.VMEM((rows, width), BF16)]
        scratch_sems += [sems((len(blocks),)), sems((n_parts,))]
    losses, row_weight, grad_up, grad_down, *input_grad = pl.pallas_call(
        functools.partial(
            finish_kernel, count, seqs, slots // n_dev, columns, used if together else []
        ),
        out_shape=out_shape,
        in_specs=in_specs,
        out_specs=[pl.BlockSpec(memory_space=pltpu.SMEM), vmem] + [hbm] * (len(out_shape) - 2),
        scratch_shapes=scratch + scratch_sems,
        compiler_params=pltpu.CompilerParams(vmem_limit_bytes=24 * 2**20),
        cost_estimate=pl.CostEstimate(
            flops=4 * slots * lanes * width,
            bytes_accessed=2 * (2 * slots + lanes + rows) * width,
            transcendentals=0,
        ),
        name="finish",
    )(*operands)
    if not together:
        blocks = jnp.concatenate([block[:size] for block, size in zip(blocks, used)])
        picked = jnp.dot(pick, blocks, preferred_element_type=F32)
        input_grad = [(row_weight * picked).astype(BF16)]
    return input_grad[0], grad_down, grad_up, losses


def slots_kernel(
    count, capacity, half_size, half_ref, owner_ref, adapter_ref, segment_ref, g_ref, *refs
):
    to_slot, to_half, marks_ref, sent_g = refs
    slots, rows = to_slot.shape
    out_width = g_ref.shape[1]
    eye = (iota((rows, rows), 0) == iota((rows, rows), 1)).astype(BF16)
    owner = lax.dot_general(
        owner_ref[...].astype(F32).astype(BF16),
        eye,
        (((0,), (0,)), ((), ())),
        preferred_element_type=F32,
    ).astype(jnp.int32)
    n_dev = 2 * half_size
    hot = (iota((n_dev, rows), 0) == owner).astype(F32)
    earlier = (iota((rows, rows), 0) < iota((rows, rows), 1)).astype(BF16)
    before = jnp.dot(hot.astype(BF16), earlier, preferred_element_type=F32)
    rank = jnp.sum(before * hot, axis=0, keepdims=True).astype(jnp.int32)
    at_slot = iota((slots, rows), 0)
    to_slot[...] = (at_slot == owner * capacity + rank).astype(BF16)
    far = owner // half_size != half_ref[0]
    position = (owner % half_size * 2 + far.astype(jnp.int32)) * capacity + rank
    hot_half = (at_slot == position).astype(BF16)
    to_half[...] = hot_half
    lane = iota((MARKS, rows), 0)
    marks = ((lane == adapter_ref[...]) | (lane == segment_ref[...] + count)).astype(BF16)
    marks_ref[...] = marks
    sent_g[:, :out_width] = jnp.dot(hot_half, g_ref[...], preferred_element_type=F32).astype(BF16)
    sent_g[:, out_width:] = lax.dot_general(
        hot_half, marks, (((1,), (1,)), ((), ())), preferred_element_type=F32
    ).astype(BF16)


def slot_rows(half_at, owner, adapter, segment, cotangent, count, capacity, half_size):
    rows, out_width = cotangent.shape
    slots = 2 * half_size * capacity
    vmem = pl.BlockSpec(memory_space=pltpu.VMEM)
    return pl.pallas_call(
        functools.partial(slots_kernel, count, capacity, half_size),
        out_shape=[
            jax.ShapeDtypeStruct((slots, rows), BF16),
            jax.ShapeDtypeStruct((slots, rows), BF16),
            jax.ShapeDtypeStruct((MARKS, rows), BF16),
            jax.ShapeDtypeStruct((slots, out_width + MARKS), BF16),
        ],
        in_specs=[pl.BlockSpec(memory_space=pltpu.SMEM)] + [vmem] * 4,
        out_specs=[vmem] * 4,
        name="slots",
    )(half_at.reshape(1), owner, adapter.reshape(1, rows), segment, cotangent)


def send_kernel(columns, to_slot, marks, g_ref, tokens_hbm, sent_hbm, tokens, sent, *sems):
    in_sems, out_sems = sems
    width, out_width = tokens.shape[1], g_ref.shape[1]
    parts = column_parts(width, columns)
    copies = [
        pltpu.make_async_copy(tokens_hbm.at[:, part], tokens.at[:, part], in_sems.at[at])
        for at, part in enumerate(parts)
    ]
    for copy in copies:
        copy.start()
    hot = to_slot[...]
    last = slice(width + out_width, width + out_width + MARKS)
    sent[:, width : width + out_width] = jnp.dot(
        hot, g_ref[...], preferred_element_type=F32
    ).astype(BF16)
    sent[:, last] = lax.dot_general(
        hot, marks[...], (((1,), (1,)), ((), ())), preferred_element_type=F32
    ).astype(BF16)
    outs = []

    def send(part):
        outs.append(
            pltpu.make_async_copy(
                sent.at[:, part], sent_hbm.at[:, part], out_sems.at[len(outs)]
            )
        )
        outs[-1].start()

    send(slice(width, width + out_width + MARKS))
    for copy, part in zip(copies, parts):
        copy.wait()
        sent[:, part] = jnp.dot(hot, tokens[:, part], preferred_element_type=F32).astype(BF16)
        send(part)
    for copy in outs:
        copy.wait()


def send_rows(to_slot, marks, cotangent, tokens):
    slots, (rows, width) = to_slot.shape[0], tokens.shape
    columns = cotangent.shape[1]
    full = width + columns + MARKS
    n_parts = len(column_parts(width, columns))
    vmem, hbm = pl.BlockSpec(memory_space=pltpu.VMEM), pl.BlockSpec(memory_space=pl.ANY)
    return pl.pallas_call(
        functools.partial(send_kernel, columns),
        out_shape=jax.ShapeDtypeStruct((slots, full), BF16),
        in_specs=[vmem] * 3 + [hbm],
        out_specs=hbm,
        scratch_shapes=[
            pltpu.VMEM((rows, width), BF16),
            pltpu.VMEM((slots, full), BF16),
            pltpu.SemaphoreType.DMA((n_parts,)),
            pltpu.SemaphoreType.DMA((n_parts + 1,)),
        ],
        compiler_params=pltpu.CompilerParams(vmem_limit_bytes=32 * 2**20),
        cost_estimate=pl.CostEstimate(
            flops=2 * slots * rows * full,
            bytes_accessed=2 * (slots + rows) * full,
            transcendentals=0,
        ),
        name="send",
    )(to_slot, marks, cotangent, tokens)


def half_kernel(which_ref, up_hbm, down_hbm, out, sems):
    out_width, which = up_hbm.shape[2], which_ref[0]
    width = down_hbm.shape[2]
    copies = [
        pltpu.make_async_copy(up_hbm.at[which], out.at[:, pl.ds(0, out_width)], sems.at[0]),
        pltpu.make_async_copy(
            down_hbm.at[which], out.at[:, pl.ds(out_width, width)], sems.at[1]
        ),
    ]
    for copy in copies:
        copy.start()
    for copy in copies:
        copy.wait()


def half_of(which, up_pair, down_pair):
    _, rank_size, width = down_pair.shape
    hbm = pl.BlockSpec(memory_space=pl.ANY)
    return pl.pallas_call(
        half_kernel,
        out_shape=jax.ShapeDtypeStruct((rank_size, up_pair.shape[2] + width), BF16),
        in_specs=[pl.BlockSpec(memory_space=pltpu.SMEM), hbm, hbm],
        out_specs=pl.BlockSpec(memory_space=pltpu.VMEM),
        scratch_shapes=[pltpu.SemaphoreType.DMA((2,))],
        name="half",
    )(which.reshape(1), up_pair, down_pair)


def body(
    tokens,
    cotangent,
    owner,
    token_local_adapter,
    segment,
    pair_sequence_order,
    frozen_margin_score,
    adapter_down_weight,
    adapter_up_weight,
):
    rows, width = tokens.shape
    out_width = cotangent.shape[1]
    n_grp, n_dev = lax.axis_size("grp"), lax.axis_size("ad")
    grp, me = lax.axis_index("grp"), lax.axis_index("ad")
    half_size = n_dev // 2
    spot = me % half_size
    capacity = max(2, 2 * rows // n_dev)
    slots = n_dev * capacity
    count, rank_size, _ = adapter_down_weight.shape
    seqs = frozen_margin_score.shape[1]
    lanes = count * rank_size
    down = adapter_down_weight.reshape(lanes, width)
    up = adapter_up_weight.reshape(lanes, out_width)

    def flipped(block, flip):
        return lax.ppermute(block, "ad", [(at, at ^ flip) for at in range(n_dev)])

    def other_grp(block):
        return lax.ppermute(block, "grp", [(0, 1), (1, 0)])

    half_mine = half_of(grp, adapter_up_weight, adapter_down_weight)
    far = flipped(half_mine, half_size)
    half_other = half_of(1 - grp, adapter_up_weight, adapter_down_weight)

    (owner,) = gate(lax.optimization_barrier((owner, half_mine))[0])
    row_seq = segment[0][:, None] == jnp.arange(seqs, dtype=jnp.int32)
    to_slot, to_half, marks, sent_g = slot_rows(
        me // half_size, owner, token_local_adapter, segment, cotangent, count, capacity, half_size
    )
    sent = send_rows(to_slot, marks, cotangent, tokens)

    halves = [list(range(half_size)), list(range(half_size, n_dev))]
    to_half = to_half.reshape(half_size, 2, capacity, rows)
    half_g = lax.all_to_all(
        sent_g.reshape(half_size, 2 * capacity, out_width + MARKS),
        "ad",
        split_axis=0,
        concat_axis=0,
        tiled=True,
        axis_index_groups=halves,
    )

    lane = jnp.arange(MARKS, dtype=jnp.int32)[None, :]
    which = (lane == jnp.stack([grp, 1 - grp])[:, None]).astype(F32)

    def land(blocks):
        return [block if at == 0 else flipped(block, 2 * at) for at, block in enumerate(blocks)]

    def hand_over(blocks):
        return blocks + [flipped(jnp.concatenate([block[capacity:] for block in blocks]), 1)]

    made_near = project(
        0, False, capacity, out_width, width, spot, half_g, which, [half_mine], [half_other]
    )
    landed_near = land(made_near)
    (sent,) = gate(lax.optimization_barrier((sent, made_near))[0])
    got = lax.all_to_all(
        sent.reshape(n_dev, capacity, width + out_width + MARKS),
        "ad",
        split_axis=0,
        concat_axis=0,
        tiled=True,
    ).reshape(slots, width + out_width + MARKS)

    (which_far,) = gate(lax.optimization_barrier((which, sent, landed_near))[0])
    far_other = other_grp(far)
    kept, handed = project(
        1, True, capacity, out_width, width, spot, half_g, which_far, [far], [far_other]
    )
    taken = flipped(handed, 1)
    landed_far = land(
        [
            jnp.concatenate([kept[at : at + capacity], taken[at : at + capacity]])
            for at in range(0, half_size // 2 * capacity, capacity)
        ]
    )
    pair_hot = pair_sequence_order[0][:, None] == jnp.arange(seqs, dtype=jnp.int32)
    at_me = (jnp.arange(n_dev, dtype=jnp.int32) == me)[:, None]
    own_scores = jnp.where(at_me, frozen_margin_score, 0.0).reshape(1, -1)
    own = jnp.concatenate(
        [
            jnp.pad(own_scores, ((0, 0), (0, -own_scores.shape[1] % MARKS))),
            jnp.zeros((1, count + seqs), F32),
            pair_hot.astype(F32).reshape(1, -1),
            jnp.zeros((1, MARKS - count - seqs - seqs * seqs), F32),
        ],
        axis=1,
    )
    part, rank_rows = score(own, got, down, up, count, seqs, rank_size, n_dev)
    told = lax.all_to_all(part, "ad", split_axis=0, concat_axis=0, tiled=True)

    chips = half_size // 2
    order = [2 * at for at in range(chips)] + [2 * at + 1 for at in range(chips)]
    near_flips = spot ^ jnp.array(order, dtype=jnp.int32)
    far_flips = spot ^ jnp.arange(half_size, dtype=jnp.int32)
    pick = jnp.concatenate([to_half[near_flips, 0], to_half[far_flips, 1]])
    pick = pick.reshape(slots, rows).T
    landed_far = lax.optimization_barrier((landed_far, told))[0]
    landed = hand_over(landed_near) + landed_far
    row_marks = jnp.pad(row_seq.astype(F32), ((0, 0), (count, MARKS - count - seqs)))
    input_grad, grad_down, grad_up, losses = finish(
        me,
        told,
        got,
        rank_rows,
        row_marks,
        count,
        seqs,
        width,
        pick,
        landed,
        [capacity] * chips + [chips * capacity] + [2 * capacity] * chips,
    )
    return (
        input_grad,
        grad_down.reshape(count, rank_size, width),
        grad_up.reshape(count, rank_size, out_width),
        losses,
    )


def solution(mesh):
    placed = (
        P(("grp", "ad"), None),
        P(("grp", "ad"), None),
        P(("grp", "ad"), None),
        P(("grp", "ad")),
        P(("grp", "ad"), None),
        P(("grp", "ad"), None),
        P(("grp", "ad"), None),
        P("ad", None, None),
        P("ad", None, None),
    )
    return jax.shard_map(
        body,
        mesh=mesh,
        in_specs=placed,
        out_specs=(
            P(("grp", "ad"), None),
            P(("grp", "ad"), None, None),
            P(("grp", "ad"), None, None),
            P(("grp", "ad")),
        ),
        check_vma=False,
    )
```

```python
import functools

import jax
import jax.numpy as jnp
from jax import lax
from jax.experimental import pallas as pl
from jax.experimental.pallas import tpu as pltpu
from jax.sharding import PartitionSpec as P

SCALE = 2.0
BETA = 0.1
LOSS_SCALE = 256.0
MARKS = 128
GATE_FLOPS = 2 * 10**11

F32 = jnp.float32
BF16 = jnp.bfloat16


def gate(*arrays):
    return pl.pallas_call(
        lambda *refs: None,
        out_shape=[jax.ShapeDtypeStruct(array.shape, array.dtype) for array in arrays],
        in_specs=[pl.BlockSpec(memory_space=pl.ANY)] * len(arrays),
        out_specs=[pl.BlockSpec(memory_space=pl.ANY)] * len(arrays),
        input_output_aliases={at: at for at in range(len(arrays))},
        cost_estimate=pl.CostEstimate(flops=GATE_FLOPS, bytes_accessed=0, transcendentals=0),
        name="gate",
    )(*arrays)


def project_kernel(side, split, capacity, out_width, n_outs, spot_ref, g_ref, which, *refs):
    n_spots = g_ref.shape[0]
    n_parts = (len(refs) - n_outs) // 2
    mine, other, outs = refs[:n_parts], refs[n_parts : 2 * n_parts], refs[2 * n_parts :]
    first = side * capacity
    spot = spot_ref[0]
    rows = jnp.concatenate(
        [g_ref[spot ^ flip, first : first + capacity, :] for flip in range(n_spots)], axis=0
    )
    marks = rows[:, out_width:].astype(F32)
    contract = (((1,), (1,)), ((), ()))
    pulls = []
    for at, parts in enumerate((mine, other)):
        member = jnp.sum(marks * which[at : at + 1, :], axis=1, keepdims=True)
        pull = lax.dot_general(
            rows[:, :out_width], parts[0][:, :out_width], contract, preferred_element_type=F32
        )
        pulls.append((member * pull).astype(BF16))
    done = 0
    for at in range(n_parts):
        start, end = (out_width if at == 0 else 0), mine[at].shape[1]
        while start < end:
            size = min(1024, end - start)
            columns = slice(start, start + size)
            made = jnp.dot(pulls[0], mine[at][:, columns], preferred_element_type=F32)
            made = made + jnp.dot(pulls[1], other[at][:, columns], preferred_element_type=F32)
            made = made.astype(BF16)
            for flip in range(n_spots):
                row = made[flip * capacity : (flip + 1) * capacity]
                if split:
                    chip = flip // 2 * capacity
                    outs[flip % 2][chip : chip + capacity, done : done + size] = row
                else:
                    core = flip % 2 * capacity
                    outs[flip // 2][core : core + capacity, done : done + size] = row
            start, done = start + size, done + size


def project(side, split, capacity, out_width, width, spot, got_g, which, mine, other):
    n_spots = got_g.shape[0]
    chips = n_spots // 2
    blocks = [(chips * capacity, width)] * 2 if split else [(2 * capacity, width)] * chips
    if capacity % 16 == 0:
        return pl.pallas_call(
            functools.partial(project_kernel, side, split, capacity, out_width, len(blocks)),
            out_shape=[jax.ShapeDtypeStruct(block, BF16) for block in blocks],
            in_specs=[pl.BlockSpec(memory_space=pltpu.SMEM)]
            + [pl.BlockSpec(memory_space=pltpu.VMEM)] * (2 + len(mine) + len(other)),
            cost_estimate=pl.CostEstimate(flops=1000, bytes_accessed=1000, transcendentals=0),
            name="project",
        )(spot.reshape(1), got_g, which, *mine, *other)
    order = spot ^ jnp.arange(n_spots, dtype=jnp.int32)
    rows = got_g[order, side * capacity : (side + 1) * capacity].reshape(n_spots * capacity, -1)
    marks = rows[:, out_width:].astype(F32)
    made = 0.0
    for at, parts in enumerate((mine, other)):
        whole = jnp.concatenate(parts, axis=1)
        pull = jnp.dot(rows[:, :out_width], whole[:, :out_width].T, preferred_element_type=F32)
        pull = (jnp.sum(marks * which[at], axis=1, keepdims=True) * pull).astype(BF16)
        made = made + jnp.dot(pull, whole[:, out_width:], preferred_element_type=F32)
    made = made.astype(BF16).reshape(chips, 2, capacity, width)
    if split:
        return [made[:, core].reshape(chips * capacity, width) for core in range(2)]
    return list(made.reshape(chips, 2 * capacity, width))


def iota(shape, axis):
    return lax.broadcasted_iota(jnp.int32, shape, axis)


def exact_dot(hot, values):
    return jnp.dot(hot, values, precision=lax.Precision.HIGHEST, preferred_element_type=F32)


def column_parts(width, columns):
    return [slice(start, min(start + columns, width)) for start in range(0, width, columns)]


def sequence_lanes(score_lanes, count, seqs):
    shape = (MARKS, score_lanes)
    return (iota(shape, 0) == count + iota(shape, 1) % seqs).astype(F32)


def pull_kernel(count, rank_size, g_ref, up, out):
    lanes, out_width = up.shape
    marks = g_ref[:, out_width:]
    lane = iota((g_ref.shape[0], lanes), 1) // rank_size
    member = jnp.zeros((g_ref.shape[0], lanes), F32)
    for which in range(count):
        member = jnp.where(lane == which, marks[:, which : which + 1].astype(F32), member)
    pull = member * lax.dot_general(
        g_ref[:, :out_width], up[...], (((1,), (1,)), ((), ())), preferred_element_type=F32
    )
    out[:, :lanes] = pull.astype(BF16)
    out[:, lanes:] = marks


def pull_rows(g_rows, up, count, rank_size):
    vmem = pl.BlockSpec(memory_space=pltpu.VMEM)
    return pl.pallas_call(
        functools.partial(pull_kernel, count, rank_size),
        out_shape=jax.ShapeDtypeStruct((g_rows.shape[0], up.shape[0] + MARKS), BF16),
        in_specs=[vmem] * 2,
        out_specs=vmem,
        cost_estimate=pl.CostEstimate(flops=1000, bytes_accessed=1000, transcendentals=0),
        name="pull",
    )(g_rows, up)


def in_slots(here, near, across):
    first = jnp.where(here == 0, near, across)
    return jnp.concatenate([first, jnp.where(here == 0, across, near)], axis=0)


def score_kernel(
    count, seqs, capacity, here_ref, own_ref, near_ref, across_ref, down, got_hbm, *refs
):
    told_ref, rows_hbm, got, hidden_rows, got_sems, rows_sem = refs
    lanes, width = down.shape
    parts = column_parts(width, 4096)
    copies = [
        pltpu.make_async_copy(got_hbm.at[:, part], got.at[:, part], got_sems.at[at])
        for at, part in enumerate(parts)
    ]
    for copy in copies:
        copy.start()
    contract = (((1,), (1,)), ((), ()))
    both = in_slots(here_ref[0], near_ref[...].astype(F32), across_ref[...].astype(F32))
    pulled, marks = both[:, :lanes], both[:, lanes:]
    slots = got.shape[0]
    lane = iota((slots, lanes), 1) // (lanes // count)
    member = jnp.zeros((slots, lanes), F32)
    for which in range(count):
        member = jnp.where(lane == which, marks[:, which : which + 1], member)
    total = jnp.zeros((slots, lanes), F32)
    for copy, part in zip(copies, parts):
        copy.wait()
        total = total + lax.dot_general(
            got[:, part], down[:, part], contract, preferred_element_type=F32
        )
    hidden = (member * total).astype(BF16)
    hidden_rows[...] = hidden
    rows_copy = pltpu.make_async_copy(hidden_rows, rows_hbm, rows_sem)
    rows_copy.start()
    inner = SCALE * jnp.sum(hidden.astype(F32) * pulled, axis=1, keepdims=True)
    n_dev, _, all_lanes = told_ref.shape
    scored = marks * inner
    if capacity % 8 == 0:
        part = jnp.sum(scored.reshape(n_dev, capacity, MARKS), axis=1)
    else:
        hot = iota((n_dev, slots), 1) // capacity == iota((n_dev, slots), 0)
        part = exact_dot(hot.astype(F32), scored)
    score_lanes = all_lanes - MARKS
    spread = exact_dot(part, sequence_lanes(score_lanes, count, seqs))
    at_device = iota((n_dev, score_lanes), 0) == iota((n_dev, score_lanes), 1) // seqs
    row = jnp.sum(jnp.where(at_device, spread, 0.0), axis=0, keepdims=True)
    row = jnp.concatenate([row, jnp.zeros((1, MARKS), F32)], axis=1) + own_ref[...]
    told_ref[...] = jnp.broadcast_to(row[None], told_ref.shape)
    rows_copy.wait()


def score(here, own, near, across, got, down, count, seqs, n_dev):
    slots = got.shape[0]
    lanes, width = down.shape
    n_parts = len(column_parts(width, 4096))
    vmem, hbm = pl.BlockSpec(memory_space=pltpu.VMEM), pl.BlockSpec(memory_space=pl.ANY)
    return pl.pallas_call(
        functools.partial(score_kernel, count, seqs, slots // n_dev),
        out_shape=[
            jax.ShapeDtypeStruct((n_dev,) + own.shape, F32),
            pltpu.HBM((slots, lanes), BF16),
        ],
        in_specs=[pl.BlockSpec(memory_space=pltpu.SMEM)] + [vmem] * 4 + [hbm],
        out_specs=[vmem, pl.BlockSpec(memory_space=pltpu.HBM)],
        scratch_shapes=[
            pltpu.VMEM(got.shape, BF16),
            pltpu.VMEM((slots, lanes), BF16),
            pltpu.SemaphoreType.DMA((n_parts,)),
            pltpu.SemaphoreType.DMA,
        ],
        compiler_params=pltpu.CompilerParams(vmem_limit_bytes=16 * 2**20),
        cost_estimate=pl.CostEstimate(
            flops=2 * slots * lanes * width,
            bytes_accessed=2 * (slots + lanes) * width,
            transcendentals=0,
        ),
        name="score",
    )(here.reshape(1), own, near, across, down, got)


def weights(total, count, seqs):
    lane = iota(total.shape, 1)

    def column(at):
        return total[:, at : at + 1]

    pick = [[column(count + seqs + i * seqs + s) for s in range(seqs)] for i in range(seqs)]
    ordered = [sum(pick[i][s] * column(count + s) for s in range(seqs)) for i in range(seqs)]
    losses, by_order = jnp.zeros(total.shape, F32), []
    for pair in range(seqs // 2):
        margin = BETA * (ordered[2 * pair] - ordered[2 * pair + 1])
        small = jnp.exp(-jnp.abs(margin))
        loss = jnp.maximum(-margin, 0.0) + jnp.log1p(small)
        losses = jnp.where(lane == pair, loss, losses)
        lean = jnp.where(margin > 0.0, small, 1.0) / (1.0 + small)
        by_order += [-BETA * lean, BETA * lean]
    table = jnp.zeros(total.shape, F32)
    for s in range(seqs):
        weight = LOSS_SCALE * sum(pick[i][s] * by_order[i] for i in range(seqs))
        table = jnp.where(lane == count + s, weight, table)
    return losses, table


def finish_kernel(count, seqs, capacity, used, place_ref, told_ref, *refs):
    row_marks, *small_hbms, got_hbm = refs[:5]
    refs = refs[5:]
    if used:
        pick, *refs = refs
    block_hbms, refs = refs[: len(used)], refs[len(used) :]
    losses_ref, row_weight, upper_ref, down_hbm, *refs = refs
    if used:
        input_hbm, *smalls = refs[:4]
        got, grad_down, rows, input_grad, *sems = refs[4:]
        small_sems, got_sems, down_sems, block_sems, input_sems = sems
    else:
        smalls, refs = refs[:3], refs[3:]
        got, grad_down, small_sems, got_sems, down_sems = refs
    lanes, width = grad_down.shape
    parts = column_parts(width, 2048)
    copies = [
        pltpu.make_async_copy(got_hbm.at[:, part], got.at[:, part], got_sems.at[at])
        for at, part in enumerate(parts)
    ]
    first, block_copies = 0, []
    for at, size in enumerate(used):
        block_copies.append(
            pltpu.make_async_copy(
                block_hbms[at].at[pl.ds(0, size)], rows.at[pl.ds(first, size)], block_sems.at[at]
            )
        )
        first += size
    small_copies = [
        pltpu.make_async_copy(hbm, small, small_sems.at[at])
        for at, (hbm, small) in enumerate(zip(small_hbms, smalls))
    ]
    for copy in small_copies + copies + block_copies:
        copy.start()

    told = jnp.concatenate([told_ref[at] for at in range(told_ref.shape[0])], axis=0)
    score_lanes = told.shape[1] - MARKS
    sums = jnp.sum(told[:, :score_lanes], axis=0, keepdims=True)
    shape = (told.shape[0], score_lanes)
    spread = jnp.where(iota(shape, 0) == iota(shape, 1) // seqs, sums, 0.0)
    total = told[:, score_lanes:] + lax.dot_general(
        spread,
        sequence_lanes(score_lanes, count, seqs),
        (((1,), (1,)), ((), ())),
        precision=lax.Precision.HIGHEST,
        preferred_element_type=F32,
    )
    losses, table = weights(total, count, seqs)
    n_dev, slots, here = total.shape[0], got.shape[0], place_ref[1]
    mine = iota(total.shape, 0) == place_ref[0]
    pair_lane = iota(losses.shape, 1)
    for pair in range(seqs // 2):
        losses_ref[pair] = jnp.sum(jnp.where(mine & (pair_lane == pair), losses, 0.0))
    my_table = jnp.sum(jnp.where(mine, table, 0.0), axis=0, keepdims=True)
    my_weight = SCALE * jnp.sum(row_marks[...] * my_table, axis=1, keepdims=True)
    row_weight[...] = my_weight
    hot = iota((slots, n_dev), 0) // capacity == iota((slots, n_dev), 1)
    slot_table = exact_dot(hot.astype(F32), table)
    for copy in small_copies:
        copy.wait()
    hidden, near_rank, across_rank = [small[...] for small in smalls]
    both = in_slots(here, near_rank.astype(F32), across_rank.astype(F32))
    pulled, marks = both[:, :lanes], both[:, lanes:]
    weight = jnp.sum(marks * slot_table, axis=1, keepdims=True)
    upper_ref[...] = (weight * hidden.astype(F32)).astype(BF16)
    lower = (weight * pulled).astype(BF16)
    contract = (((0,), (0,)), ((), ()))
    outs = []
    for at, part in enumerate(parts):
        copies[at].wait()
        made = lax.dot_general(lower, got[:, part], contract, preferred_element_type=F32)
        grad_down[:, part] = (SCALE * made).astype(BF16)
        outs.append(
            pltpu.make_async_copy(grad_down.at[:, part], down_hbm.at[:, part], down_sems.at[at])
        )
        outs[-1].start()
    if used:
        for copy in block_copies:
            copy.wait()
        for at, part in enumerate(parts):
            picked = jnp.dot(pick[...], rows[:, part], preferred_element_type=F32)
            input_grad[:, part] = (my_weight * picked).astype(BF16)
            outs.append(
                pltpu.make_async_copy(
                    input_grad.at[:, part], input_hbm.at[:, part], input_sems.at[at]
                )
            )
            outs[-1].start()
    for copy in outs:
        copy.wait()


def finish(place, told, got, smalls, row_marks, count, seqs, pick, blocks, used):
    (slots, width), lanes = got.shape, smalls[0].shape[1]
    rows = row_marks.shape[0]
    n_dev = told.shape[0]
    n_parts = len(column_parts(width, 2048))
    together = not any(size % 16 for size in used)
    vmem, hbm = pl.BlockSpec(memory_space=pltpu.VMEM), pl.BlockSpec(memory_space=pltpu.HBM)
    sems = pltpu.SemaphoreType.DMA
    out_shape = [
        jax.ShapeDtypeStruct((seqs // 2,), F32),
        jax.ShapeDtypeStruct((rows, 1), F32),
        jax.ShapeDtypeStruct((slots, lanes), BF16),
        jax.ShapeDtypeStruct((lanes, width), BF16),
    ]
    in_specs = [pl.BlockSpec(memory_space=pltpu.SMEM)] + [vmem] * 2 + [hbm] * 4
    smalls = [pltpu.with_memory_space_constraint(small, pltpu.HBM) for small in smalls]
    operands = [place, told, row_marks, *smalls, got]
    scratch = [
        *[pltpu.VMEM(small.shape, BF16) for small in smalls],
        pltpu.VMEM(got.shape, BF16),
        pltpu.VMEM((lanes, width), BF16),
    ]
    scratch_sems = [sems((3,)), sems((n_parts,)), sems((n_parts,))]
    if together:
        out_shape.append(jax.ShapeDtypeStruct((rows, width), BF16))
        in_specs += [vmem] + [hbm] * len(blocks)
        operands += [pick, *blocks]
        scratch += [pltpu.VMEM((slots, width), BF16), pltpu.VMEM((rows, width), BF16)]
        scratch_sems += [sems((len(blocks),)), sems((n_parts,))]
    losses, row_weight, upper, grad_down, *input_grad = pl.pallas_call(
        functools.partial(
            finish_kernel, count, seqs, slots // n_dev, used if together else []
        ),
        out_shape=out_shape,
        in_specs=in_specs,
        out_specs=[pl.BlockSpec(memory_space=pltpu.SMEM), vmem, vmem] + [hbm] * (len(out_shape) - 3),
        scratch_shapes=scratch + scratch_sems,
        compiler_params=pltpu.CompilerParams(vmem_limit_bytes=24 * 2**20),
        cost_estimate=pl.CostEstimate(
            flops=4 * slots * lanes * width,
            bytes_accessed=2 * (2 * slots + lanes + rows) * width,
            transcendentals=0,
        ),
        name="finish",
    )(*operands)
    if not together:
        blocks = jnp.concatenate([block[:size] for block, size in zip(blocks, used)])
        picked = jnp.dot(pick, blocks, preferred_element_type=F32)
        input_grad = [(row_weight * picked).astype(BF16)]
    return input_grad[0], grad_down, upper, losses


def up_kernel(here_ref, upper, near_g, across_g, out):
    out_width = out.shape[1]
    contract = (((0,), (0,)), ((), ()))
    g_rows = in_slots(here_ref[0], near_g[:, :out_width], across_g[:, :out_width])
    made = lax.dot_general(upper[...], g_rows, contract, preferred_element_type=F32)
    out[...] = (SCALE * made).astype(BF16)


def up_gradient(here, upper, near_g, across_g):
    vmem = pl.BlockSpec(memory_space=pltpu.VMEM)
    return pl.pallas_call(
        up_kernel,
        out_shape=jax.ShapeDtypeStruct((upper.shape[1], near_g.shape[1] - MARKS), BF16),
        in_specs=[pl.BlockSpec(memory_space=pltpu.SMEM)] + [vmem] * 3,
        out_specs=vmem,
        cost_estimate=pl.CostEstimate(
            flops=2 * upper.shape[0] * upper.shape[1] * near_g.shape[1],
            bytes_accessed=4 * near_g.shape[0] * near_g.shape[1],
            transcendentals=0,
        ),
        name="up",
    )(here.reshape(1), upper, near_g, across_g)


def slots_kernel(
    count, capacity, half_size, half_ref, owner_ref, adapter_ref, segment_ref, g_ref, *refs
):
    to_slot, to_half, sent_g = refs
    slots, rows = to_slot.shape
    out_width = g_ref.shape[1]
    eye = (iota((rows, rows), 0) == iota((rows, rows), 1)).astype(BF16)
    owner = lax.dot_general(
        owner_ref[...].astype(F32).astype(BF16),
        eye,
        (((0,), (0,)), ((), ())),
        preferred_element_type=F32,
    ).astype(jnp.int32)
    n_dev = 2 * half_size
    hot = (iota((n_dev, rows), 0) == owner).astype(F32)
    earlier = (iota((rows, rows), 0) < iota((rows, rows), 1)).astype(BF16)
    before = jnp.dot(hot.astype(BF16), earlier, preferred_element_type=F32)
    rank = jnp.sum(before * hot, axis=0, keepdims=True).astype(jnp.int32)
    at_slot = iota((slots, rows), 0)
    to_slot[...] = (at_slot == owner * capacity + rank).astype(BF16)
    far = owner // half_size != half_ref[0]
    position = (owner % half_size * 2 + far.astype(jnp.int32)) * capacity + rank
    hot_half = (at_slot == position).astype(BF16)
    to_half[...] = hot_half
    lane = iota((MARKS, rows), 0)
    marks = ((lane == adapter_ref[...]) | (lane == segment_ref[...] + count)).astype(BF16)
    sent_g[:, :out_width] = jnp.dot(hot_half, g_ref[...], preferred_element_type=F32).astype(BF16)
    sent_g[:, out_width:] = lax.dot_general(
        hot_half, marks, (((1,), (1,)), ((), ())), preferred_element_type=F32
    ).astype(BF16)


def slot_rows(half_at, owner, adapter, segment, cotangent, count, capacity, half_size):
    rows, out_width = cotangent.shape
    slots = 2 * half_size * capacity
    vmem = pl.BlockSpec(memory_space=pltpu.VMEM)
    return pl.pallas_call(
        functools.partial(slots_kernel, count, capacity, half_size),
        out_shape=[
            jax.ShapeDtypeStruct((slots, rows), BF16),
            jax.ShapeDtypeStruct((slots, rows), BF16),
            jax.ShapeDtypeStruct((slots, out_width + MARKS), BF16),
        ],
        in_specs=[pl.BlockSpec(memory_space=pltpu.SMEM)] + [vmem] * 4,
        out_specs=[vmem] * 3,
        name="slots",
    )(half_at.reshape(1), owner, adapter.reshape(1, rows), segment, cotangent)


def send_kernel(to_slot, tokens_hbm, sent_hbm, tokens, sent, in_sems, out_sems):
    parts = column_parts(tokens.shape[1], 1024)
    copies = [
        pltpu.make_async_copy(tokens_hbm.at[:, part], tokens.at[:, part], in_sems.at[at])
        for at, part in enumerate(parts)
    ]
    for copy in copies:
        copy.start()
    hot = to_slot[...]
    outs = []
    for at, part in enumerate(parts):
        copies[at].wait()
        sent[:, part] = jnp.dot(hot, tokens[:, part], preferred_element_type=F32).astype(BF16)
        outs.append(
            pltpu.make_async_copy(sent.at[:, part], sent_hbm.at[:, part], out_sems.at[at])
        )
        outs[-1].start()
    for copy in outs:
        copy.wait()


def send_rows(to_slot, tokens):
    slots, (rows, width) = to_slot.shape[0], tokens.shape
    n_parts = len(column_parts(width, 1024))
    vmem, hbm = pl.BlockSpec(memory_space=pltpu.VMEM), pl.BlockSpec(memory_space=pl.ANY)
    return pl.pallas_call(
        send_kernel,
        out_shape=jax.ShapeDtypeStruct((slots, width), BF16),
        in_specs=[vmem, hbm],
        out_specs=hbm,
        scratch_shapes=[
            pltpu.VMEM((rows, width), BF16),
            pltpu.VMEM((slots, width), BF16),
            pltpu.SemaphoreType.DMA((n_parts,)),
            pltpu.SemaphoreType.DMA((n_parts,)),
        ],
        compiler_params=pltpu.CompilerParams(vmem_limit_bytes=32 * 2**20),
        cost_estimate=pl.CostEstimate(
            flops=2 * slots * rows * width,
            bytes_accessed=2 * (slots + rows) * width,
            transcendentals=0,
        ),
        name="send",
    )(to_slot, tokens)


def half_kernel(which_ref, up_hbm, down_hbm, out, sems):
    out_width, which = up_hbm.shape[2], which_ref[0]
    width = down_hbm.shape[2]
    copies = [
        pltpu.make_async_copy(up_hbm.at[which], out.at[:, pl.ds(0, out_width)], sems.at[0]),
        pltpu.make_async_copy(
            down_hbm.at[which], out.at[:, pl.ds(out_width, width)], sems.at[1]
        ),
    ]
    for copy in copies:
        copy.start()
    for copy in copies:
        copy.wait()


def half_of(which, up_pair, down_pair):
    _, rank_size, width = down_pair.shape
    hbm = pl.BlockSpec(memory_space=pl.ANY)
    return pl.pallas_call(
        half_kernel,
        out_shape=jax.ShapeDtypeStruct((rank_size, up_pair.shape[2] + width), BF16),
        in_specs=[pl.BlockSpec(memory_space=pltpu.SMEM), hbm, hbm],
        out_specs=pl.BlockSpec(memory_space=pltpu.VMEM),
        scratch_shapes=[pltpu.SemaphoreType.DMA((2,))],
        name="half",
    )(which.reshape(1), up_pair, down_pair)


def body(
    tokens,
    cotangent,
    owner,
    token_local_adapter,
    segment,
    pair_sequence_order,
    frozen_margin_score,
    adapter_down_weight,
    adapter_up_weight,
):
    rows, width = tokens.shape
    out_width = cotangent.shape[1]
    n_grp, n_dev = lax.axis_size("grp"), lax.axis_size("ad")
    grp, me = lax.axis_index("grp"), lax.axis_index("ad")
    half_size = n_dev // 2
    spot = me % half_size
    capacity = max(2, 2 * rows // n_dev)
    slots = n_dev * capacity
    count, rank_size, _ = adapter_down_weight.shape
    seqs = frozen_margin_score.shape[1]
    lanes = count * rank_size
    down = adapter_down_weight.reshape(lanes, width)
    up = adapter_up_weight.reshape(lanes, out_width)

    def flipped(block, flip):
        return lax.ppermute(block, "ad", [(at, at ^ flip) for at in range(n_dev)])

    def other_grp(block):
        return lax.ppermute(block, "grp", [(0, 1), (1, 0)])

    half_mine = half_of(grp, adapter_up_weight, adapter_down_weight)
    far = flipped(half_mine, half_size)
    half_other = half_of(1 - grp, adapter_up_weight, adapter_down_weight)

    (owner,) = gate(lax.optimization_barrier((owner, half_mine))[0])
    row_seq = segment[0][:, None] == jnp.arange(seqs, dtype=jnp.int32)
    to_slot, to_half, sent_g = slot_rows(
        me // half_size, owner, token_local_adapter, segment, cotangent, count, capacity, half_size
    )
    sent = send_rows(to_slot, tokens)

    halves = [list(range(half_size)), list(range(half_size, n_dev))]
    to_half = to_half.reshape(half_size, 2, capacity, rows)
    half_g = lax.all_to_all(
        sent_g.reshape(half_size, 2 * capacity, out_width + MARKS),
        "ad",
        split_axis=0,
        concat_axis=0,
        tiled=True,
        axis_index_groups=halves,
    )

    lane = jnp.arange(MARKS, dtype=jnp.int32)[None, :]
    which = (lane == jnp.stack([grp, 1 - grp])[:, None]).astype(F32)

    def land(blocks):
        return [block if at == 0 else flipped(block, 2 * at) for at, block in enumerate(blocks)]

    def hand_over(blocks):
        return blocks + [flipped(jnp.concatenate([block[capacity:] for block in blocks]), 1)]

    made_near = project(
        0, False, capacity, out_width, width, spot, half_g, which, [half_mine], [half_other]
    )
    landed_near = land(made_near)
    (sent,) = gate(lax.optimization_barrier((sent, made_near))[0])
    got = lax.all_to_all(
        sent.reshape(n_dev, capacity, width),
        "ad",
        split_axis=0,
        concat_axis=0,
        tiled=True,
    ).reshape(slots, width)

    (which_far,) = gate(lax.optimization_barrier((which, sent, landed_near))[0])
    far_other = other_grp(far)
    kept, handed = project(
        1, True, capacity, out_width, width, spot, half_g, which_far, [far], [far_other]
    )
    taken = flipped(handed, 1)
    landed_far = land(
        [
            jnp.concatenate([kept[at : at + capacity], taken[at : at + capacity]])
            for at in range(0, half_size // 2 * capacity, capacity)
        ]
    )
    here = me // half_size
    near_g = half_g[:, :capacity].reshape(-1, out_width + MARKS)
    far_g = half_g[:, capacity:].reshape(-1, out_width + MARKS)
    far_ups = far[:, :out_width], far_other[:, :out_width]
    far_up = jnp.concatenate(
        [jnp.where(grp == 0, *far_ups), jnp.where(grp == 0, *far_ups[::-1])]
    )
    near_rank = pull_rows(near_g, up, count, rank_size)
    across_rank = flipped(pull_rows(far_g, far_up, count, rank_size), half_size)
    across_g = flipped(lax.optimization_barrier((far_g, got))[0], half_size)

    pair_hot = pair_sequence_order[0][:, None] == jnp.arange(seqs, dtype=jnp.int32)
    at_me = (jnp.arange(n_dev, dtype=jnp.int32) == me)[:, None]
    own_scores = jnp.where(at_me, frozen_margin_score, 0.0).reshape(1, -1)
    own = jnp.concatenate(
        [
            jnp.pad(own_scores, ((0, 0), (0, -own_scores.shape[1] % MARKS))),
            jnp.zeros((1, count + seqs), F32),
            pair_hot.astype(F32).reshape(1, -1),
            jnp.zeros((1, MARKS - count - seqs - seqs * seqs), F32),
        ],
        axis=1,
    )
    part, hidden_rows = score(
        here, own, near_rank, across_rank, got, down, count, seqs, n_dev
    )
    told = lax.all_to_all(part, "ad", split_axis=0, concat_axis=0, tiled=True)

    chips = half_size // 2
    order = [2 * at for at in range(chips)] + [2 * at + 1 for at in range(chips)]
    near_flips = spot ^ jnp.array(order, dtype=jnp.int32)
    far_flips = spot ^ jnp.arange(half_size, dtype=jnp.int32)
    pick = jnp.concatenate([to_half[near_flips, 0], to_half[far_flips, 1]])
    pick = pick.reshape(slots, rows).T
    landed_far = lax.optimization_barrier((landed_far, told))[0]
    landed = hand_over(landed_near) + landed_far
    row_marks = jnp.pad(row_seq.astype(F32), ((0, 0), (count, MARKS - count - seqs)))
    input_grad, grad_down, upper, losses = finish(
        jnp.stack([me, here]),
        told,
        got,
        [hidden_rows, near_rank, across_rank],
        row_marks,
        count,
        seqs,
        pick,
        landed,
        [capacity] * chips + [chips * capacity] + [2 * capacity] * chips,
    )
    grad_up = up_gradient(here, upper, near_g, across_g)
    return (
        input_grad,
        grad_down.reshape(count, rank_size, width),
        grad_up.reshape(count, rank_size, out_width),
        losses,
    )


def solution(mesh):
    placed = (
        P(("grp", "ad"), None),
        P(("grp", "ad"), None),
        P(("grp", "ad"), None),
        P(("grp", "ad")),
        P(("grp", "ad"), None),
        P(("grp", "ad"), None),
        P(("grp", "ad"), None),
        P("ad", None, None),
        P("ad", None, None),
    )
    return jax.shard_map(
        body,
        mesh=mesh,
        in_specs=placed,
        out_specs=(
            P(("grp", "ad"), None),
            P(("grp", "ad"), None, None),
            P(("grp", "ad"), None, None),
            P(("grp", "ad")),
        ),
        check_vma=False,
    )
```

```python
import functools

import jax
import jax.numpy as jnp
from jax import lax
from jax.experimental import pallas as pl
from jax.experimental.pallas import tpu as pltpu
from jax.sharding import PartitionSpec as P

SCALE = 2.0
BETA = 0.1
LOSS_SCALE = 256.0
MARKS = 128
GATE_FLOPS = 2 * 10**11

F32 = jnp.float32
BF16 = jnp.bfloat16


def gate(*arrays):
    return pl.pallas_call(
        lambda *refs: None,
        out_shape=[jax.ShapeDtypeStruct(array.shape, array.dtype) for array in arrays],
        in_specs=[pl.BlockSpec(memory_space=pl.ANY)] * len(arrays),
        out_specs=[pl.BlockSpec(memory_space=pl.ANY)] * len(arrays),
        input_output_aliases={at: at for at in range(len(arrays))},
        cost_estimate=pl.CostEstimate(flops=GATE_FLOPS, bytes_accessed=0, transcendentals=0),
        name="gate",
    )(*arrays)


def project_kernel(side, split, capacity, out_width, n_outs, spot_ref, g_ref, which, *refs):
    n_spots = g_ref.shape[0]
    n_parts = (len(refs) - n_outs) // 2
    mine, other, outs = refs[:n_parts], refs[n_parts : 2 * n_parts], refs[2 * n_parts :]
    first = side * capacity
    spot = spot_ref[0]
    rows = jnp.concatenate(
        [g_ref[spot ^ flip, first : first + capacity, :] for flip in range(n_spots)], axis=0
    )
    marks = rows[:, out_width:].astype(F32)
    contract = (((1,), (1,)), ((), ()))
    pulls = []
    for at, parts in enumerate((mine, other)):
        member = jnp.sum(marks * which[at : at + 1, :], axis=1, keepdims=True)
        pull = lax.dot_general(
            rows[:, :out_width], parts[0][:, :out_width], contract, preferred_element_type=F32
        )
        pulls.append((member * pull).astype(BF16))
    done = 0
    for at in range(n_parts):
        start, end = (out_width if at == 0 else 0), mine[at].shape[1]
        while start < end:
            size = min(1024, end - start)
            columns = slice(start, start + size)
            made = jnp.dot(pulls[0], mine[at][:, columns], preferred_element_type=F32)
            made = made + jnp.dot(pulls[1], other[at][:, columns], preferred_element_type=F32)
            made = made.astype(BF16)
            for flip in range(n_spots):
                row = made[flip * capacity : (flip + 1) * capacity]
                if split:
                    chip = flip // 2 * capacity
                    outs[flip % 2][chip : chip + capacity, done : done + size] = row
                else:
                    core = flip % 2 * capacity
                    outs[flip // 2][core : core + capacity, done : done + size] = row
            start, done = start + size, done + size


def project(side, split, capacity, out_width, width, spot, got_g, which, mine, other):
    n_spots = got_g.shape[0]
    chips = n_spots // 2
    blocks = [(chips * capacity, width)] * 2 if split else [(2 * capacity, width)] * chips
    if capacity % 16 == 0:
        return pl.pallas_call(
            functools.partial(project_kernel, side, split, capacity, out_width, len(blocks)),
            out_shape=[jax.ShapeDtypeStruct(block, BF16) for block in blocks],
            in_specs=[pl.BlockSpec(memory_space=pltpu.SMEM)]
            + [pl.BlockSpec(memory_space=pltpu.VMEM)] * (2 + len(mine) + len(other)),
            cost_estimate=pl.CostEstimate(flops=1000, bytes_accessed=1000, transcendentals=0),
            name="project",
        )(spot.reshape(1), got_g, which, *mine, *other)
    order = spot ^ jnp.arange(n_spots, dtype=jnp.int32)
    rows = got_g[order, side * capacity : (side + 1) * capacity].reshape(n_spots * capacity, -1)
    marks = rows[:, out_width:].astype(F32)
    made = 0.0
    for at, parts in enumerate((mine, other)):
        whole = jnp.concatenate(parts, axis=1)
        pull = jnp.dot(rows[:, :out_width], whole[:, :out_width].T, preferred_element_type=F32)
        pull = (jnp.sum(marks * which[at], axis=1, keepdims=True) * pull).astype(BF16)
        made = made + jnp.dot(pull, whole[:, out_width:], preferred_element_type=F32)
    made = made.astype(BF16).reshape(chips, 2, capacity, width)
    if split:
        return [made[:, core].reshape(chips * capacity, width) for core in range(2)]
    return list(made.reshape(chips, 2 * capacity, width))


def iota(shape, axis):
    return lax.broadcasted_iota(jnp.int32, shape, axis)


def exact_dot(hot, values):
    return jnp.dot(hot, values, precision=lax.Precision.HIGHEST, preferred_element_type=F32)


def column_parts(width, columns):
    return [slice(start, min(start + columns, width)) for start in range(0, width, columns)]


def sequence_lanes(score_lanes, count, seqs):
    shape = (MARKS, score_lanes)
    return (iota(shape, 0) == count + iota(shape, 1) % seqs).astype(F32)


def pull_kernel(count, rank_size, g_ref, up, out):
    lanes, out_width = up.shape
    marks = g_ref[:, out_width:]
    lane = iota((g_ref.shape[0], lanes), 1) // rank_size
    member = jnp.zeros((g_ref.shape[0], lanes), F32)
    for which in range(count):
        member = jnp.where(lane == which, marks[:, which : which + 1].astype(F32), member)
    pull = member * lax.dot_general(
        g_ref[:, :out_width], up[...], (((1,), (1,)), ((), ())), preferred_element_type=F32
    )
    out[:, :lanes] = pull.astype(BF16)
    out[:, lanes:] = marks


def pull_rows(g_rows, up, count, rank_size):
    vmem = pl.BlockSpec(memory_space=pltpu.VMEM)
    return pl.pallas_call(
        functools.partial(pull_kernel, count, rank_size),
        out_shape=jax.ShapeDtypeStruct((g_rows.shape[0], up.shape[0] + MARKS), BF16),
        in_specs=[vmem] * 2,
        out_specs=vmem,
        cost_estimate=pl.CostEstimate(flops=1000, bytes_accessed=1000, transcendentals=0),
        name="pull",
    )(g_rows, up)


def in_slots(here, near, across):
    first = jnp.where(here == 0, near, across)
    return jnp.concatenate([first, jnp.where(here == 0, across, near)], axis=0)


def score_kernel(
    count, seqs, capacity, here_ref, own_ref, near_ref, across_ref, down, got_hbm, *refs
):
    told_ref, rows_hbm, got, hidden_rows, got_sems, rows_sem = refs
    lanes, width = down.shape
    parts = column_parts(width, 4096)
    copies = [
        pltpu.make_async_copy(got_hbm.at[:, part], got.at[:, part], got_sems.at[at])
        for at, part in enumerate(parts)
    ]
    for copy in copies:
        copy.start()
    contract = (((1,), (1,)), ((), ()))
    both = in_slots(here_ref[0], near_ref[...].astype(F32), across_ref[...].astype(F32))
    pulled, marks = both[:, :lanes], both[:, lanes:]
    slots = got.shape[0]
    lane = iota((slots, lanes), 1) // (lanes // count)
    member = jnp.zeros((slots, lanes), F32)
    for which in range(count):
        member = jnp.where(lane == which, marks[:, which : which + 1], member)
    total = jnp.zeros((slots, lanes), F32)
    for copy, part in zip(copies, parts):
        copy.wait()
        total = total + lax.dot_general(
            got[:, part], down[:, part], contract, preferred_element_type=F32
        )
    hidden = (member * total).astype(BF16)
    hidden_rows[...] = hidden
    rows_copy = pltpu.make_async_copy(hidden_rows, rows_hbm, rows_sem)
    rows_copy.start()
    inner = SCALE * jnp.sum(hidden.astype(F32) * pulled, axis=1, keepdims=True)
    n_dev, _, all_lanes = told_ref.shape
    scored = marks * inner
    if capacity % 8 == 0:
        part = jnp.sum(scored.reshape(n_dev, capacity, MARKS), axis=1)
    else:
        hot = iota((n_dev, slots), 1) // capacity == iota((n_dev, slots), 0)
        part = exact_dot(hot.astype(F32), scored)
    score_lanes = all_lanes - MARKS
    spread = exact_dot(part, sequence_lanes(score_lanes, count, seqs))
    at_device = iota((n_dev, score_lanes), 0) == iota((n_dev, score_lanes), 1) // seqs
    row = jnp.sum(jnp.where(at_device, spread, 0.0), axis=0, keepdims=True)
    row = jnp.concatenate([row, jnp.zeros((1, MARKS), F32)], axis=1) + own_ref[...]
    told_ref[...] = jnp.broadcast_to(row[None], told_ref.shape)
    rows_copy.wait()


def score(here, own, near, across, got, down, count, seqs, n_dev):
    slots = got.shape[0]
    lanes, width = down.shape
    n_parts = len(column_parts(width, 4096))
    vmem, hbm = pl.BlockSpec(memory_space=pltpu.VMEM), pl.BlockSpec(memory_space=pl.ANY)
    return pl.pallas_call(
        functools.partial(score_kernel, count, seqs, slots // n_dev),
        out_shape=[
            jax.ShapeDtypeStruct((n_dev,) + own.shape, F32),
            pltpu.HBM((slots, lanes), BF16),
        ],
        in_specs=[pl.BlockSpec(memory_space=pltpu.SMEM)] + [vmem] * 4 + [hbm],
        out_specs=[vmem, pl.BlockSpec(memory_space=pltpu.HBM)],
        scratch_shapes=[
            pltpu.VMEM(got.shape, BF16),
            pltpu.VMEM((slots, lanes), BF16),
            pltpu.SemaphoreType.DMA((n_parts,)),
            pltpu.SemaphoreType.DMA,
        ],
        compiler_params=pltpu.CompilerParams(vmem_limit_bytes=16 * 2**20),
        cost_estimate=pl.CostEstimate(
            flops=2 * slots * lanes * width,
            bytes_accessed=2 * (slots + lanes) * width,
            transcendentals=0,
        ),
        name="score",
    )(here.reshape(1), own, near, across, down, got)


def weights(total, count, seqs):
    lane = iota(total.shape, 1)

    def column(at):
        return total[:, at : at + 1]

    pick = [[column(count + seqs + i * seqs + s) for s in range(seqs)] for i in range(seqs)]
    ordered = [sum(pick[i][s] * column(count + s) for s in range(seqs)) for i in range(seqs)]
    losses, by_order = jnp.zeros(total.shape, F32), []
    for pair in range(seqs // 2):
        margin = BETA * (ordered[2 * pair] - ordered[2 * pair + 1])
        small = jnp.exp(-jnp.abs(margin))
        loss = jnp.maximum(-margin, 0.0) + jnp.log1p(small)
        losses = jnp.where(lane == pair, loss, losses)
        lean = jnp.where(margin > 0.0, small, 1.0) / (1.0 + small)
        by_order += [-BETA * lean, BETA * lean]
    table = jnp.zeros(total.shape, F32)
    for s in range(seqs):
        weight = LOSS_SCALE * sum(pick[i][s] * by_order[i] for i in range(seqs))
        table = jnp.where(lane == count + s, weight, table)
    return losses, table


def finish_kernel(count, seqs, capacity, used, place_ref, told_ref, *refs):
    row_marks, *small_hbms, got_hbm = refs[:5]
    refs = refs[5:]
    if used:
        pick, *refs = refs
    block_hbms, refs = refs[: len(used)], refs[len(used) :]
    losses_ref, row_weight, upper_hbm, down_hbm, *refs, upper, upper_sem = refs
    if used:
        input_hbm, *smalls = refs[:4]
        got, grad_down, rows, input_grad, *sems = refs[4:]
        small_sems, got_sems, down_sems, block_sems, input_sems = sems
    else:
        smalls, refs = refs[:3], refs[3:]
        got, grad_down, small_sems, got_sems, down_sems = refs
    lanes, width = grad_down.shape
    parts = column_parts(width, 2048)
    copies = [
        pltpu.make_async_copy(got_hbm.at[:, part], got.at[:, part], got_sems.at[at])
        for at, part in enumerate(parts)
    ]
    first, block_copies = 0, []
    for at, size in enumerate(used):
        block_copies.append(
            pltpu.make_async_copy(
                block_hbms[at].at[pl.ds(0, size)], rows.at[pl.ds(first, size)], block_sems.at[at]
            )
        )
        first += size
    small_copies = [
        pltpu.make_async_copy(hbm, small, small_sems.at[at])
        for at, (hbm, small) in enumerate(zip(small_hbms, smalls))
    ]
    for copy in small_copies + copies + block_copies:
        copy.start()

    told = jnp.concatenate([told_ref[at] for at in range(told_ref.shape[0])], axis=0)
    score_lanes = told.shape[1] - MARKS
    sums = jnp.sum(told[:, :score_lanes], axis=0, keepdims=True)
    shape = (told.shape[0], score_lanes)
    spread = jnp.where(iota(shape, 0) == iota(shape, 1) // seqs, sums, 0.0)
    total = told[:, score_lanes:] + lax.dot_general(
        spread,
        sequence_lanes(score_lanes, count, seqs),
        (((1,), (1,)), ((), ())),
        precision=lax.Precision.HIGHEST,
        preferred_element_type=F32,
    )
    losses, table = weights(total, count, seqs)
    n_dev, slots, here = total.shape[0], got.shape[0], place_ref[1]
    mine = iota(total.shape, 0) == place_ref[0]
    pair_lane = iota(losses.shape, 1)
    for pair in range(seqs // 2):
        losses_ref[pair] = jnp.sum(jnp.where(mine & (pair_lane == pair), losses, 0.0))
    my_table = jnp.sum(jnp.where(mine, table, 0.0), axis=0, keepdims=True)
    my_weight = SCALE * jnp.sum(row_marks[...] * my_table, axis=1, keepdims=True)
    row_weight[...] = my_weight
    hot = iota((slots, n_dev), 0) // capacity == iota((slots, n_dev), 1)
    slot_table = exact_dot(hot.astype(F32), table)
    for copy in small_copies:
        copy.wait()
    hidden, near_rank, across_rank = [small[...] for small in smalls]
    both = in_slots(here, near_rank.astype(F32), across_rank.astype(F32))
    pulled, marks = both[:, :lanes], both[:, lanes:]
    weight = jnp.sum(marks * slot_table, axis=1, keepdims=True)
    upper[...] = (weight * hidden.astype(F32)).astype(BF16)
    lower = (weight * pulled).astype(BF16)
    contract = (((0,), (0,)), ((), ()))
    outs = [pltpu.make_async_copy(upper, upper_hbm, upper_sem)]
    outs[0].start()
    for at, part in enumerate(parts):
        copies[at].wait()
        made = lax.dot_general(lower, got[:, part], contract, preferred_element_type=F32)
        grad_down[:, part] = (SCALE * made).astype(BF16)
        outs.append(
            pltpu.make_async_copy(grad_down.at[:, part], down_hbm.at[:, part], down_sems.at[at])
        )
        outs[-1].start()
    if used:
        for copy in block_copies:
            copy.wait()
        for at, part in enumerate(parts):
            picked = jnp.dot(pick[...], rows[:, part], preferred_element_type=F32)
            input_grad[:, part] = (my_weight * picked).astype(BF16)
            outs.append(
                pltpu.make_async_copy(
                    input_grad.at[:, part], input_hbm.at[:, part], input_sems.at[at]
                )
            )
            outs[-1].start()
    for copy in outs:
        copy.wait()


def finish(place, told, got, smalls, row_marks, count, seqs, pick, blocks, used):
    (slots, width), lanes = got.shape, smalls[0].shape[1]
    rows = row_marks.shape[0]
    n_dev = told.shape[0]
    n_parts = len(column_parts(width, 2048))
    together = not any(size % 16 for size in used)
    vmem, hbm = pl.BlockSpec(memory_space=pltpu.VMEM), pl.BlockSpec(memory_space=pltpu.HBM)
    sems = pltpu.SemaphoreType.DMA
    out_shape = [
        jax.ShapeDtypeStruct((seqs // 2,), F32),
        jax.ShapeDtypeStruct((rows, 1), F32),
        pltpu.HBM((slots, lanes), BF16),
        jax.ShapeDtypeStruct((lanes, width), BF16),
    ]
    in_specs = [pl.BlockSpec(memory_space=pltpu.SMEM)] + [vmem] * 2 + [hbm] * 4
    smalls = [pltpu.with_memory_space_constraint(small, pltpu.HBM) for small in smalls]
    operands = [place, told, row_marks, *smalls, got]
    scratch = [
        *[pltpu.VMEM(small.shape, BF16) for small in smalls],
        pltpu.VMEM(got.shape, BF16),
        pltpu.VMEM((lanes, width), BF16),
    ]
    scratch_sems = [sems((3,)), sems((n_parts,)), sems((n_parts,))]
    if together:
        out_shape.append(jax.ShapeDtypeStruct((rows, width), BF16))
        in_specs += [vmem] + [hbm] * len(blocks)
        operands += [pick, *blocks]
        scratch += [pltpu.VMEM((slots, width), BF16), pltpu.VMEM((rows, width), BF16)]
        scratch_sems += [sems((len(blocks),)), sems((n_parts,))]
    losses, row_weight, upper, grad_down, *input_grad = pl.pallas_call(
        functools.partial(
            finish_kernel, count, seqs, slots // n_dev, used if together else []
        ),
        out_shape=out_shape,
        in_specs=in_specs,
        out_specs=[pl.BlockSpec(memory_space=pltpu.SMEM), vmem] + [hbm] * (len(out_shape) - 2),
        scratch_shapes=scratch + scratch_sems + [pltpu.VMEM((slots, lanes), BF16), sems],
        compiler_params=pltpu.CompilerParams(vmem_limit_bytes=24 * 2**20),
        cost_estimate=pl.CostEstimate(
            flops=4 * slots * lanes * width,
            bytes_accessed=2 * (2 * slots + lanes + rows) * width,
            transcendentals=0,
        ),
        name="finish",
    )(*operands)
    if not together:
        blocks = jnp.concatenate([block[:size] for block, size in zip(blocks, used)])
        picked = jnp.dot(pick, blocks, preferred_element_type=F32)
        input_grad = [(row_weight * picked).astype(BF16)]
    return input_grad[0], grad_down, upper, losses


def up_kernel(here_ref, upper_hbm, near_hbm, across_hbm, out, upper, near, across, sems):
    copies = [
        pltpu.make_async_copy(near_hbm.at[:, pl.ds(0, out.shape[1])], near, sems.at[0]),
        pltpu.make_async_copy(across_hbm, across, sems.at[1]),
        pltpu.make_async_copy(upper_hbm, upper, sems.at[2]),
    ]
    for copy in copies:
        copy.start()
    size = near.shape[0]
    copies[2].wait()
    first, second = upper[:size, :].astype(F32), upper[size:, :].astype(F32)
    here = here_ref[0]
    near_upper = jnp.where(here == 0, first, second).astype(BF16)
    across_upper = jnp.where(here == 0, second, first).astype(BF16)
    contract = (((0,), (0,)), ((), ()))
    copies[0].wait()
    made = lax.dot_general(near_upper, near[...], contract, preferred_element_type=F32)
    copies[1].wait()
    made = made + lax.dot_general(
        across_upper, across[...], contract, preferred_element_type=F32
    )
    out[...] = (SCALE * made).astype(BF16)


def up_gradient(here, upper, near_g, across_g):
    vmem, hbm = pl.BlockSpec(memory_space=pltpu.VMEM), pl.BlockSpec(memory_space=pltpu.HBM)
    upper = pltpu.with_memory_space_constraint(upper, pltpu.HBM)
    near_g = pltpu.with_memory_space_constraint(near_g, pltpu.HBM)
    across_g = pltpu.with_memory_space_constraint(across_g, pltpu.HBM)
    return pl.pallas_call(
        up_kernel,
        out_shape=jax.ShapeDtypeStruct((upper.shape[1], across_g.shape[1]), BF16),
        in_specs=[pl.BlockSpec(memory_space=pltpu.SMEM), hbm, hbm, hbm],
        out_specs=vmem,
        scratch_shapes=[
            pltpu.VMEM(upper.shape, BF16),
            pltpu.VMEM(across_g.shape, BF16),
            pltpu.VMEM(across_g.shape, BF16),
            pltpu.SemaphoreType.DMA((3,)),
        ],
        cost_estimate=pl.CostEstimate(
            flops=2 * upper.shape[0] * upper.shape[1] * across_g.shape[1],
            bytes_accessed=4 * across_g.shape[0] * across_g.shape[1],
            transcendentals=0,
        ),
        name="up",
    )(here.reshape(1), upper, near_g, across_g)


def slots_kernel(
    count, capacity, half_size, half_ref, owner_ref, adapter_ref, segment_ref, g_ref, *refs
):
    to_slot, to_half, sent_g = refs
    slots, rows = to_slot.shape
    out_width = g_ref.shape[1]
    eye = (iota((rows, rows), 0) == iota((rows, rows), 1)).astype(BF16)
    owner = lax.dot_general(
        owner_ref[...].astype(F32).astype(BF16),
        eye,
        (((0,), (0,)), ((), ())),
        preferred_element_type=F32,
    ).astype(jnp.int32)
    n_dev = 2 * half_size
    hot = (iota((n_dev, rows), 0) == owner).astype(F32)
    earlier = (iota((rows, rows), 0) < iota((rows, rows), 1)).astype(BF16)
    before = jnp.dot(hot.astype(BF16), earlier, preferred_element_type=F32)
    rank = jnp.sum(before * hot, axis=0, keepdims=True).astype(jnp.int32)
    at_slot = iota((slots, rows), 0)
    to_slot[...] = (at_slot == owner * capacity + rank).astype(BF16)
    far = owner // half_size != half_ref[0]
    position = (owner % half_size * 2 + far.astype(jnp.int32)) * capacity + rank
    hot_half = (at_slot == position).astype(BF16)
    to_half[...] = hot_half
    lane = iota((MARKS, rows), 0)
    marks = ((lane == adapter_ref[...]) | (lane == segment_ref[...] + count)).astype(BF16)
    sent_g[:, :out_width] = jnp.dot(hot_half, g_ref[...], preferred_element_type=F32).astype(BF16)
    sent_g[:, out_width:] = lax.dot_general(
        hot_half, marks, (((1,), (1,)), ((), ())), preferred_element_type=F32
    ).astype(BF16)


def slot_rows(half_at, owner, adapter, segment, cotangent, count, capacity, half_size):
    rows, out_width = cotangent.shape
    slots = 2 * half_size * capacity
    vmem = pl.BlockSpec(memory_space=pltpu.VMEM)
    return pl.pallas_call(
        functools.partial(slots_kernel, count, capacity, half_size),
        out_shape=[
            jax.ShapeDtypeStruct((slots, rows), BF16),
            jax.ShapeDtypeStruct((slots, rows), BF16),
            jax.ShapeDtypeStruct((slots, out_width + MARKS), BF16),
        ],
        in_specs=[pl.BlockSpec(memory_space=pltpu.SMEM)] + [vmem] * 4,
        out_specs=[vmem] * 3,
        name="slots",
    )(half_at.reshape(1), owner, adapter.reshape(1, rows), segment, cotangent)


def send_kernel(to_slot, tokens_hbm, sent_hbm, tokens, sent, in_sems, out_sems):
    parts = column_parts(tokens.shape[1], 1024)
    copies = [
        pltpu.make_async_copy(tokens_hbm.at[:, part], tokens.at[:, part], in_sems.at[at])
        for at, part in enumerate(parts)
    ]
    for copy in copies:
        copy.start()
    hot = to_slot[...]
    outs = []
    for at, part in enumerate(parts):
        copies[at].wait()
        sent[:, part] = jnp.dot(hot, tokens[:, part], preferred_element_type=F32).astype(BF16)
        outs.append(
            pltpu.make_async_copy(sent.at[:, part], sent_hbm.at[:, part], out_sems.at[at])
        )
        outs[-1].start()
    for copy in outs:
        copy.wait()


def send_rows(to_slot, tokens):
    slots, (rows, width) = to_slot.shape[0], tokens.shape
    n_parts = len(column_parts(width, 1024))
    vmem, hbm = pl.BlockSpec(memory_space=pltpu.VMEM), pl.BlockSpec(memory_space=pl.ANY)
    return pl.pallas_call(
        send_kernel,
        out_shape=jax.ShapeDtypeStruct((slots, width), BF16),
        in_specs=[vmem, hbm],
        out_specs=hbm,
        scratch_shapes=[
            pltpu.VMEM((rows, width), BF16),
            pltpu.VMEM((slots, width), BF16),
            pltpu.SemaphoreType.DMA((n_parts,)),
            pltpu.SemaphoreType.DMA((n_parts,)),
        ],
        compiler_params=pltpu.CompilerParams(vmem_limit_bytes=32 * 2**20),
        cost_estimate=pl.CostEstimate(
            flops=2 * slots * rows * width,
            bytes_accessed=2 * (slots + rows) * width,
            transcendentals=0,
        ),
        name="send",
    )(to_slot, tokens)


def half_kernel(which_ref, up_hbm, down_hbm, out, sems):
    out_width, which = up_hbm.shape[2], which_ref[0]
    width = down_hbm.shape[2]
    copies = [
        pltpu.make_async_copy(up_hbm.at[which], out.at[:, pl.ds(0, out_width)], sems.at[0]),
        pltpu.make_async_copy(
            down_hbm.at[which], out.at[:, pl.ds(out_width, width)], sems.at[1]
        ),
    ]
    for copy in copies:
        copy.start()
    for copy in copies:
        copy.wait()


def half_of(which, up_pair, down_pair):
    _, rank_size, width = down_pair.shape
    hbm = pl.BlockSpec(memory_space=pl.ANY)
    return pl.pallas_call(
        half_kernel,
        out_shape=jax.ShapeDtypeStruct((rank_size, up_pair.shape[2] + width), BF16),
        in_specs=[pl.BlockSpec(memory_space=pltpu.SMEM), hbm, hbm],
        out_specs=pl.BlockSpec(memory_space=pltpu.VMEM),
        scratch_shapes=[pltpu.SemaphoreType.DMA((2,))],
        name="half",
    )(which.reshape(1), up_pair, down_pair)


def body(
    tokens,
    cotangent,
    owner,
    token_local_adapter,
    segment,
    pair_sequence_order,
    frozen_margin_score,
    adapter_down_weight,
    adapter_up_weight,
):
    rows, width = tokens.shape
    out_width = cotangent.shape[1]
    n_grp, n_dev = lax.axis_size("grp"), lax.axis_size("ad")
    grp, me = lax.axis_index("grp"), lax.axis_index("ad")
    half_size = n_dev // 2
    spot = me % half_size
    capacity = max(2, 2 * rows // n_dev)
    slots = n_dev * capacity
    count, rank_size, _ = adapter_down_weight.shape
    seqs = frozen_margin_score.shape[1]
    lanes = count * rank_size
    down = adapter_down_weight.reshape(lanes, width)
    up = adapter_up_weight.reshape(lanes, out_width)

    def flipped(block, flip):
        return lax.ppermute(block, "ad", [(at, at ^ flip) for at in range(n_dev)])

    def other_grp(block):
        return lax.ppermute(block, "grp", [(0, 1), (1, 0)])

    half_mine = half_of(grp, adapter_up_weight, adapter_down_weight)
    far = flipped(half_mine, half_size)
    half_other = half_of(1 - grp, adapter_up_weight, adapter_down_weight)

    (owner,) = gate(lax.optimization_barrier((owner, half_mine))[0])
    row_seq = segment[0][:, None] == jnp.arange(seqs, dtype=jnp.int32)
    to_slot, to_half, sent_g = slot_rows(
        me // half_size, owner, token_local_adapter, segment, cotangent, count, capacity, half_size
    )
    sent = send_rows(to_slot, tokens)

    halves = [list(range(half_size)), list(range(half_size, n_dev))]
    to_half = to_half.reshape(half_size, 2, capacity, rows)
    half_g = lax.all_to_all(
        sent_g.reshape(half_size, 2 * capacity, out_width + MARKS),
        "ad",
        split_axis=0,
        concat_axis=0,
        tiled=True,
        axis_index_groups=halves,
    )

    lane = jnp.arange(MARKS, dtype=jnp.int32)[None, :]
    which = (lane == jnp.stack([grp, 1 - grp])[:, None]).astype(F32)

    def land(blocks):
        return [block if at == 0 else flipped(block, 2 * at) for at, block in enumerate(blocks)]

    def hand_over(blocks):
        return blocks + [flipped(jnp.concatenate([block[capacity:] for block in blocks]), 1)]

    made_near = project(
        0, False, capacity, out_width, width, spot, half_g, which, [half_mine], [half_other]
    )
    landed_near = land(made_near)
    (sent,) = gate(lax.optimization_barrier((sent, half_g))[0])
    got = lax.all_to_all(
        sent.reshape(n_dev, capacity, width),
        "ad",
        split_axis=0,
        concat_axis=0,
        tiled=True,
    ).reshape(slots, width)

    (which_far,) = gate(lax.optimization_barrier((which, sent, landed_near))[0])
    far_other = other_grp(far)
    kept, handed = project(
        1, True, capacity, out_width, width, spot, half_g, which_far, [far], [far_other]
    )
    taken = flipped(handed, 1)
    landed_far = land(
        [
            jnp.concatenate([kept[at : at + capacity], taken[at : at + capacity]])
            for at in range(0, half_size // 2 * capacity, capacity)
        ]
    )
    here = me // half_size
    near_g = half_g[:, :capacity].reshape(-1, out_width + MARKS)
    far_g = half_g[:, capacity:].reshape(-1, out_width + MARKS)
    far_ups = far[:, :out_width], far_other[:, :out_width]
    far_up = jnp.concatenate(
        [jnp.where(grp == 0, *far_ups), jnp.where(grp == 0, *far_ups[::-1])]
    )
    near_rank = pull_rows(near_g, up, count, rank_size)
    across_rank = flipped(pull_rows(far_g, far_up, count, rank_size), half_size)
    across_g = flipped(lax.optimization_barrier((far_g[:, :out_width], got))[0], half_size)

    pair_hot = pair_sequence_order[0][:, None] == jnp.arange(seqs, dtype=jnp.int32)
    at_me = (jnp.arange(n_dev, dtype=jnp.int32) == me)[:, None]
    own_scores = jnp.where(at_me, frozen_margin_score, 0.0).reshape(1, -1)
    own = jnp.concatenate(
        [
            jnp.pad(own_scores, ((0, 0), (0, -own_scores.shape[1] % MARKS))),
            jnp.zeros((1, count + seqs), F32),
            pair_hot.astype(F32).reshape(1, -1),
            jnp.zeros((1, MARKS - count - seqs - seqs * seqs), F32),
        ],
        axis=1,
    )
    part, hidden_rows = score(
        here, own, near_rank, across_rank, got, down, count, seqs, n_dev
    )
    told = lax.all_to_all(part, "ad", split_axis=0, concat_axis=0, tiled=True)

    chips = half_size // 2
    order = [2 * at for at in range(chips)] + [2 * at + 1 for at in range(chips)]
    near_flips = spot ^ jnp.array(order, dtype=jnp.int32)
    far_flips = spot ^ jnp.arange(half_size, dtype=jnp.int32)
    pick = jnp.concatenate([to_half[near_flips, 0], to_half[far_flips, 1]])
    pick = pick.reshape(slots, rows).T
    landed_far = lax.optimization_barrier((landed_far, told))[0]
    landed = hand_over(landed_near) + landed_far
    row_marks = jnp.pad(row_seq.astype(F32), ((0, 0), (count, MARKS - count - seqs)))
    input_grad, grad_down, upper, losses = finish(
        jnp.stack([me, here]),
        told,
        got,
        [hidden_rows, near_rank, across_rank],
        row_marks,
        count,
        seqs,
        pick,
        landed,
        [capacity] * chips + [chips * capacity] + [2 * capacity] * chips,
    )
    grad_up = up_gradient(here, upper, near_g, across_g)
    return (
        input_grad,
        grad_down.reshape(count, rank_size, width),
        grad_up.reshape(count, rank_size, out_width),
        losses,
    )


def solution(mesh):
    placed = (
        P(("grp", "ad"), None),
        P(("grp", "ad"), None),
        P(("grp", "ad"), None),
        P(("grp", "ad")),
        P(("grp", "ad"), None),
        P(("grp", "ad"), None),
        P(("grp", "ad"), None),
        P("ad", None, None),
        P("ad", None, None),
    )
    return jax.shard_map(
        body,
        mesh=mesh,
        in_specs=placed,
        out_specs=(
            P(("grp", "ad"), None),
            P(("grp", "ad"), None, None),
            P(("grp", "ad"), None, None),
            P(("grp", "ad")),
        ),
        check_vma=False,
    )
```

```python
import functools

import jax
import jax.numpy as jnp
from jax import lax
from jax.experimental import pallas as pl
from jax.experimental.pallas import tpu as pltpu
from jax.sharding import PartitionSpec as P

SCALE = 2.0
BETA = 0.1
LOSS_SCALE = 256.0
MARKS = 128
GATE_FLOPS = 2 * 10**11

F32 = jnp.float32
BF16 = jnp.bfloat16


def gate(*arrays):
    return pl.pallas_call(
        lambda *refs: None,
        out_shape=[jax.ShapeDtypeStruct(array.shape, array.dtype) for array in arrays],
        in_specs=[pl.BlockSpec(memory_space=pl.ANY)] * len(arrays),
        out_specs=[pl.BlockSpec(memory_space=pl.ANY)] * len(arrays),
        input_output_aliases={at: at for at in range(len(arrays))},
        cost_estimate=pl.CostEstimate(flops=GATE_FLOPS, bytes_accessed=0, transcendentals=0),
        name="gate",
    )(*arrays)


def project_kernel(side, split, capacity, out_width, n_outs, spot_ref, g_ref, which, *refs):
    n_spots = g_ref.shape[0]
    n_parts = (len(refs) - n_outs) // 2
    mine, other, outs = refs[:n_parts], refs[n_parts : 2 * n_parts], refs[2 * n_parts :]
    first = side * capacity
    spot = spot_ref[0]
    rows = jnp.concatenate(
        [g_ref[spot ^ flip, first : first + capacity, :] for flip in range(n_spots)], axis=0
    )
    marks = rows[:, out_width:].astype(F32)
    contract = (((1,), (1,)), ((), ()))
    pulls = []
    for at, parts in enumerate((mine, other)):
        member = jnp.sum(marks * which[at : at + 1, :], axis=1, keepdims=True)
        pull = lax.dot_general(
            rows[:, :out_width], parts[0][:, :out_width], contract, preferred_element_type=F32
        )
        pulls.append((member * pull).astype(BF16))
    done = 0
    for at in range(n_parts):
        start, end = (out_width if at == 0 else 0), mine[at].shape[1]
        while start < end:
            size = min(1024, end - start)
            columns = slice(start, start + size)
            made = jnp.dot(pulls[0], mine[at][:, columns], preferred_element_type=F32)
            made = made + jnp.dot(pulls[1], other[at][:, columns], preferred_element_type=F32)
            made = made.astype(BF16)
            for flip in range(n_spots):
                row = made[flip * capacity : (flip + 1) * capacity]
                if split:
                    chip = flip // 2 * capacity
                    outs[flip % 2][chip : chip + capacity, done : done + size] = row
                else:
                    core = flip % 2 * capacity
                    outs[flip // 2][core : core + capacity, done : done + size] = row
            start, done = start + size, done + size


def project(side, split, capacity, out_width, width, spot, got_g, which, mine, other):
    n_spots = got_g.shape[0]
    chips = n_spots // 2
    blocks = [(chips * capacity, width)] * 2 if split else [(2 * capacity, width)] * chips
    if capacity % 16 == 0:
        return pl.pallas_call(
            functools.partial(project_kernel, side, split, capacity, out_width, len(blocks)),
            out_shape=[jax.ShapeDtypeStruct(block, BF16) for block in blocks],
            in_specs=[pl.BlockSpec(memory_space=pltpu.SMEM)]
            + [pl.BlockSpec(memory_space=pltpu.VMEM)] * (2 + len(mine) + len(other)),
            cost_estimate=pl.CostEstimate(flops=1000, bytes_accessed=1000, transcendentals=0),
            name="project",
        )(spot.reshape(1), got_g, which, *mine, *other)
    order = spot ^ jnp.arange(n_spots, dtype=jnp.int32)
    rows = got_g[order, side * capacity : (side + 1) * capacity].reshape(n_spots * capacity, -1)
    marks = rows[:, out_width:].astype(F32)
    made = 0.0
    for at, parts in enumerate((mine, other)):
        whole = jnp.concatenate(parts, axis=1)
        pull = jnp.dot(rows[:, :out_width], whole[:, :out_width].T, preferred_element_type=F32)
        pull = (jnp.sum(marks * which[at], axis=1, keepdims=True) * pull).astype(BF16)
        made = made + jnp.dot(pull, whole[:, out_width:], preferred_element_type=F32)
    made = made.astype(BF16).reshape(chips, 2, capacity, width)
    if split:
        return [made[:, core].reshape(chips * capacity, width) for core in range(2)]
    return list(made.reshape(chips, 2 * capacity, width))


def iota(shape, axis):
    return lax.broadcasted_iota(jnp.int32, shape, axis)


def exact_dot(hot, values):
    return jnp.dot(hot, values, precision=lax.Precision.HIGHEST, preferred_element_type=F32)


def column_parts(width, columns):
    return [slice(start, min(start + columns, width)) for start in range(0, width, columns)]


def sequence_lanes(score_lanes, count, seqs):
    shape = (MARKS, score_lanes)
    return (iota(shape, 0) == count + iota(shape, 1) % seqs).astype(F32)


def pull_kernel(count, rank_size, g_ref, up, out):
    lanes, out_width = up.shape
    marks = g_ref[:, out_width:]
    lane = iota((g_ref.shape[0], lanes), 1) // rank_size
    member = jnp.zeros((g_ref.shape[0], lanes), F32)
    for which in range(count):
        member = jnp.where(lane == which, marks[:, which : which + 1].astype(F32), member)
    pull = member * lax.dot_general(
        g_ref[:, :out_width], up[...], (((1,), (1,)), ((), ())), preferred_element_type=F32
    )
    out[:, :lanes] = pull.astype(BF16)
    out[:, lanes:] = marks


def pull_rows(g_rows, up, count, rank_size):
    vmem = pl.BlockSpec(memory_space=pltpu.VMEM)
    return pl.pallas_call(
        functools.partial(pull_kernel, count, rank_size),
        out_shape=jax.ShapeDtypeStruct((g_rows.shape[0], up.shape[0] + MARKS), BF16),
        in_specs=[vmem] * 2,
        out_specs=vmem,
        cost_estimate=pl.CostEstimate(flops=1000, bytes_accessed=1000, transcendentals=0),
        name="pull",
    )(g_rows, up)


def in_slots(here, near, across):
    first = jnp.where(here == 0, near, across)
    return jnp.concatenate([first, jnp.where(here == 0, across, near)], axis=0)


def score_kernel(
    count, seqs, capacity, here_ref, own_ref, near_ref, across_ref, down, got_hbm, *refs
):
    told_ref, rows_hbm, got, hidden_rows, got_sems, rows_sem = refs
    lanes, width = down.shape
    parts = column_parts(width, 4096)
    copies = [
        pltpu.make_async_copy(got_hbm.at[:, part], got.at[:, part], got_sems.at[at])
        for at, part in enumerate(parts)
    ]
    for copy in copies:
        copy.start()
    contract = (((1,), (1,)), ((), ()))
    both = in_slots(here_ref[0], near_ref[...].astype(F32), across_ref[...].astype(F32))
    pulled, marks = both[:, :lanes], both[:, lanes:]
    slots = got.shape[0]
    lane = iota((slots, lanes), 1) // (lanes // count)
    member = jnp.zeros((slots, lanes), F32)
    for which in range(count):
        member = jnp.where(lane == which, marks[:, which : which + 1], member)
    total = jnp.zeros((slots, lanes), F32)
    for copy, part in zip(copies, parts):
        copy.wait()
        total = total + lax.dot_general(
            got[:, part], down[:, part], contract, preferred_element_type=F32
        )
    hidden = (member * total).astype(BF16)
    hidden_rows[...] = hidden
    rows_copy = pltpu.make_async_copy(hidden_rows, rows_hbm, rows_sem)
    rows_copy.start()
    inner = SCALE * jnp.sum(hidden.astype(F32) * pulled, axis=1, keepdims=True)
    n_dev, _, all_lanes = told_ref.shape
    scored = marks * inner
    if capacity % 8 == 0:
        part = jnp.sum(scored.reshape(n_dev, capacity, MARKS), axis=1)
    else:
        hot = iota((n_dev, slots), 1) // capacity == iota((n_dev, slots), 0)
        part = exact_dot(hot.astype(F32), scored)
    score_lanes = all_lanes - MARKS
    spread = exact_dot(part, sequence_lanes(score_lanes, count, seqs))
    at_device = iota((n_dev, score_lanes), 0) == iota((n_dev, score_lanes), 1) // seqs
    row = jnp.sum(jnp.where(at_device, spread, 0.0), axis=0, keepdims=True)
    row = jnp.concatenate([row, jnp.zeros((1, MARKS), F32)], axis=1) + own_ref[...]
    told_ref[...] = jnp.broadcast_to(row[None], told_ref.shape)
    rows_copy.wait()


def score(here, own, near, across, got, down, count, seqs, n_dev):
    slots = got.shape[0]
    lanes, width = down.shape
    n_parts = len(column_parts(width, 4096))
    vmem, hbm = pl.BlockSpec(memory_space=pltpu.VMEM), pl.BlockSpec(memory_space=pl.ANY)
    return pl.pallas_call(
        functools.partial(score_kernel, count, seqs, slots // n_dev),
        out_shape=[
            jax.ShapeDtypeStruct((n_dev,) + own.shape, F32),
            pltpu.HBM((slots, lanes), BF16),
        ],
        in_specs=[pl.BlockSpec(memory_space=pltpu.SMEM)] + [vmem] * 4 + [hbm],
        out_specs=[vmem, pl.BlockSpec(memory_space=pltpu.HBM)],
        scratch_shapes=[
            pltpu.VMEM(got.shape, BF16),
            pltpu.VMEM((slots, lanes), BF16),
            pltpu.SemaphoreType.DMA((n_parts,)),
            pltpu.SemaphoreType.DMA,
        ],
        compiler_params=pltpu.CompilerParams(vmem_limit_bytes=16 * 2**20),
        cost_estimate=pl.CostEstimate(
            flops=2 * slots * lanes * width,
            bytes_accessed=2 * (slots + lanes) * width,
            transcendentals=0,
        ),
        name="score",
    )(here.reshape(1), own, near, across, down, got)


def weights(total, count, seqs):
    lane = iota(total.shape, 1)

    def column(at):
        return total[:, at : at + 1]

    pick = [[column(count + seqs + i * seqs + s) for s in range(seqs)] for i in range(seqs)]
    ordered = [sum(pick[i][s] * column(count + s) for s in range(seqs)) for i in range(seqs)]
    losses, by_order = jnp.zeros(total.shape, F32), []
    for pair in range(seqs // 2):
        margin = BETA * (ordered[2 * pair] - ordered[2 * pair + 1])
        small = jnp.exp(-jnp.abs(margin))
        loss = jnp.maximum(-margin, 0.0) + jnp.log1p(small)
        losses = jnp.where(lane == pair, loss, losses)
        lean = jnp.where(margin > 0.0, small, 1.0) / (1.0 + small)
        by_order += [-BETA * lean, BETA * lean]
    table = jnp.zeros(total.shape, F32)
    for s in range(seqs):
        weight = LOSS_SCALE * sum(pick[i][s] * by_order[i] for i in range(seqs))
        table = jnp.where(lane == count + s, weight, table)
    return losses, table


def finish_kernel(count, seqs, capacity, used, place_ref, told_ref, *refs):
    row_marks, *small_hbms, got_hbm = refs[:5]
    refs = refs[5:]
    if used:
        pick, *refs = refs
    block_hbms, refs = refs[: len(used)], refs[len(used) :]
    losses_ref, row_weight, upper_hbm, down_hbm, *refs, upper, upper_sem = refs
    if used:
        input_hbm, *smalls = refs[:4]
        got, grad_down, rows, input_grad, *sems = refs[4:]
        small_sems, got_sems, down_sems, block_sems, input_sems = sems
    else:
        smalls, refs = refs[:3], refs[3:]
        got, grad_down, small_sems, got_sems, down_sems = refs
    lanes, width = grad_down.shape
    parts = column_parts(width, 4096)
    copies = [
        pltpu.make_async_copy(got_hbm.at[:, part], got.at[:, part], got_sems.at[at])
        for at, part in enumerate(parts)
    ]
    first, block_copies = 0, []
    for at, size in enumerate(used):
        block_copies.append(
            pltpu.make_async_copy(
                block_hbms[at].at[pl.ds(0, size)], rows.at[pl.ds(first, size)], block_sems.at[at]
            )
        )
        first += size
    small_copies = [
        pltpu.make_async_copy(hbm, small, small_sems.at[at])
        for at, (hbm, small) in enumerate(zip(small_hbms, smalls))
    ]
    for copy in small_copies + copies + block_copies:
        copy.start()

    told = jnp.concatenate([told_ref[at] for at in range(told_ref.shape[0])], axis=0)
    score_lanes = told.shape[1] - MARKS
    sums = jnp.sum(told[:, :score_lanes], axis=0, keepdims=True)
    shape = (told.shape[0], score_lanes)
    spread = jnp.where(iota(shape, 0) == iota(shape, 1) // seqs, sums, 0.0)
    total = told[:, score_lanes:] + lax.dot_general(
        spread,
        sequence_lanes(score_lanes, count, seqs),
        (((1,), (1,)), ((), ())),
        precision=lax.Precision.HIGHEST,
        preferred_element_type=F32,
    )
    losses, table = weights(total, count, seqs)
    n_dev, slots, here = total.shape[0], got.shape[0], place_ref[1]
    mine = iota(total.shape, 0) == place_ref[0]
    pair_lane = iota(losses.shape, 1)
    for pair in range(seqs // 2):
        losses_ref[pair] = jnp.sum(jnp.where(mine & (pair_lane == pair), losses, 0.0))
    my_table = jnp.sum(jnp.where(mine, table, 0.0), axis=0, keepdims=True)
    my_weight = SCALE * jnp.sum(row_marks[...] * my_table, axis=1, keepdims=True)
    row_weight[...] = my_weight
    hot = iota((slots, n_dev), 0) // capacity == iota((slots, n_dev), 1)
    slot_table = exact_dot(hot.astype(F32), table)
    for copy in small_copies:
        copy.wait()
    hidden, near_rank, across_rank = [small[...] for small in smalls]
    both = in_slots(here, near_rank.astype(F32), across_rank.astype(F32))
    pulled, marks = both[:, :lanes], both[:, lanes:]
    weight = jnp.sum(marks * slot_table, axis=1, keepdims=True)
    upper[...] = (weight * hidden.astype(F32)).astype(BF16)
    lower = (weight * pulled).astype(BF16)
    contract = (((0,), (0,)), ((), ()))
    outs = [pltpu.make_async_copy(upper, upper_hbm, upper_sem)]
    outs[0].start()
    for at, part in enumerate(parts):
        copies[at].wait()
        made = lax.dot_general(lower, got[:, part], contract, preferred_element_type=F32)
        grad_down[:, part] = (SCALE * made).astype(BF16)
        outs.append(
            pltpu.make_async_copy(grad_down.at[:, part], down_hbm.at[:, part], down_sems.at[at])
        )
        outs[-1].start()
    if used:
        for copy in block_copies:
            copy.wait()
        for at, part in enumerate(parts):
            picked = jnp.dot(pick[...], rows[:, part], preferred_element_type=F32)
            input_grad[:, part] = (my_weight * picked).astype(BF16)
            outs.append(
                pltpu.make_async_copy(
                    input_grad.at[:, part], input_hbm.at[:, part], input_sems.at[at]
                )
            )
            outs[-1].start()
    for copy in outs:
        copy.wait()


def finish(place, told, got, smalls, row_marks, count, seqs, pick, blocks, used):
    (slots, width), lanes = got.shape, smalls[0].shape[1]
    rows = row_marks.shape[0]
    n_dev = told.shape[0]
    n_parts = len(column_parts(width, 4096))
    together = not any(size % 16 for size in used)
    vmem, hbm = pl.BlockSpec(memory_space=pltpu.VMEM), pl.BlockSpec(memory_space=pltpu.HBM)
    sems = pltpu.SemaphoreType.DMA
    out_shape = [
        jax.ShapeDtypeStruct((seqs // 2,), F32),
        jax.ShapeDtypeStruct((rows, 1), F32),
        pltpu.HBM((slots, lanes), BF16),
        jax.ShapeDtypeStruct((lanes, width), BF16),
    ]
    in_specs = [pl.BlockSpec(memory_space=pltpu.SMEM)] + [vmem] * 2 + [hbm] * 4
    smalls = [pltpu.with_memory_space_constraint(small, pltpu.HBM) for small in smalls]
    operands = [place, told, row_marks, *smalls, got]
    scratch = [
        *[pltpu.VMEM(small.shape, BF16) for small in smalls],
        pltpu.VMEM(got.shape, BF16),
        pltpu.VMEM((lanes, width), BF16),
    ]
    scratch_sems = [sems((3,)), sems((n_parts,)), sems((n_parts,))]
    if together:
        out_shape.append(jax.ShapeDtypeStruct((rows, width), BF16))
        in_specs += [vmem] + [hbm] * len(blocks)
        operands += [pick, *blocks]
        scratch += [pltpu.VMEM((slots, width), BF16), pltpu.VMEM((rows, width), BF16)]
        scratch_sems += [sems((len(blocks),)), sems((n_parts,))]
    losses, row_weight, upper, grad_down, *input_grad = pl.pallas_call(
        functools.partial(
            finish_kernel, count, seqs, slots // n_dev, used if together else []
        ),
        out_shape=out_shape,
        in_specs=in_specs,
        out_specs=[pl.BlockSpec(memory_space=pltpu.SMEM), vmem] + [hbm] * (len(out_shape) - 2),
        scratch_shapes=scratch + scratch_sems + [pltpu.VMEM((slots, lanes), BF16), sems],
        compiler_params=pltpu.CompilerParams(vmem_limit_bytes=24 * 2**20),
        cost_estimate=pl.CostEstimate(
            flops=4 * slots * lanes * width,
            bytes_accessed=2 * (2 * slots + lanes + rows) * width,
            transcendentals=0,
        ),
        name="finish",
    )(*operands)
    if not together:
        blocks = jnp.concatenate([block[:size] for block, size in zip(blocks, used)])
        picked = jnp.dot(pick, blocks, preferred_element_type=F32)
        input_grad = [(row_weight * picked).astype(BF16)]
    return input_grad[0], grad_down, upper, losses


def up_kernel(here_ref, upper_hbm, near_hbm, across_hbm, out, upper, near, across, sems):
    copies = [
        pltpu.make_async_copy(near_hbm.at[:, pl.ds(0, out.shape[1])], near, sems.at[0]),
        pltpu.make_async_copy(across_hbm, across, sems.at[1]),
        pltpu.make_async_copy(upper_hbm, upper, sems.at[2]),
    ]
    for copy in copies:
        copy.start()
    size = near.shape[0]
    copies[2].wait()
    first, second = upper[:size, :].astype(F32), upper[size:, :].astype(F32)
    here = here_ref[0]
    near_upper = jnp.where(here == 0, first, second).astype(BF16)
    across_upper = jnp.where(here == 0, second, first).astype(BF16)
    contract = (((0,), (0,)), ((), ()))
    copies[0].wait()
    made = lax.dot_general(near_upper, near[...], contract, preferred_element_type=F32)
    copies[1].wait()
    made = made + lax.dot_general(
        across_upper, across[...], contract, preferred_element_type=F32
    )
    out[...] = (SCALE * made).astype(BF16)


def up_gradient(here, upper, near_g, across_g):
    vmem, hbm = pl.BlockSpec(memory_space=pltpu.VMEM), pl.BlockSpec(memory_space=pltpu.HBM)
    upper = pltpu.with_memory_space_constraint(upper, pltpu.HBM)
    near_g = pltpu.with_memory_space_constraint(near_g, pltpu.HBM)
    across_g = pltpu.with_memory_space_constraint(across_g, pltpu.HBM)
    return pl.pallas_call(
        up_kernel,
        out_shape=jax.ShapeDtypeStruct((upper.shape[1], across_g.shape[1]), BF16),
        in_specs=[pl.BlockSpec(memory_space=pltpu.SMEM), hbm, hbm, hbm],
        out_specs=vmem,
        scratch_shapes=[
            pltpu.VMEM(upper.shape, BF16),
            pltpu.VMEM(across_g.shape, BF16),
            pltpu.VMEM(across_g.shape, BF16),
            pltpu.SemaphoreType.DMA((3,)),
        ],
        cost_estimate=pl.CostEstimate(
            flops=2 * upper.shape[0] * upper.shape[1] * across_g.shape[1],
            bytes_accessed=4 * across_g.shape[0] * across_g.shape[1],
            transcendentals=0,
        ),
        name="up",
    )(here.reshape(1), upper, near_g, across_g)


def slots_kernel(
    count, capacity, half_size, half_ref, owner_ref, adapter_ref, segment_ref, g_ref, *refs
):
    to_slot, to_half, sent_g = refs
    slots, rows = to_slot.shape
    out_width = g_ref.shape[1]
    eye = (iota((rows, rows), 0) == iota((rows, rows), 1)).astype(BF16)
    owner = lax.dot_general(
        owner_ref[...].astype(F32).astype(BF16),
        eye,
        (((0,), (0,)), ((), ())),
        preferred_element_type=F32,
    ).astype(jnp.int32)
    n_dev = 2 * half_size
    hot = (iota((n_dev, rows), 0) == owner).astype(F32)
    earlier = (iota((rows, rows), 0) < iota((rows, rows), 1)).astype(BF16)
    before = jnp.dot(hot.astype(BF16), earlier, preferred_element_type=F32)
    rank = jnp.sum(before * hot, axis=0, keepdims=True).astype(jnp.int32)
    at_slot = iota((slots, rows), 0)
    to_slot[...] = (at_slot == owner * capacity + rank).astype(BF16)
    far = owner // half_size != half_ref[0]
    position = (owner % half_size * 2 + far.astype(jnp.int32)) * capacity + rank
    hot_half = (at_slot == position).astype(BF16)
    to_half[...] = hot_half
    lane = iota((MARKS, rows), 0)
    marks = ((lane == adapter_ref[...]) | (lane == segment_ref[...] + count)).astype(BF16)
    sent_g[:, :out_width] = jnp.dot(hot_half, g_ref[...], preferred_element_type=F32).astype(BF16)
    sent_g[:, out_width:] = lax.dot_general(
        hot_half, marks, (((1,), (1,)), ((), ())), preferred_element_type=F32
    ).astype(BF16)


def slot_rows(half_at, owner, adapter, segment, cotangent, count, capacity, half_size):
    rows, out_width = cotangent.shape
    slots = 2 * half_size * capacity
    vmem = pl.BlockSpec(memory_space=pltpu.VMEM)
    return pl.pallas_call(
        functools.partial(slots_kernel, count, capacity, half_size),
        out_shape=[
            jax.ShapeDtypeStruct((slots, rows), BF16),
            jax.ShapeDtypeStruct((slots, rows), BF16),
            jax.ShapeDtypeStruct((slots, out_width + MARKS), BF16),
        ],
        in_specs=[pl.BlockSpec(memory_space=pltpu.SMEM)] + [vmem] * 4,
        out_specs=[vmem] * 3,
        name="slots",
    )(half_at.reshape(1), owner, adapter.reshape(1, rows), segment, cotangent)


def send_kernel(to_slot, tokens_hbm, sent_hbm, tokens, sent, in_sems, out_sems):
    parts = column_parts(tokens.shape[1], 1024)
    copies = [
        pltpu.make_async_copy(tokens_hbm.at[:, part], tokens.at[:, part], in_sems.at[at])
        for at, part in enumerate(parts)
    ]
    for copy in copies:
        copy.start()
    hot = to_slot[...]
    outs = []
    for at, part in enumerate(parts):
        copies[at].wait()
        sent[:, part] = jnp.dot(hot, tokens[:, part], preferred_element_type=F32).astype(BF16)
        outs.append(
            pltpu.make_async_copy(sent.at[:, part], sent_hbm.at[:, part], out_sems.at[at])
        )
        outs[-1].start()
    for copy in outs:
        copy.wait()


def send_rows(to_slot, tokens):
    slots, (rows, width) = to_slot.shape[0], tokens.shape
    n_parts = len(column_parts(width, 1024))
    vmem, hbm = pl.BlockSpec(memory_space=pltpu.VMEM), pl.BlockSpec(memory_space=pl.ANY)
    return pl.pallas_call(
        send_kernel,
        out_shape=jax.ShapeDtypeStruct((slots, width), BF16),
        in_specs=[vmem, hbm],
        out_specs=hbm,
        scratch_shapes=[
            pltpu.VMEM((rows, width), BF16),
            pltpu.VMEM((slots, width), BF16),
            pltpu.SemaphoreType.DMA((n_parts,)),
            pltpu.SemaphoreType.DMA((n_parts,)),
        ],
        compiler_params=pltpu.CompilerParams(vmem_limit_bytes=32 * 2**20),
        cost_estimate=pl.CostEstimate(
            flops=2 * slots * rows * width,
            bytes_accessed=2 * (slots + rows) * width,
            transcendentals=0,
        ),
        name="send",
    )(to_slot, tokens)


def half_kernel(which_ref, up_hbm, down_hbm, out, sems):
    out_width, which = up_hbm.shape[2], which_ref[0]
    width = down_hbm.shape[2]
    copies = [
        pltpu.make_async_copy(up_hbm.at[which], out.at[:, pl.ds(0, out_width)], sems.at[0]),
        pltpu.make_async_copy(
            down_hbm.at[which], out.at[:, pl.ds(out_width, width)], sems.at[1]
        ),
    ]
    for copy in copies:
        copy.start()
    for copy in copies:
        copy.wait()


def half_of(which, up_pair, down_pair):
    _, rank_size, width = down_pair.shape
    hbm = pl.BlockSpec(memory_space=pl.ANY)
    return pl.pallas_call(
        half_kernel,
        out_shape=jax.ShapeDtypeStruct((rank_size, up_pair.shape[2] + width), BF16),
        in_specs=[pl.BlockSpec(memory_space=pltpu.SMEM), hbm, hbm],
        out_specs=pl.BlockSpec(memory_space=pltpu.VMEM),
        scratch_shapes=[pltpu.SemaphoreType.DMA((2,))],
        name="half",
    )(which.reshape(1), up_pair, down_pair)


def body(
    tokens,
    cotangent,
    owner,
    token_local_adapter,
    segment,
    pair_sequence_order,
    frozen_margin_score,
    adapter_down_weight,
    adapter_up_weight,
):
    rows, width = tokens.shape
    out_width = cotangent.shape[1]
    n_grp, n_dev = lax.axis_size("grp"), lax.axis_size("ad")
    grp, me = lax.axis_index("grp"), lax.axis_index("ad")
    half_size = n_dev // 2
    spot = me % half_size
    capacity = max(2, 2 * rows // n_dev)
    slots = n_dev * capacity
    count, rank_size, _ = adapter_down_weight.shape
    seqs = frozen_margin_score.shape[1]
    lanes = count * rank_size
    down = adapter_down_weight.reshape(lanes, width)
    up = adapter_up_weight.reshape(lanes, out_width)

    def flipped(block, flip):
        return lax.ppermute(block, "ad", [(at, at ^ flip) for at in range(n_dev)])

    def other_grp(block):
        return lax.ppermute(block, "grp", [(0, 1), (1, 0)])

    half_mine = half_of(grp, adapter_up_weight, adapter_down_weight)
    far = flipped(half_mine, half_size)
    half_other = half_of(1 - grp, adapter_up_weight, adapter_down_weight)

    (owner,) = gate(lax.optimization_barrier((owner, half_mine))[0])
    row_seq = segment[0][:, None] == jnp.arange(seqs, dtype=jnp.int32)
    to_slot, to_half, sent_g = slot_rows(
        me // half_size, owner, token_local_adapter, segment, cotangent, count, capacity, half_size
    )
    sent = send_rows(to_slot, tokens)

    halves = [list(range(half_size)), list(range(half_size, n_dev))]
    to_half = to_half.reshape(half_size, 2, capacity, rows)
    half_g = lax.all_to_all(
        sent_g.reshape(half_size, 2 * capacity, out_width + MARKS),
        "ad",
        split_axis=0,
        concat_axis=0,
        tiled=True,
        axis_index_groups=halves,
    )

    lane = jnp.arange(MARKS, dtype=jnp.int32)[None, :]
    which = (lane == jnp.stack([grp, 1 - grp])[:, None]).astype(F32)

    def land(blocks):
        return [block if at == 0 else flipped(block, 2 * at) for at, block in enumerate(blocks)]

    def hand_over(blocks):
        return blocks + [flipped(jnp.concatenate([block[capacity:] for block in blocks]), 1)]

    made_near = project(
        0, False, capacity, out_width, width, spot, half_g, which, [half_mine], [half_other]
    )
    landed_near = land(made_near)
    (sent,) = gate(lax.optimization_barrier((sent, half_g))[0])
    got = lax.all_to_all(
        sent.reshape(n_dev, capacity, width),
        "ad",
        split_axis=0,
        concat_axis=0,
        tiled=True,
    ).reshape(slots, width)

    (which_far,) = gate(lax.optimization_barrier((which, sent, landed_near))[0])
    far_other = other_grp(far)
    kept, handed = project(
        1, True, capacity, out_width, width, spot, half_g, which_far, [far], [far_other]
    )
    taken = flipped(handed, 1)
    landed_far = land(
        [
            jnp.concatenate([kept[at : at + capacity], taken[at : at + capacity]])
            for at in range(0, half_size // 2 * capacity, capacity)
        ]
    )
    here = me // half_size
    near_g = half_g[:, :capacity].reshape(-1, out_width + MARKS)
    far_g = half_g[:, capacity:].reshape(-1, out_width + MARKS)
    far_ups = far[:, :out_width], far_other[:, :out_width]
    far_up = jnp.concatenate(
        [jnp.where(grp == 0, *far_ups), jnp.where(grp == 0, *far_ups[::-1])]
    )
    near_rank = pull_rows(near_g, up, count, rank_size)
    across_rank = flipped(pull_rows(far_g, far_up, count, rank_size), half_size)
    across_g = flipped(lax.optimization_barrier((far_g[:, :out_width], got))[0], half_size)

    pair_hot = pair_sequence_order[0][:, None] == jnp.arange(seqs, dtype=jnp.int32)
    at_me = (jnp.arange(n_dev, dtype=jnp.int32) == me)[:, None]
    own_scores = jnp.where(at_me, frozen_margin_score, 0.0).reshape(1, -1)
    own = jnp.concatenate(
        [
            jnp.pad(own_scores, ((0, 0), (0, -own_scores.shape[1] % MARKS))),
            jnp.zeros((1, count + seqs), F32),
            pair_hot.astype(F32).reshape(1, -1),
            jnp.zeros((1, MARKS - count - seqs - seqs * seqs), F32),
        ],
        axis=1,
    )
    part, hidden_rows = score(
        here, own, near_rank, across_rank, got, down, count, seqs, n_dev
    )
    told = lax.all_to_all(part, "ad", split_axis=0, concat_axis=0, tiled=True)

    chips = half_size // 2
    order = [2 * at for at in range(chips)] + [2 * at + 1 for at in range(chips)]
    near_flips = spot ^ jnp.array(order, dtype=jnp.int32)
    far_flips = spot ^ jnp.arange(half_size, dtype=jnp.int32)
    pick = jnp.concatenate([to_half[near_flips, 0], to_half[far_flips, 1]])
    pick = pick.reshape(slots, rows).T
    landed_far = lax.optimization_barrier((landed_far, told))[0]
    landed = hand_over(landed_near) + landed_far
    row_marks = jnp.pad(row_seq.astype(F32), ((0, 0), (count, MARKS - count - seqs)))
    input_grad, grad_down, upper, losses = finish(
        jnp.stack([me, here]),
        told,
        got,
        [hidden_rows, near_rank, across_rank],
        row_marks,
        count,
        seqs,
        pick,
        landed,
        [capacity] * chips + [chips * capacity] + [2 * capacity] * chips,
    )
    grad_up = up_gradient(here, upper, near_g, across_g)
    return (
        input_grad,
        grad_down.reshape(count, rank_size, width),
        grad_up.reshape(count, rank_size, out_width),
        losses,
    )


def solution(mesh):
    placed = (
        P(("grp", "ad"), None),
        P(("grp", "ad"), None),
        P(("grp", "ad"), None),
        P(("grp", "ad")),
        P(("grp", "ad"), None),
        P(("grp", "ad"), None),
        P(("grp", "ad"), None),
        P("ad", None, None),
        P("ad", None, None),
    )
    return jax.shard_map(
        body,
        mesh=mesh,
        in_specs=placed,
        out_specs=(
            P(("grp", "ad"), None),
            P(("grp", "ad"), None, None),
            P(("grp", "ad"), None, None),
            P(("grp", "ad")),
        ),
        check_vma=False,
    )
```
